32 devices in a mesh: groups: 2 (over x), space: 16 (over z, y, core).
Axes of the slice: x: 2, y: 2, z: 4, core: 2. Of those that a mesh axis runs over, the one named last changes fastest.
Arguments:
- model: float32 [128, 64, 128], P(('groups', 'space')), parts along dimension 0, may hold values from -3.35 to 3.35
- forward: bfloat16 [8, 128, 64, 128], P(None, ('groups', 'space')), parts along dimension 1, may hold values from -6 to 6
- warm_start: bfloat16 [8, 128, 64, 128], P(None, ('groups', 'space')), parts along dimension 1, may hold values from -6 to 6
- residual_data: float32 [16, 8, 256], P('groups'), parts along dimension 0, may hold values from -6 to 6
- electrodes: int32 [512], P('groups'), parts along dimension 0, may hold values from 0 to 65535
- survey_order: int32 [16], P('groups'), parts along dimension 0, may hold values from 0 to 7, each once
Outputs:
- adjoint: bfloat16 [8, 128, 64, 128], P(None, ('groups', 'space')), parts along dimension 1
- gradient: float32 [128, 64, 128], P(('groups', 'space')), parts along dimension 0
The draws below stay inside these ranges and needn't reach their ends.
There are 2 independent parts, one for each index of `groups`. The reference program is written for one: setup_inputs(seed, part) draws one part's arguments, and reference() takes and returns one part's arrays. A program takes and returns all parts, laid end to end along the dimension named above; each array names one. Nothing has to cross between parts.
All inputs are finite; a program needn't handle non-finite values.
Results may differ from the reference program's by a relative error of at most 0.001.
Values sent between devices are 32-bit elements; how exact they have to be, the bound alone decides.
No kernel may reach another device: no remote copies, remote signals or barrier semaphores. Data moves between devices by JAX's collectives and lax.ppermute only.
A program may use at most 128 MiB of HBM per device.

```python
import jax
import jax.numpy as jnp
from jax import lax

SURVEYS = 8
SOURCES = 8
ELECTRODES = 256
ITERS = 4
NY = 64
NZ = 128
NX = 8


def draw_model(key, part):
    key = jax.random.fold_in(key, 7)
    noise_key, board_key, phase_key = jax.random.split(key, 3)
    stacked = SURVEYS * NX
    height = 2.5
    noise = jnp.clip(0.3 * jax.random.normal(noise_key, (stacked, NY, NZ), jnp.float32), -0.85, 0.85)
    shifted = (jnp.arange(stacked, dtype=jnp.int32) + NX // 2) % stacked
    survey = shifted // NX
    layer_index = shifted % NX
    board = jax.random.randint(board_key, (SURVEYS,), 0, 2).astype(jnp.int32)
    phase = jax.random.randint(phase_key, (SURVEYS, NY, NZ), 0, 2).astype(jnp.int32)
    across = jnp.arange(NY, dtype=jnp.int32)[:, None] + jnp.arange(NZ, dtype=jnp.int32)[None, :]
    on_line = (across[None] + board[survey][:, None, None]) % 2 == 0
    raised = on_line & ((layer_index[:, None, None] + phase[survey]) % 2 == 0)
    return jnp.where(raised, height, -height).astype(jnp.float32) + noise


def plant(values, rng, least, high):
    dims = values.shape
    place = [jax.random.randint(jax.random.fold_in(rng, axis), (), 0, dims[axis]) for axis in range(len(dims))]
    values = values.at[tuple(place)].set(least)
    longest = dims.index(max(dims))
    place[longest] = (place[longest] + 1) % dims[longest]
    return values.at[tuple(place)].set(high)


def block_levels(rng, shape, cuts, low, largest):
    loudness, own = 1.0, jax.random.fold_in(rng, 6)
    for dim, shards_of in cuts:
        steps = jnp.exp(jax.random.uniform(jax.random.fold_in(own, dim), (shards_of,), jnp.float32, low / len(cuts), largest / len(cuts)))
        loudness = loudness * jnp.repeat(steps, shape[dim] // shards_of).reshape([-1 if axis == dim else 1 for axis in range(len(shape))])
    return loudness


def gaussian(rng, extent, deviation, limit, cuts=(), kind=jnp.bfloat16):
    factor_of = block_levels(rng, extent, cuts, -0.22, 0.18) if cuts else 1.0
    entries = jax.random.normal(rng, extent, jnp.float32) * deviation * factor_of
    return jnp.minimum(jnp.maximum(entries, -limit), limit).astype(kind)


def setup_inputs(seed: int = 0, part: int = 0) -> dict:
    splits = jax.random.split(jax.random.key(seed), 7)
    part_splits = jax.random.split(jax.random.fold_in(splits[6], part), 7)
    return {
        "model": draw_model(jax.random.fold_in(jax.random.fold_in(splits[6], part), 71), part),
        "forward": gaussian(part_splits[1], (SOURCES, SURVEYS * NX, NY, NZ), 1.0, 6.0, ((1, 16),)),
        "warm_start": gaussian(part_splits[2], (SOURCES, SURVEYS * NX, NY, NZ), 1.0, 6.0, ((1, 16),)),
        "residual_data": gaussian(part_splits[3], (SURVEYS, SOURCES, ELECTRODES), 1.0, 6.0, (), jnp.float32),
        "electrodes": plant(jax.random.randint(part_splits[4], (ELECTRODES,), 0, NX * NY * NZ), jax.random.fold_in(part_splits[4], 1), 0, (NX * NY * NZ) - 1).astype(jnp.int32),
        "survey_order": jax.random.permutation(part_splits[5], SURVEYS).astype(jnp.int32),
    }


GROUND = 0.5
CENTER = 1.0
HALF_WIDTH = 0.99


def face_diff(field, axis):
    count = field.shape[axis]
    return lax.slice_in_dim(field, 0, count - 1, axis=axis) - lax.slice_in_dim(field, 1, count, axis=axis)


def edge_zeros(field, axis):
    shape = list(field.shape)
    shape[axis] = 1
    return jnp.zeros(shape, jnp.float32)


def pad_diff(faces, axis):
    zeros = edge_zeros(faces, axis)
    return jnp.concatenate([faces, zeros], axis=axis) - jnp.concatenate([zeros, faces], axis=axis)


def pad_sum(faces, axis):
    zeros = edge_zeros(faces, axis)
    return jnp.concatenate([faces, zeros], axis=axis) + jnp.concatenate([zeros, faces], axis=axis)


def one_survey(inputs, electrodes):
    layer, potential, start, residual = inputs
    sigma = jnp.exp(layer)
    conduct = [0.5 * (lax.slice_in_dim(sigma, 0, sigma.shape[a] - 1, axis=a) + lax.slice_in_dim(sigma, 1, sigma.shape[a], axis=a)) for a in range(3)]
    diagonal = pad_sum(conduct[0], 0) + pad_sum(conduct[1], 1) + pad_sum(conduct[2], 2) + GROUND * sigma

    def operate(field):
        total = pad_diff(conduct[0][None] * face_diff(field, 1), 1)
        total = total + pad_diff(conduct[1][None] * face_diff(field, 2), 2)
        total = total + pad_diff(conduct[2][None] * face_diff(field, 3), 3)
        return total + GROUND * sigma[None] * field

    rhs = jnp.zeros((SOURCES, NX * NY * NZ), jnp.float32).at[:, electrodes].add(residual).reshape(SOURCES, NX, NY, NZ)
    iterate = start.astype(jnp.float32)
    remain = rhs - operate(iterate)
    direction = remain / diagonal[None] / CENTER
    weight_now = HALF_WIDTH / CENTER
    for sweep_index in range(ITERS):
        iterate = iterate + direction
        if sweep_index + 1 < ITERS:
            remain = remain - operate(direction)
            weight_new = 1.0 / (2.0 * CENTER / HALF_WIDTH - weight_now)
            direction = weight_new * weight_now * direction + (2.0 * weight_new / HALF_WIDTH) * (remain / diagonal[None])
            weight_now = weight_new
    potential_f = potential.astype(jnp.float32)
    terms = pad_sum(jnp.sum(face_diff(potential_f, 1) * face_diff(iterate, 1), axis=0), 0)
    terms = terms + pad_sum(jnp.sum(face_diff(potential_f, 2) * face_diff(iterate, 2), axis=0), 1)
    terms = terms + pad_sum(jnp.sum(face_diff(potential_f, 3) * face_diff(iterate, 3), axis=0), 2)
    data_term = -sigma * (0.5 * terms + GROUND * jnp.sum(potential_f * iterate, axis=0))
    return iterate.astype(jnp.bfloat16), data_term


def reference(model, forward, warm_start, residual_data, electrodes, survey_order):
    offset = NX // 2
    model_s = jnp.roll(model, offset, axis=0).reshape(SURVEYS, NX, NY, NZ)
    forward_s = jnp.transpose(jnp.roll(forward, offset, axis=1).reshape(SOURCES, SURVEYS, NX, NY, NZ), (1, 0, 2, 3, 4))
    start_s = jnp.transpose(jnp.roll(warm_start, offset, axis=1).reshape(SOURCES, SURVEYS, NX, NY, NZ), (1, 0, 2, 3, 4))
    adjoint, data_term = lax.map(lambda inputs: one_survey(inputs, electrodes), (model_s, forward_s, start_s, residual_data))
    space_term = pad_diff(face_diff(model_s, 1), 1) + pad_diff(face_diff(model_s, 2), 2) + pad_diff(face_diff(model_s, 3), 3)
    ordered = model_s[survey_order]
    time_sorted = pad_diff(face_diff(ordered, 0), 0)
    time_term = jnp.zeros_like(model_s).at[survey_order].set(time_sorted)
    gradient = (data_term + space_term + time_term).reshape(SURVEYS * NX, NY, NZ)
    gradient = jnp.roll(gradient, -offset, axis=0)
    adjoint_out = jnp.transpose(adjoint, (1, 0, 2, 3, 4)).reshape(SOURCES, SURVEYS * NX, NY, NZ)
    adjoint_out = jnp.roll(adjoint_out, -offset, axis=1)
    return adjoint_out, gradient
```

```python
import jax
import jax.numpy as jnp
from jax import lax
from jax.experimental import pallas as pl
from jax.experimental.pallas import tpu as pltpu
from jax.sharding import PartitionSpec as P

SURVEYS = 8
ITERS = 4


GROUND = 0.5
CENTER = 1.0
HALF_WIDTH = 0.99


def padded(shard, sides, width):
    for axis, dim in sides:
        devices, length = (lax.axis_size(axis), shard.shape[dim])
        up = [(i, (i + 1) % devices) for i in range(devices)]
        down = [(j, i) for i, j in up]
        last = lax.slice_in_dim(shard, length - width, length, axis=dim)
        leading = lax.slice_in_dim(shard, 0, width, axis=dim)
        before = lax.ppermute(last, axis, up)
        after = lax.ppermute(leading, axis, down)
        shard = jnp.concatenate([before, shard, after], axis=dim)
    return shard


def swapped(value, axis, bit):
    mask = 2**bit
    pairs = [(source, source ^ mask) for source in range(lax.axis_size(axis))]
    return lax.ppermute(value, axis, pairs)


def face_diff(field, axis):
    count = field.shape[axis]
    return lax.slice_in_dim(field, 0, count - 1, axis=axis) - lax.slice_in_dim(
        field, 1, count, axis=axis
    )


def edge_zeros(field, axis):
    shape = list(field.shape)
    shape[axis] = 1
    return jnp.zeros(shape, jnp.float32)


def pad_diff(faces, axis):
    zeros = edge_zeros(faces, axis)
    return jnp.concatenate([faces, zeros], axis=axis) - jnp.concatenate([zeros, faces], axis=axis)


def pad_sum(faces, axis):
    zeros = edge_zeros(faces, axis)
    return jnp.concatenate([faces, zeros], axis=axis) + jnp.concatenate([zeros, faces], axis=axis)


def extend(field):
    return padded(field, (("space", 1),), 1)


def layered(model, forward, warm_start, residual_data, electrodes, survey_order):
    sources, layers, rows_y, rows_z = forward.shape
    position = lax.axis_index("space")
    devices = lax.axis_size("space")
    tiles = devices // SURVEYS
    half_tiles = tiles // 2
    shifted = position + half_tiles
    tile = shifted % tiles
    survey = shifted // tiles % SURVEYS
    block = position // tiles
    rotation = jnp.where(position % tiles >= half_tiles, 1, 0).astype(jnp.int32)
    valid = jnp.ones((layers + 1,), jnp.float32)
    valid = valid.at[0].set(jnp.where(tile == 0, 0.0, 1.0))
    valid = valid.at[layers].set(jnp.where(tile == tiles - 1, 0.0, 1.0))
    valid_faces = valid[:, None, None]
    model_pad = padded(model, (("space", 0),), 1)
    sigma_pad = jnp.exp(model_pad)
    sigma = sigma_pad[1:-1]
    conduct_x = 0.5 * (sigma_pad[:-1] + sigma_pad[1:]) * valid_faces
    conduct_y = 0.5 * (sigma[:, :-1] + sigma[:, 1:])
    conduct_z = 0.5 * (sigma[:, :, :-1] + sigma[:, :, 1:])
    diagonal = (
        conduct_x[1:]
        + conduct_x[:-1]
        + pad_sum(conduct_y, 1)
        + pad_sum(conduct_z, 2)
        + GROUND * sigma
    )
    inverse_diag = (1.0 / diagonal)[None]

    def operate(field_pad):
        field = field_pad[:, 1:-1]
        flux_x = conduct_x[None] * (field_pad[:, :-1] - field_pad[:, 1:])
        total = flux_x[:, 1:] - flux_x[:, :-1]
        total = total + pad_diff(conduct_y[None] * face_diff(field, 2), 2)
        total = total + pad_diff(conduct_z[None] * face_diff(field, 3), 3)
        return total + GROUND * sigma[None] * field

    cells = layers * rows_y * rows_z
    residual = lax.dynamic_index_in_dim(residual_data, survey, 0, keepdims=False)
    local_index = electrodes - tile * cells
    inside = (local_index >= 0) & (local_index < cells)
    target = jnp.where(inside, local_index, 0)
    amount = jnp.where(inside[None, :], residual, 0.0)
    rhs = jnp.zeros((sources, cells), jnp.float32).at[:, target].add(amount)
    rhs = rhs.reshape(sources, layers, rows_y, rows_z)
    iterate = warm_start.astype(jnp.float32)
    remain = rhs - operate(extend(iterate))
    direction = remain * inverse_diag / CENTER
    weight_now = HALF_WIDTH / CENTER
    for sweep_index in range(ITERS):
        iterate = iterate + direction
        if sweep_index + 1 < ITERS:
            remain = remain - operate(extend(direction))
            weight_new = 1.0 / (2.0 * CENTER / HALF_WIDTH - weight_now)
            direction = weight_new * weight_now * direction + 2.0 * weight_new / HALF_WIDTH * (
                remain * inverse_diag
            )
            weight_now = weight_new
    both = padded(
        jnp.concatenate([forward.astype(jnp.float32), iterate], axis=0), (("space", 1),), 1
    )
    forward_pad = both[:sources]
    adjoint_pad = both[sources:]
    potential = forward_pad[:, 1:-1]
    product_x = (
        jnp.sum(
            (forward_pad[:, :-1] - forward_pad[:, 1:]) * (adjoint_pad[:, :-1] - adjoint_pad[:, 1:]),
            axis=0,
        )
        * valid_faces
    )
    terms = product_x[1:] + product_x[:-1]
    terms = terms + pad_sum(jnp.sum(face_diff(potential, 2) * face_diff(iterate, 2), axis=0), 1)
    terms = terms + pad_sum(jnp.sum(face_diff(potential, 3) * face_diff(iterate, 3), axis=0), 2)
    data_term = -sigma * (0.5 * terms + GROUND * jnp.sum(potential * iterate, axis=0))
    model_x = (model_pad[:-1] - model_pad[1:]) * valid_faces
    space_term = (
        model_x[1:]
        - model_x[:-1]
        + pad_diff(face_diff(model, 1), 1)
        + pad_diff(face_diff(model, 2), 2)
    )
    base_bit = tiles.bit_length() - 1
    collected = model
    for level in range(SURVEYS.bit_length() - 1):
        partner = swapped(collected, "space", base_bit + level)
        upper = block >> level & 1 == 1
        lower_half = jnp.where(upper, partner, collected)
        upper_half = jnp.where(upper, collected, partner)
        collected = jnp.concatenate([lower_half, upper_half], axis=0)
    all_blocks = collected.reshape(SURVEYS, layers, rows_y, rows_z)
    ranks = jnp.arange(SURVEYS, dtype=jnp.int32)
    placed = (survey_order[:, None] == ranks[None, :]).astype(jnp.float32)
    apart = jnp.abs(ranks[:, None] - ranks[None, :])
    degree = jnp.where((ranks == 0) | (ranks == SURVEYS - 1), 1.0, 2.0)
    path = jnp.where(apart == 0, degree[:, None], 0.0) - jnp.where(apart == 1, 1.0, 0.0)
    coupling = jnp.dot(
        placed.T,
        jnp.dot(path, placed, precision=lax.Precision.HIGHEST),
        precision=lax.Precision.HIGHEST,
    )
    row_weights = lax.dynamic_index_in_dim(coupling, survey, 0, keepdims=False)
    block_survey = (ranks + rotation) % SURVEYS
    picker = (block_survey[:, None] == ranks[None, :]).astype(jnp.float32)
    block_weights = jnp.dot(picker, row_weights, precision=lax.Precision.HIGHEST)
    time_term = jnp.sum(block_weights[:, None, None, None] * all_blocks, axis=0)
    return (iterate.astype(jnp.bfloat16), data_term + space_term + time_term)


def weights():
    now = HALF_WIDTH / CENTER
    steps = []
    for _ in range(ITERS - 1):
        new = 1.0 / (2.0 * CENTER / HALF_WIDTH - now)
        steps.append((new * now, 2.0 * new / HALF_WIDTH))
        now = new
    return steps


def after(x, axis):
    return pltpu.roll(x, x.shape[axis] - 1, axis)


def before(x, axis):
    return pltpu.roll(x, 1, axis)


def inner(shape, axis):
    return lax.broadcasted_iota(jnp.int32, shape, axis) < shape[axis] - 1


def face_prod(field, other, axis):
    return (field - after(field, axis)) * (other - after(other, axis))


def pack_first(info, model, warm, out):
    layers = model.shape[0]
    out[:layers] = model[...]
    for q in range(warm.shape[0]):
        out[layers * (q + 1) : layers * (q + 2)] = warm[q].astype(jnp.float32)


def pack_second(info, warm, forward, out):
    count, layers = warm.shape[:2]
    for q in range(count):
        out[layers * q : layers * (q + 1)] = warm[q].astype(jnp.float32)
    for q in range(forward.shape[0]):
        out[count * layers + q] = forward[q, 0].astype(jnp.float32)


def inject(info, residual, electrodes, out):
    tile = info[0]
    sources, _, rows_y, rows_z = out.shape
    half = residual.shape[1] // 2
    cells = out.shape[1] * rows_y * rows_z
    where_cell = lax.rem(electrodes[...] + tile * (cells // 2), cells)
    row = where_cell // rows_z
    lane = lax.rem(where_cell, rows_z)
    count = row.shape[1]
    rows = cells // rows_z
    at_row = lax.broadcasted_iota(jnp.int32, (rows, count), 0) == row
    at_row = jnp.where(at_row, 1.0, 0.0).astype(jnp.bfloat16)
    at_lane = lax.broadcasted_iota(jnp.int32, (rows_z, count), 0) == lane
    mine = jnp.where(tile == 0, residual[0, :half], residual[0, half:])
    total = None
    for _ in range(3):
        part = mine.astype(jnp.bfloat16).astype(jnp.float32)
        mine = mine - part
        right = jnp.concatenate(
            [jnp.where(at_lane, part[q : q + 1], 0.0) for q in range(sources)], axis=0
        ).astype(jnp.bfloat16)
        term = lax.dot_general(
            at_row, right, (((1,), (1,)), ((), ())), preferred_element_type=jnp.float32
        )
        total = term if total is None else total + term
    for q in range(sources):
        out[q] = total[:, q * rows_z : (q + 1) * rows_z].reshape(out.shape[1:])


def find_coefs(tile, model, other, sigma, coefs):
    layers = model.shape[0]
    full = 2 * layers
    shape = model.shape[1:]
    for i in range(layers):
        sigma[i] = jnp.exp(model[i])
        sigma[layers + i] = jnp.exp(other[i])
    in_y, in_z = inner(shape, 0), inner(shape, 1)
    middle = jnp.where(tile == 0, 1.0, 0.0)
    for i in range(full):
        mine = sigma[i]
        up = 0.5 * (mine + sigma[(i + 1) % full])
        down = 0.5 * (mine + sigma[(i - 1) % full])
        if i == layers - 1:
            up = up * middle
        if i == full - 1:
            up = up * (1.0 - middle)
        if i == layers:
            down = down * middle
        if i == 0:
            down = down * (1.0 - middle)
        right_y = jnp.where(in_y, 0.5 * (mine + after(mine, 0)), 0.0)
        right_z = jnp.where(in_z, 0.5 * (mine + after(mine, 1)), 0.0)
        left_y = before(right_y, 0)
        left_z = before(right_z, 1)
        scale = 1.0 / (up + down + right_y + left_y + right_z + left_z + GROUND * mine)
        for k, face in enumerate((up, down, right_y, left_y, right_z, left_z)):
            coefs[k, i] = face * scale
        coefs[6, i] = scale


def sweeps(coefs, rhs, start, rest, lam, mine, sent):
    count, full = start.shape[:2]

    def around(field, q, i, weight):
        here = field[q, i]
        total = weight[0] * field[q, (i + 1) % full] + weight[1] * field[q, (i + full - 1) % full]
        total = total + (weight[2] * after(here, 0) + weight[3] * before(here, 0))
        total = total + (weight[4] * after(here, 1) + weight[5] * before(here, 1))
        return here, total

    def first(i, carry):
        weight = [coefs[k, i] for k in range(7)]
        for q in range(count):
            here, total = around(start, q, i, weight)
            step = rhs[q, i] * weight[6] - here + total
            mine[0, q, i] = step
            lam[q, i] = here + step
        return carry

    lax.fori_loop(0, full, first, 0)
    for index, (keep, gain) in enumerate(weights()):
        source, target = mine.at[index % 2], mine.at[1 - index % 2]
        last = index == ITERS - 2

        def later(i, carry):
            weight = [coefs[k, i] for k in range(6)]
            for q in range(count):
                here, total = around(source, q, i, weight)
                if index > 0:
                    total = rest[q, i] - here + total
                step = keep * here + gain * total
                if not last:
                    rest[q, i] = total
                    target[q, i] = step
                lam[q, i] = lam[q, i] + step
            return carry

        lax.fori_loop(0, full, later, 0)


def solve_first(info, model, got, warm, rhs, coefs, own, sent, sigma, start, rest, lam, mine):
    layers = model.shape[0]
    count = warm.shape[0]
    find_coefs(info[0], model, got.at[:layers], sigma, coefs)
    for q in range(count):
        start[q, :layers] = warm[q].astype(jnp.float32)
        start[q, layers:] = got[layers * (q + 1) : layers * (q + 2)]
    sweeps(coefs, rhs, start, rest, lam, mine, None)
    for q in range(count):
        own[q] = lam[q, :layers]
        sent[layers * q : layers * (q + 1)] = lam[q, layers:]


def solve_second(info, coefs, got, warm, rhs, face, own_first, sent_first, own, sent, start, rest, lam, mine):
    count, layers = warm.shape[:2]
    for q in range(count):
        start[q, :layers] = warm[q].astype(jnp.float32)
        start[q, layers:] = got[layers * q : layers * (q + 1)]
    sweeps(coefs, rhs, start, rest, lam, mine, None)
    near = (layers - 1) * (1 - info[0])
    far = (layers - 1) * info[0]
    total = None
    for q in range(2 * count):
        slope = face[q, 0].astype(jnp.float32) - got[count * layers + q]
        if q < count:
            drop = own_first[q, near] - sent_first[layers * q + far]
        else:
            drop = lam[q - count, near] - lam[q - count, layers + far]
        total = slope * drop if total is None else total + slope * drop
    for q in range(count):
        own[q] = lam[q, :layers]
        sent[layers * q : layers * (q + 1)] = lam[q, layers:]
    sent[count * layers] = total


def data_sums(pairs, layers, along_x, along_y, along_z, mass):
    def add(ref, i, value, first):
        ref[i] = value if first else ref[i] + value

    for i in range(layers):
        totals = [None] * 4
        for forward, lam in pairs:
            here, other = forward(i), lam(i)
            terms = [None, face_prod(here, other, 0), face_prod(here, other, 1), here * other]
            if i + 1 < layers:
                terms[0] = (here - forward(i + 1)) * (other - lam(i + 1))
            totals = [t if a is None else (a if t is None else a + t) for a, t in zip(totals, terms)]
        if i + 1 < layers:
            along_x[i] = along_x[i] + totals[0]
        along_y[i] = along_y[i] + totals[1]
        along_z[i] = along_z[i] + totals[2]
        mass[i] = mass[i] + totals[3]


def gather_terms(info, forward_a, forward_b, forward_c, own_first, own_second, back, sums, adjoint):
    count, layers = own_first.shape[:2]
    sums[...] = jnp.zeros(sums.shape, jnp.float32)
    pairs = []
    for forward, lam in ((forward_a, own_first), (forward_b, own_second)):
        for q in range(count):
            pairs.append((
                lambda i, f=forward, q=q: f[q, i].astype(jnp.float32),
                lambda i, l=lam, q=q: l[q, i],
            ))
    for q in range(count):
        pairs.append((
            lambda i, q=q: forward_c[q, i].astype(jnp.float32),
            lambda i, q=q: back[layers * q + i],
        ))
    data_sums(pairs, layers, sums.at[0], sums.at[1], sums.at[2], sums.at[3])
    for q in range(count):
        adjoint[q] = own_first[q].astype(jnp.bfloat16)
        adjoint[count + q] = own_second[q].astype(jnp.bfloat16)
        adjoint[2 * count + q] = back[layers * q : layers * (q + 1)].astype(jnp.bfloat16)


def finish(info, sums, back, sent, forward, model, other, times, near_a, near_b, near_c, three, adjoint, gradient):
    tile = info[0]
    count, layers = forward.shape[:2]
    shape = model.shape[1:]
    pairs = []
    for q in range(count):
        pairs.append((
            lambda i, q=q: forward[q, i].astype(jnp.float32),
            lambda i, q=q: back[layers * q + i],
        ))
    in_y, in_z = inner(shape, 0), inner(shape, 1)
    low = jnp.where(tile == 0, 0.0, 1.0)
    high = 1.0 - low
    cross = back[count * layers] + sent[0]
    bridge = other[(layers - 1) * tile]
    products, falls = [low * cross], [low * (bridge - model[0])]
    for i in range(layers):
        if i + 1 < layers:
            total = sums[0, i]
            for f, l in pairs:
                total = total + (f(i) - f(i + 1)) * (l(i) - l(i + 1))
            products.append(total)
            falls.append(model[i] - model[i + 1])
        else:
            products.append(high * cross)
            falls.append(high * (model[i] - bridge))
    for i in range(layers):
        total_y, total_z, mass = sums[1, i], sums[2, i], sums[3, i]
        for f, l in pairs:
            here, there = f(i), l(i)
            total_y = total_y + face_prod(here, there, 0)
            total_z = total_z + face_prod(here, there, 1)
            mass = mass + here * there
        total_y = jnp.where(in_y, total_y, 0.0)
        total_z = jnp.where(in_z, total_z, 0.0)
        terms = products[i] + products[i + 1]
        terms = terms + (total_y + before(total_y, 0)) + (total_z + before(total_z, 1))
        value = model[i]
        fall_y = jnp.where(in_y, value - after(value, 0), 0.0)
        fall_z = jnp.where(in_z, value - after(value, 1), 0.0)
        space = falls[i + 1] - falls[i] + (fall_y - before(fall_y, 0)) + (fall_z - before(fall_z, 1))
        time = times[i] + near_a[i] + near_b[i] + near_c[i]
        gradient[i] = space + time - jnp.exp(value) * (0.5 * terms + GROUND * mass)
    spot = count * 2 * tile
    for q in range(2 * count):
        adjoint[spot + q] = three[q]
    spot = count * 2 * (1 - tile)
    for q in range(count):
        adjoint[spot + q] = three[2 * count + q]
        adjoint[spot + count + q] = back[layers * q : layers * (q + 1)].astype(jnp.bfloat16)


def time_parts(info, order, model, beside, times, part_a, part_b, part_c):
    surveys = order.shape[0]

    def rank(survey):
        found = 0
        for i in range(surveys):
            found = found + jnp.where(order[i] == survey, i, 0)
        return found

    def couple(first, second):
        a, b = rank(first), rank(second)
        ends = jnp.where(a == 0, 1, 0) + jnp.where(a == surveys - 1, 1, 0)
        value = jnp.where(a == b, 2 - ends, jnp.where(jnp.abs(a - b) == 1, -1, 0))
        return value.astype(jnp.float32)

    mine, sibling = info[1], info[2]
    for k, out in enumerate((times, part_a, part_b, part_c)):
        target = info[3 + k]
        out[...] = couple(target, mine) * model[...] + couple(target, sibling) * beside[...]


def call(kernel, info, operands, specs, out_shapes, out_specs=None, scratch=()):
    if out_specs is None:
        out_specs = [whole(s.shape) for s in out_shapes]
    several = len(out_shapes) > 1
    return pl.pallas_call(
        kernel,
        out_shape=out_shapes if several else out_shapes[0],
        grid_spec=pltpu.PrefetchScalarGridSpec(
            num_scalar_prefetch=1,
            grid=(1,),
            in_specs=specs,
            out_specs=out_specs if several else out_specs[0],
            scratch_shapes=list(scratch),
        ),
        compiler_params=pltpu.CompilerParams(vmem_limit_bytes=48 * 2**20),
    )(info, *operands)


def whole(shape):
    zeros = (0,) * len(shape)
    return pl.BlockSpec(tuple(shape), lambda g, info: zeros)


def f32(*shape):
    return jax.ShapeDtypeStruct(shape, jnp.float32)


def paired(model, forward, warm_start, residual_data, electrodes, survey_order):
    sources, layers, ny, nz = forward.shape
    half, count = sources // 2, sources // 4
    full = 2 * layers
    devices = lax.axis_size("space")
    position = lax.axis_index("space")
    tile = (position + 1) % 2
    survey = (position + 1) // 2 % SURVEYS
    sibling = (position ^ 1) + 1
    sibling = sibling // 2 % SURVEYS
    targets = [((position ^ (4 * k)) + 1) // 2 % SURVEYS for k in range(4)]
    info = jnp.stack([tile, survey, sibling] + targets).astype(jnp.int32)
    pairs = []
    for p in range(1, devices, 2):
        pairs += [(p, (p + 1) % devices), ((p + 1) % devices, p)]

    def swap(x, mask=None):
        links = pairs if mask is None else [(p, p ^ mask) for p in range(devices)]
        return lax.ppermute(x, "space", links)

    block = (count, layers, ny, nz)
    mine_a = pl.BlockSpec(block, lambda g, info: (2 * info[0], 0, 0, 0))
    mine_b = pl.BlockSpec(block, lambda g, info: (2 * info[0] + 1, 0, 0, 0))
    theirs_a = pl.BlockSpec(block, lambda g, info: (2 - 2 * info[0], 0, 0, 0))
    theirs_b = pl.BlockSpec(block, lambda g, info: (3 - 2 * info[0], 0, 0, 0))
    edge = (half, 1, ny, nz)
    my_edge = pl.BlockSpec(edge, lambda g, info: (info[0], (layers - 1) * (1 - info[0]), 0, 0))
    their_edge = pl.BlockSpec(edge, lambda g, info: (1 - info[0], (layers - 1) * (1 - info[0]), 0, 0))

    slab = (layers, ny, nz)
    first = call(
        pack_first, info, (model, warm_start), [whole(slab), theirs_a], [f32((count + 1) * layers, ny, nz)]
    )
    got_first = swap(first)
    second = call(
        pack_second, info, (warm_start, forward), [theirs_b, their_edge], [f32(count * layers + half, ny, nz)]
    )
    got_second = swap(second)
    electrodes_row = electrodes.reshape(1, -1)
    rhs = call(
        inject,
        info,
        (residual_data, electrodes_row),
        [
            pl.BlockSpec((1,) + residual_data.shape[1:], lambda g, info: (info[1], 0, 0)),
            whole(electrodes_row.shape),
        ],
        [f32(half, full, ny, nz)],
    )
    other = got_first[:layers]
    beside = swap(other, 1)
    fields = [
        pltpu.VMEM((count, full, ny, nz), jnp.float32),
        pltpu.VMEM((count, full, ny, nz), jnp.float32),
        pltpu.VMEM((count, full, ny, nz), jnp.float32),
        pltpu.VMEM((2, count, full, ny, nz), jnp.float32),
    ]
    rhs_block = (count, full, ny, nz)
    coefs, own_first, sent_first = call(
        solve_first,
        info,
        (model, got_first, warm_start, rhs),
        [whole(slab), whole(got_first.shape), mine_a, pl.BlockSpec(rhs_block, lambda g, info: (0, 0, 0, 0))],
        [f32(7, full, ny, nz), f32(*block), f32(count * layers, ny, nz)],
        scratch=[pltpu.VMEM((full, ny, nz), jnp.float32)] + fields,
    )
    back_first = swap(sent_first)
    times, part_a, part_b, part_c = pl.pallas_call(
        time_parts,
        out_shape=[f32(*slab)] * 4,
        grid_spec=pltpu.PrefetchScalarGridSpec(
            num_scalar_prefetch=2,
            grid=(1,),
            in_specs=[pl.BlockSpec(slab, lambda g, info, order: (0, 0, 0))] * 2,
            out_specs=[pl.BlockSpec(slab, lambda g, info, order: (0, 0, 0))] * 4,
        ),
    )(info, survey_order, model, beside)
    near = [swap(part, 4 * (k + 1)) for k, part in enumerate((part_a, part_b, part_c))]
    own_second, sent_second = call(
        solve_second,
        info,
        (coefs, got_second, warm_start, rhs, forward, own_first, sent_first),
        [
            whole(coefs.shape),
            whole(got_second.shape),
            mine_b,
            pl.BlockSpec(rhs_block, lambda g, info: (1, 0, 0, 0)),
            my_edge,
            whole(own_first.shape),
            whole(sent_first.shape),
        ],
        [f32(*block), f32(count * layers + 1, ny, nz)],
        scratch=fields,
    )
    back_second = swap(sent_second)
    sums, three = call(
        gather_terms,
        info,
        (forward, forward, forward, own_first, own_second, back_first),
        [mine_a, mine_b, theirs_a, whole(own_first.shape), whole(own_second.shape), whole(back_first.shape)],
        [f32(4, *slab), jax.ShapeDtypeStruct((3 * count, layers, ny, nz), jnp.bfloat16)],
    )
    adjoint, gradient = call(
        finish,
        info,
        (sums, back_second, sent_second, forward, model, got_first, times, *near, three),
        [
            whole(sums.shape),
            whole(back_second.shape),
            pl.BlockSpec((1, ny, nz), lambda g, info: (count * layers, 0, 0)),
            theirs_b,
            whole(slab),
            whole(slab),
            whole(slab),
            whole(slab),
            whole(slab),
            whole(slab),
            whole(three.shape),
        ],
        [jax.ShapeDtypeStruct(forward.shape, jnp.bfloat16), f32(*slab)],
    )
    return adjoint, gradient


def solution(mesh):
    body = paired if mesh.shape["space"] == 2 * SURVEYS else layered
    in_specs = (
        P(("groups", "space"), None, None),
        P(None, ("groups", "space"), None, None),
        P(None, ("groups", "space"), None, None),
        P("groups", None, None),
        P("groups"),
        P("groups"),
    )
    out_specs = (P(None, ("groups", "space"), None, None), P(("groups", "space"), None, None))
    return jax.shard_map(body, mesh=mesh, in_specs=in_specs, out_specs=out_specs, check_vma=False)
```

```python
import jax
import jax.numpy as jnp
from jax import lax
from jax.experimental import pallas as pl
from jax.experimental.pallas import tpu as pltpu
from jax.sharding import PartitionSpec as P

SURVEYS = 8
ITERS = 4


GROUND = 0.5
CENTER = 1.0
HALF_WIDTH = 0.99


def padded(shard, sides, width):
    for axis, dim in sides:
        devices, length = (lax.axis_size(axis), shard.shape[dim])
        up = [(i, (i + 1) % devices) for i in range(devices)]
        down = [(j, i) for i, j in up]
        last = lax.slice_in_dim(shard, length - width, length, axis=dim)
        leading = lax.slice_in_dim(shard, 0, width, axis=dim)
        before = lax.ppermute(last, axis, up)
        after = lax.ppermute(leading, axis, down)
        shard = jnp.concatenate([before, shard, after], axis=dim)
    return shard


def swapped(value, axis, bit):
    mask = 2**bit
    pairs = [(source, source ^ mask) for source in range(lax.axis_size(axis))]
    return lax.ppermute(value, axis, pairs)


def face_diff(field, axis):
    count = field.shape[axis]
    return lax.slice_in_dim(field, 0, count - 1, axis=axis) - lax.slice_in_dim(
        field, 1, count, axis=axis
    )


def edge_zeros(field, axis):
    shape = list(field.shape)
    shape[axis] = 1
    return jnp.zeros(shape, jnp.float32)


def pad_diff(faces, axis):
    zeros = edge_zeros(faces, axis)
    return jnp.concatenate([faces, zeros], axis=axis) - jnp.concatenate([zeros, faces], axis=axis)


def pad_sum(faces, axis):
    zeros = edge_zeros(faces, axis)
    return jnp.concatenate([faces, zeros], axis=axis) + jnp.concatenate([zeros, faces], axis=axis)


def extend(field):
    return padded(field, (("space", 1),), 1)


def layered(model, forward, warm_start, residual_data, electrodes, survey_order):
    sources, layers, rows_y, rows_z = forward.shape
    position = lax.axis_index("space")
    devices = lax.axis_size("space")
    tiles = devices // SURVEYS
    half_tiles = tiles // 2
    shifted = position + half_tiles
    tile = shifted % tiles
    survey = shifted // tiles % SURVEYS
    block = position // tiles
    rotation = jnp.where(position % tiles >= half_tiles, 1, 0).astype(jnp.int32)
    valid = jnp.ones((layers + 1,), jnp.float32)
    valid = valid.at[0].set(jnp.where(tile == 0, 0.0, 1.0))
    valid = valid.at[layers].set(jnp.where(tile == tiles - 1, 0.0, 1.0))
    valid_faces = valid[:, None, None]
    model_pad = padded(model, (("space", 0),), 1)
    sigma_pad = jnp.exp(model_pad)
    sigma = sigma_pad[1:-1]
    conduct_x = 0.5 * (sigma_pad[:-1] + sigma_pad[1:]) * valid_faces
    conduct_y = 0.5 * (sigma[:, :-1] + sigma[:, 1:])
    conduct_z = 0.5 * (sigma[:, :, :-1] + sigma[:, :, 1:])
    diagonal = (
        conduct_x[1:]
        + conduct_x[:-1]
        + pad_sum(conduct_y, 1)
        + pad_sum(conduct_z, 2)
        + GROUND * sigma
    )
    inverse_diag = (1.0 / diagonal)[None]

    def operate(field_pad):
        field = field_pad[:, 1:-1]
        flux_x = conduct_x[None] * (field_pad[:, :-1] - field_pad[:, 1:])
        total = flux_x[:, 1:] - flux_x[:, :-1]
        total = total + pad_diff(conduct_y[None] * face_diff(field, 2), 2)
        total = total + pad_diff(conduct_z[None] * face_diff(field, 3), 3)
        return total + GROUND * sigma[None] * field

    cells = layers * rows_y * rows_z
    residual = lax.dynamic_index_in_dim(residual_data, survey, 0, keepdims=False)
    local_index = electrodes - tile * cells
    inside = (local_index >= 0) & (local_index < cells)
    target = jnp.where(inside, local_index, 0)
    amount = jnp.where(inside[None, :], residual, 0.0)
    rhs = jnp.zeros((sources, cells), jnp.float32).at[:, target].add(amount)
    rhs = rhs.reshape(sources, layers, rows_y, rows_z)
    iterate = warm_start.astype(jnp.float32)
    remain = rhs - operate(extend(iterate))
    direction = remain * inverse_diag / CENTER
    weight_now = HALF_WIDTH / CENTER
    for sweep_index in range(ITERS):
        iterate = iterate + direction
        if sweep_index + 1 < ITERS:
            remain = remain - operate(extend(direction))
            weight_new = 1.0 / (2.0 * CENTER / HALF_WIDTH - weight_now)
            direction = weight_new * weight_now * direction + 2.0 * weight_new / HALF_WIDTH * (
                remain * inverse_diag
            )
            weight_now = weight_new
    both = padded(
        jnp.concatenate([forward.astype(jnp.float32), iterate], axis=0), (("space", 1),), 1
    )
    forward_pad = both[:sources]
    adjoint_pad = both[sources:]
    potential = forward_pad[:, 1:-1]
    product_x = (
        jnp.sum(
            (forward_pad[:, :-1] - forward_pad[:, 1:]) * (adjoint_pad[:, :-1] - adjoint_pad[:, 1:]),
            axis=0,
        )
        * valid_faces
    )
    terms = product_x[1:] + product_x[:-1]
    terms = terms + pad_sum(jnp.sum(face_diff(potential, 2) * face_diff(iterate, 2), axis=0), 1)
    terms = terms + pad_sum(jnp.sum(face_diff(potential, 3) * face_diff(iterate, 3), axis=0), 2)
    data_term = -sigma * (0.5 * terms + GROUND * jnp.sum(potential * iterate, axis=0))
    model_x = (model_pad[:-1] - model_pad[1:]) * valid_faces
    space_term = (
        model_x[1:]
        - model_x[:-1]
        + pad_diff(face_diff(model, 1), 1)
        + pad_diff(face_diff(model, 2), 2)
    )
    base_bit = tiles.bit_length() - 1
    collected = model
    for level in range(SURVEYS.bit_length() - 1):
        partner = swapped(collected, "space", base_bit + level)
        upper = block >> level & 1 == 1
        lower_half = jnp.where(upper, partner, collected)
        upper_half = jnp.where(upper, collected, partner)
        collected = jnp.concatenate([lower_half, upper_half], axis=0)
    all_blocks = collected.reshape(SURVEYS, layers, rows_y, rows_z)
    ranks = jnp.arange(SURVEYS, dtype=jnp.int32)
    placed = (survey_order[:, None] == ranks[None, :]).astype(jnp.float32)
    apart = jnp.abs(ranks[:, None] - ranks[None, :])
    degree = jnp.where((ranks == 0) | (ranks == SURVEYS - 1), 1.0, 2.0)
    path = jnp.where(apart == 0, degree[:, None], 0.0) - jnp.where(apart == 1, 1.0, 0.0)
    coupling = jnp.dot(
        placed.T,
        jnp.dot(path, placed, precision=lax.Precision.HIGHEST),
        precision=lax.Precision.HIGHEST,
    )
    row_weights = lax.dynamic_index_in_dim(coupling, survey, 0, keepdims=False)
    block_survey = (ranks + rotation) % SURVEYS
    picker = (block_survey[:, None] == ranks[None, :]).astype(jnp.float32)
    block_weights = jnp.dot(picker, row_weights, precision=lax.Precision.HIGHEST)
    time_term = jnp.sum(block_weights[:, None, None, None] * all_blocks, axis=0)
    return (iterate.astype(jnp.bfloat16), data_term + space_term + time_term)


def weights():
    now = HALF_WIDTH / CENTER
    steps = []
    for _ in range(ITERS - 1):
        new = 1.0 / (2.0 * CENTER / HALF_WIDTH - now)
        steps.append((new * now, 2.0 * new / HALF_WIDTH))
        now = new
    return steps


def after(x, axis):
    return pltpu.roll(x, x.shape[axis] - 1, axis)


def before(x, axis):
    return pltpu.roll(x, 1, axis)


def inner(shape, axis):
    return lax.broadcasted_iota(jnp.int32, shape, axis) < shape[axis] - 1


def face_prod(field, other, axis):
    return (field - after(field, axis)) * (other - after(other, axis))


def pack(info, warm, forward, first, second, held, edges, sems):
    tile = info[0]
    half, layers = held.shape[:2]
    count = half // 2
    theirs = half * (1 - tile)
    face = (layers - 1) * (1 - tile)
    copies = [
        pltpu.make_async_copy(warm.at[pl.ds(theirs, count)], held.at[:count], sems.at[0]),
        pltpu.make_async_copy(warm.at[pl.ds(theirs + count, count)], held.at[count:], sems.at[1]),
        pltpu.make_async_copy(forward.at[pl.ds(theirs, half), pl.ds(face, 1)], edges, sems.at[2]),
    ]
    for copy in copies:
        copy.start()
    copies[0].wait()
    for q in range(count):
        first[layers * q : layers * (q + 1)] = held[q].astype(jnp.float32)
    copies[1].wait()
    for q in range(count):
        second[layers * q : layers * (q + 1)] = held[count + q].astype(jnp.float32)
    copies[2].wait()
    for q in range(half):
        second[count * layers + q] = edges[q, 0].astype(jnp.float32)


def inject(info, order, residual, electrodes, out, weights):
    tile = info[0]
    surveys = order.shape[0]
    ranks = []
    for k in range(6):
        found = 0
        for i in range(surveys):
            found = found + jnp.where(order[i] == info[1 + k], i, 0)
        ranks.append(found)
    for k in range(4):
        a = ranks[2 + k]
        ends = jnp.where(a == 0, 1, 0) + jnp.where(a == surveys - 1, 1, 0)
        for m in range(2):
            b = ranks[m]
            value = jnp.where(a == b, 2 - ends, jnp.where(jnp.abs(a - b) == 1, -1, 0))
            weights[2 * k + m] = value.astype(jnp.float32)
    sources, _, rows_y, rows_z = out.shape
    half = residual.shape[1] // 2
    cells = out.shape[1] * rows_y * rows_z
    where_cell = lax.rem(electrodes[...] + tile * (cells // 2), cells)
    row = where_cell // rows_z
    lane = lax.rem(where_cell, rows_z)
    count = row.shape[1]
    rows = cells // rows_z
    at_row = lax.broadcasted_iota(jnp.int32, (rows, count), 0) == row
    at_row = jnp.where(at_row, 1.0, 0.0).astype(jnp.bfloat16)
    at_lane = lax.broadcasted_iota(jnp.int32, (rows_z, count), 0) == lane
    mine = residual[info[1]]
    mine = jnp.where(tile == 0, mine[:half], mine[half:])
    total = None
    for _ in range(3):
        part = mine.astype(jnp.bfloat16).astype(jnp.float32)
        mine = mine - part
        right = jnp.concatenate(
            [jnp.where(at_lane, part[q : q + 1], 0.0) for q in range(sources)], axis=0
        ).astype(jnp.bfloat16)
        term = lax.dot_general(
            at_row, right, (((1,), (1,)), ((), ())), preferred_element_type=jnp.float32
        )
        total = term if total is None else total + term
    for q in range(sources):
        out[q] = total[:, q * rows_z : (q + 1) * rows_z].reshape(out.shape[1:])


def find_coefs(info, model, other, coefs, sigma):
    tile = info[0]
    layers = model.shape[0]
    full = 2 * layers
    shape = model.shape[1:]
    for i in range(layers):
        sigma[i] = jnp.exp(model[i])
        sigma[layers + i] = jnp.exp(other[i])
    in_y, in_z = inner(shape, 0), inner(shape, 1)
    middle = jnp.where(tile == 0, 1.0, 0.0)
    for i in range(full):
        mine = sigma[i]
        up = 0.5 * (mine + sigma[(i + 1) % full])
        down = 0.5 * (mine + sigma[(i - 1) % full])
        if i == layers - 1:
            up = up * middle
        if i == full - 1:
            up = up * (1.0 - middle)
        if i == layers:
            down = down * middle
        if i == 0:
            down = down * (1.0 - middle)
        right_y = jnp.where(in_y, 0.5 * (mine + after(mine, 0)), 0.0)
        right_z = jnp.where(in_z, 0.5 * (mine + after(mine, 1)), 0.0)
        left_y = before(right_y, 0)
        left_z = before(right_z, 1)
        scale = 1.0 / (up + down + right_y + left_y + right_z + left_z + GROUND * mine)
        for k, face in enumerate((up, down, right_y, left_y, right_z, left_z)):
            coefs[k, i] = face * scale
        coefs[6, i] = scale


def sweeps(coefs, rhs, base, start, rest, lam, mine):
    count, full = start.shape[:2]

    def around(field, q, i, weight):
        here = field[q, i]
        total = weight[0] * field[q, (i + 1) % full] + weight[1] * field[q, (i + full - 1) % full]
        total = total + (weight[2] * after(here, 0) + weight[3] * before(here, 0))
        total = total + (weight[4] * after(here, 1) + weight[5] * before(here, 1))
        return here, total

    def first(i, carry):
        weight = [coefs[k, i] for k in range(7)]
        for q in range(count):
            here, total = around(start, q, i, weight)
            step = rhs[base + q, i] * weight[6] - here + total
            mine[0, q, i] = step
            lam[q, i] = here + step
        return carry

    lax.fori_loop(0, full, first, 0)
    for index, (keep, gain) in enumerate(weights()):
        source, target = mine.at[index % 2], mine.at[1 - index % 2]
        last = index == ITERS - 2

        def later(i, carry):
            weight = [coefs[k, i] for k in range(6)]
            for q in range(count):
                here, total = around(source, q, i, weight)
                if index > 0:
                    total = rest[q, i] - here + total
                step = keep * here + gain * total
                if not last:
                    rest[q, i] = total
                    target[q, i] = step
                lam[q, i] = lam[q, i] + step
            return carry

        lax.fori_loop(0, full, later, 0)


def load_start(warm, source, got, start):
    count, full = start.shape[:2]
    layers = full // 2
    for q in range(count):
        start[q, :layers] = warm[source + q].astype(jnp.float32)
        start[q, layers:] = got[layers * q : layers * (q + 1)]


def solve_first(info, coefs, got, warm, rhs, own, sent, start, rest, lam, mine):
    count, layers = own.shape[:2]
    load_start(warm, 2 * count * info[0], got, start)
    sweeps(coefs, rhs, 0, start, rest, lam, mine)
    for q in range(count):
        own[q] = lam[q, :layers]
        sent[layers * q : layers * (q + 1)] = lam[q, layers:]


def solve_second(info, coefs, got, warm, rhs, forward, own_first, sent_first, times, near_a, near_b, near_c, own, sent, time, start, rest, lam, mine):
    count, layers = own.shape[:2]
    time[...] = (times[...] + near_a[...]) + (near_b[...] + near_c[...])
    source = 2 * count * info[0]
    load_start(warm, source + count, got, start)
    sweeps(coefs, rhs, count, start, rest, lam, mine)
    near = (layers - 1) * (1 - info[0])
    far = (layers - 1) * info[0]
    total = None
    for q in range(2 * count):
        slope = forward[source + q, near].astype(jnp.float32) - got[count * layers + q]
        if q < count:
            drop = own_first[q, near] - sent_first[layers * q + far]
        else:
            drop = lam[q - count, near] - lam[q - count, layers + far]
        total = slope * drop if total is None else total + slope * drop
    for q in range(count):
        own[q] = lam[q, :layers]
        sent[layers * q : layers * (q + 1)] = lam[q, layers:]
    sent[count * layers] = total


def data_sums(pairs, layers, along_x, along_y, along_z, mass):
    def add(ref, i, value, first):
        ref[i] = value if first else ref[i] + value

    for i in range(layers):
        totals = [None] * 4
        for forward, lam in pairs:
            here, other = forward(i), lam(i)
            terms = [None, face_prod(here, other, 0), face_prod(here, other, 1), here * other]
            if i + 1 < layers:
                terms[0] = (here - forward(i + 1)) * (other - lam(i + 1))
            totals = [t if a is None else (a if t is None else a + t) for a, t in zip(totals, terms)]
        if i + 1 < layers:
            along_x[i] = along_x[i] + totals[0]
        along_y[i] = along_y[i] + totals[1]
        along_z[i] = along_z[i] + totals[2]
        mass[i] = mass[i] + totals[3]


def gather_terms(info, forward, own_first, own_second, back, sums, adjoint, rounded, sems):
    count, layers = own_first.shape[:2]
    tile = info[0]
    mine, theirs = 2 * count * tile, 2 * count * (1 - tile)
    for q in range(count):
        rounded[q] = own_first[q].astype(jnp.bfloat16)
        rounded[count + q] = own_second[q].astype(jnp.bfloat16)
        rounded[2 * count + q] = back[layers * q : layers * (q + 1)].astype(jnp.bfloat16)
    copies = [
        pltpu.make_async_copy(rounded.at[: 2 * count], adjoint.at[pl.ds(mine, 2 * count)], sems.at[0]),
        pltpu.make_async_copy(rounded.at[2 * count :], adjoint.at[pl.ds(theirs, count)], sems.at[1]),
    ]
    for copy in copies:
        copy.start()
    sums[...] = jnp.zeros(sums.shape, jnp.float32)
    pairs = []
    for q in range(count):
        pairs.append((mine + q, lambda i, q=q: own_first[q, i]))
        pairs.append((mine + count + q, lambda i, q=q: own_second[q, i]))
        pairs.append((theirs + q, lambda i, q=q: back[layers * q + i]))
    pairs = [(lambda i, s=s: forward[s, i].astype(jnp.float32), lam) for s, lam in pairs]
    data_sums(pairs, layers, sums.at[0], sums.at[1], sums.at[2], sums.at[3])
    for copy in copies:
        copy.wait()


def finish(info, sums, back, sent, forward, model, other, times, kept, adjoint, gradient, rounded, result, sems):
    tile = info[0]
    count, layers = rounded.shape[:2]
    theirs = 2 * count * (1 - tile) + count
    for q in range(count):
        rounded[q] = back[layers * q : layers * (q + 1)].astype(jnp.bfloat16)
    copies = [pltpu.make_async_copy(rounded, adjoint.at[pl.ds(theirs, count)], sems.at[layers])]
    copies[0].start()
    shape = model.shape[1:]
    pairs = []
    for q in range(count):
        pairs.append((
            lambda i, q=q: forward[theirs + q, i].astype(jnp.float32),
            lambda i, q=q: back[layers * q + i],
        ))
    in_y, in_z = inner(shape, 0), inner(shape, 1)
    low = jnp.where(tile == 0, 0.0, 1.0)
    high = 1.0 - low
    cross = back[count * layers] + sent[count * layers]
    bridge = other[(layers - 1) * tile]
    products, falls = [low * cross], [low * (bridge - model[0])]
    for i in range(layers):
        if i + 1 < layers:
            total = sums[0, i]
            for f, l in pairs:
                total = total + (f(i) - f(i + 1)) * (l(i) - l(i + 1))
            products.append(total)
            falls.append(model[i] - model[i + 1])
        else:
            products.append(high * cross)
            falls.append(high * (model[i] - bridge))
    for i in range(layers):
        total_y, total_z, mass = sums[1, i], sums[2, i], sums[3, i]
        for f, l in pairs:
            here, there = f(i), l(i)
            total_y = total_y + face_prod(here, there, 0)
            total_z = total_z + face_prod(here, there, 1)
            mass = mass + here * there
        total_y = jnp.where(in_y, total_y, 0.0)
        total_z = jnp.where(in_z, total_z, 0.0)
        terms = products[i] + products[i + 1]
        terms = terms + (total_y + before(total_y, 0)) + (total_z + before(total_z, 1))
        value = model[i]
        fall_y = jnp.where(in_y, value - after(value, 0), 0.0)
        fall_z = jnp.where(in_z, value - after(value, 1), 0.0)
        space = falls[i + 1] - falls[i] + (fall_y - before(fall_y, 0)) + (fall_z - before(fall_z, 1))
        result[i] = space + times[i] - jnp.exp(value) * (0.5 * terms + GROUND * mass)
        copies.append(pltpu.make_async_copy(result.at[i], gradient.at[i], sems.at[i]))
        copies[-1].start()
    for copy in copies:
        copy.wait()


def time_parts(weights, model, beside, times, part_a, part_b, part_c):
    for k, out in enumerate((times, part_a, part_b, part_c)):
        out[...] = weights[2 * k] * model[...] + weights[2 * k + 1] * beside[...]


V, S, H = pltpu.VMEM, pltpu.SMEM, pltpu.HBM


def call(kernel, operands, spaces, out_shapes, out_spaces=None, scratch=(), aliases=None, micros=1, room=16):
    several = len(out_shapes) > 1
    specs = [pl.BlockSpec(memory_space=m) for m in spaces]
    out_specs = [pl.BlockSpec(memory_space=m) for m in out_spaces or [V] * len(out_shapes)]
    return pl.pallas_call(
        kernel,
        out_shape=out_shapes if several else out_shapes[0],
        in_specs=specs,
        out_specs=out_specs if several else out_specs[0],
        scratch_shapes=list(scratch),
        input_output_aliases=aliases or {},
        compiler_params=pltpu.CompilerParams(vmem_limit_bytes=room * 2**20),
        cost_estimate=pl.CostEstimate(
            flops=micros * 10**9, bytes_accessed=micros * 3 * 10**6, transcendentals=0
        ),
    )(*operands)


def f32(*shape):
    return jax.ShapeDtypeStruct(shape, jnp.float32)


def bf16(*shape):
    return jax.ShapeDtypeStruct(shape, jnp.bfloat16)


def paired(model, forward, warm_start, residual_data, electrodes, survey_order):
    sources, layers, ny, nz = forward.shape
    half, count = sources // 2, sources // 4
    full = 2 * layers
    devices = lax.axis_size("space")
    position = lax.axis_index("space")
    places = [position, position ^ 1] + [position ^ (4 * k) for k in range(4)]
    tile = (position + 1) & 1
    info = jnp.stack([tile] + [((p + 1) >> 1) & (SURVEYS - 1) for p in places]).astype(jnp.int32)
    pairs = []
    for p in range(1, devices, 2):
        pairs += [(p, (p + 1) % devices), ((p + 1) % devices, p)]

    def swap(x, mask=None):
        links = pairs if mask is None else [(p, p ^ mask) for p in range(devices)]
        return lax.ppermute(x, "space", links)

    dma = pltpu.SemaphoreType.DMA
    slab = (layers, ny, nz)
    other = swap(model)
    first, second = call(
        pack,
        (info, warm_start, forward),
        (S, H, H),
        [f32(count * layers, ny, nz), f32(count * layers + half, ny, nz)],
        scratch=[V((half, *slab), jnp.bfloat16), V((half, 1, ny, nz), jnp.bfloat16), dma((3,))],
        room=60,
    )
    got_first = swap(first)
    got_second = swap(second)
    rhs, weights_time = call(
        inject,
        (info, survey_order, residual_data, electrodes.reshape(1, -1)),
        (S, S, V, V),
        [f32(half, full, ny, nz), f32(8)],
        [V, S],
    )
    beside = swap(other, 1)
    coefs = call(
        find_coefs,
        (info, model, other),
        (S, V, V),
        [f32(7, full, ny, nz)],
        scratch=[V((full, ny, nz), jnp.float32)],
    )
    times, part_a, part_b, part_c = call(
        time_parts, (weights_time, model, beside), (S, V, V), [f32(*slab)] * 4
    )
    near = [swap(part, 4 * (k + 1)) for k, part in enumerate((part_a, part_b, part_c))]
    field = V((count, full, ny, nz), jnp.float32)
    fields = [field, field, field, V((2, count, full, ny, nz), jnp.float32)]
    block = f32(count, *slab)
    own_first, sent_first = call(
        solve_first,
        (info, coefs, got_first, warm_start, rhs),
        (S, V, V, V, V),
        [block, f32(count * layers, ny, nz)],
        scratch=fields,
        micros=4,
    )
    back_first = swap(sent_first)
    own_second, sent_second, time = call(
        solve_second,
        (info, coefs, got_second, warm_start, rhs, forward, own_first, sent_first, times, *near),
        (S, V, V, V, V, V, V, V, V, V, V, V),
        [block, f32(count * layers + 1, ny, nz), f32(*slab)],
        scratch=fields,
        micros=4,
    )
    back_second = swap(sent_second)
    sums, kept = call(
        gather_terms,
        (info, forward, own_first, own_second, back_first),
        (S, V, V, V, V),
        [f32(4, *slab), bf16(*forward.shape)],
        [V, H],
        scratch=[V((3 * count, *slab), jnp.bfloat16), dma((2,))],
        micros=2,
    )
    adjoint, gradient = call(
        finish,
        (info, sums, back_second, sent_second, forward, model, other, time, kept),
        (S, V, V, V, V, V, V, V, H),
        [bf16(*forward.shape), f32(*slab)],
        [H, H],
        scratch=[V((count, *slab), jnp.bfloat16), V(slab, jnp.float32), dma((layers + 1,))],
        aliases={8: 0},
    )
    return adjoint, gradient


def solution(mesh):
    body = paired if mesh.shape["space"] == 2 * SURVEYS else layered
    in_specs = (
        P(("groups", "space"), None, None),
        P(None, ("groups", "space"), None, None),
        P(None, ("groups", "space"), None, None),
        P("groups", None, None),
        P("groups"),
        P("groups"),
    )
    out_specs = (P(None, ("groups", "space"), None, None), P(("groups", "space"), None, None))
    return jax.shard_map(body, mesh=mesh, in_specs=in_specs, out_specs=out_specs, check_vma=False)
```

```python
import jax
import jax.numpy as jnp
from jax import lax
from jax.experimental import pallas as pl
from jax.experimental.pallas import tpu as pltpu
from jax.sharding import PartitionSpec as P

SURVEYS = 8
ITERS = 4


GROUND = 0.5
CENTER = 1.0
HALF_WIDTH = 0.99


def padded(shard, sides, width):
    for axis, dim in sides:
        devices, length = (lax.axis_size(axis), shard.shape[dim])
        up = [(i, (i + 1) % devices) for i in range(devices)]
        down = [(j, i) for i, j in up]
        last = lax.slice_in_dim(shard, length - width, length, axis=dim)
        leading = lax.slice_in_dim(shard, 0, width, axis=dim)
        before = lax.ppermute(last, axis, up)
        after = lax.ppermute(leading, axis, down)
        shard = jnp.concatenate([before, shard, after], axis=dim)
    return shard


def swapped(value, axis, bit):
    mask = 2**bit
    pairs = [(source, source ^ mask) for source in range(lax.axis_size(axis))]
    return lax.ppermute(value, axis, pairs)


def face_diff(field, axis):
    count = field.shape[axis]
    return lax.slice_in_dim(field, 0, count - 1, axis=axis) - lax.slice_in_dim(
        field, 1, count, axis=axis
    )


def edge_zeros(field, axis):
    shape = list(field.shape)
    shape[axis] = 1
    return jnp.zeros(shape, jnp.float32)


def pad_diff(faces, axis):
    zeros = edge_zeros(faces, axis)
    return jnp.concatenate([faces, zeros], axis=axis) - jnp.concatenate([zeros, faces], axis=axis)


def pad_sum(faces, axis):
    zeros = edge_zeros(faces, axis)
    return jnp.concatenate([faces, zeros], axis=axis) + jnp.concatenate([zeros, faces], axis=axis)


def extend(field):
    return padded(field, (("space", 1),), 1)


def layered(model, forward, warm_start, residual_data, electrodes, survey_order):
    sources, layers, rows_y, rows_z = forward.shape
    position = lax.axis_index("space")
    devices = lax.axis_size("space")
    tiles = devices // SURVEYS
    half_tiles = tiles // 2
    shifted = position + half_tiles
    tile = shifted % tiles
    survey = shifted // tiles % SURVEYS
    block = position // tiles
    rotation = jnp.where(position % tiles >= half_tiles, 1, 0).astype(jnp.int32)
    valid = jnp.ones((layers + 1,), jnp.float32)
    valid = valid.at[0].set(jnp.where(tile == 0, 0.0, 1.0))
    valid = valid.at[layers].set(jnp.where(tile == tiles - 1, 0.0, 1.0))
    valid_faces = valid[:, None, None]
    model_pad = padded(model, (("space", 0),), 1)
    sigma_pad = jnp.exp(model_pad)
    sigma = sigma_pad[1:-1]
    conduct_x = 0.5 * (sigma_pad[:-1] + sigma_pad[1:]) * valid_faces
    conduct_y = 0.5 * (sigma[:, :-1] + sigma[:, 1:])
    conduct_z = 0.5 * (sigma[:, :, :-1] + sigma[:, :, 1:])
    diagonal = (
        conduct_x[1:]
        + conduct_x[:-1]
        + pad_sum(conduct_y, 1)
        + pad_sum(conduct_z, 2)
        + GROUND * sigma
    )
    inverse_diag = (1.0 / diagonal)[None]

    def operate(field_pad):
        field = field_pad[:, 1:-1]
        flux_x = conduct_x[None] * (field_pad[:, :-1] - field_pad[:, 1:])
        total = flux_x[:, 1:] - flux_x[:, :-1]
        total = total + pad_diff(conduct_y[None] * face_diff(field, 2), 2)
        total = total + pad_diff(conduct_z[None] * face_diff(field, 3), 3)
        return total + GROUND * sigma[None] * field

    cells = layers * rows_y * rows_z
    residual = lax.dynamic_index_in_dim(residual_data, survey, 0, keepdims=False)
    local_index = electrodes - tile * cells
    inside = (local_index >= 0) & (local_index < cells)
    target = jnp.where(inside, local_index, 0)
    amount = jnp.where(inside[None, :], residual, 0.0)
    rhs = jnp.zeros((sources, cells), jnp.float32).at[:, target].add(amount)
    rhs = rhs.reshape(sources, layers, rows_y, rows_z)
    iterate = warm_start.astype(jnp.float32)
    remain = rhs - operate(extend(iterate))
    direction = remain * inverse_diag / CENTER
    weight_now = HALF_WIDTH / CENTER
    for sweep_index in range(ITERS):
        iterate = iterate + direction
        if sweep_index + 1 < ITERS:
            remain = remain - operate(extend(direction))
            weight_new = 1.0 / (2.0 * CENTER / HALF_WIDTH - weight_now)
            direction = weight_new * weight_now * direction + 2.0 * weight_new / HALF_WIDTH * (
                remain * inverse_diag
            )
            weight_now = weight_new
    both = padded(
        jnp.concatenate([forward.astype(jnp.float32), iterate], axis=0), (("space", 1),), 1
    )
    forward_pad = both[:sources]
    adjoint_pad = both[sources:]
    potential = forward_pad[:, 1:-1]
    product_x = (
        jnp.sum(
            (forward_pad[:, :-1] - forward_pad[:, 1:]) * (adjoint_pad[:, :-1] - adjoint_pad[:, 1:]),
            axis=0,
        )
        * valid_faces
    )
    terms = product_x[1:] + product_x[:-1]
    terms = terms + pad_sum(jnp.sum(face_diff(potential, 2) * face_diff(iterate, 2), axis=0), 1)
    terms = terms + pad_sum(jnp.sum(face_diff(potential, 3) * face_diff(iterate, 3), axis=0), 2)
    data_term = -sigma * (0.5 * terms + GROUND * jnp.sum(potential * iterate, axis=0))
    model_x = (model_pad[:-1] - model_pad[1:]) * valid_faces
    space_term = (
        model_x[1:]
        - model_x[:-1]
        + pad_diff(face_diff(model, 1), 1)
        + pad_diff(face_diff(model, 2), 2)
    )
    base_bit = tiles.bit_length() - 1
    collected = model
    for level in range(SURVEYS.bit_length() - 1):
        partner = swapped(collected, "space", base_bit + level)
        upper = block >> level & 1 == 1
        lower_half = jnp.where(upper, partner, collected)
        upper_half = jnp.where(upper, collected, partner)
        collected = jnp.concatenate([lower_half, upper_half], axis=0)
    all_blocks = collected.reshape(SURVEYS, layers, rows_y, rows_z)
    ranks = jnp.arange(SURVEYS, dtype=jnp.int32)
    placed = (survey_order[:, None] == ranks[None, :]).astype(jnp.float32)
    apart = jnp.abs(ranks[:, None] - ranks[None, :])
    degree = jnp.where((ranks == 0) | (ranks == SURVEYS - 1), 1.0, 2.0)
    path = jnp.where(apart == 0, degree[:, None], 0.0) - jnp.where(apart == 1, 1.0, 0.0)
    coupling = jnp.dot(
        placed.T,
        jnp.dot(path, placed, precision=lax.Precision.HIGHEST),
        precision=lax.Precision.HIGHEST,
    )
    row_weights = lax.dynamic_index_in_dim(coupling, survey, 0, keepdims=False)
    block_survey = (ranks + rotation) % SURVEYS
    picker = (block_survey[:, None] == ranks[None, :]).astype(jnp.float32)
    block_weights = jnp.dot(picker, row_weights, precision=lax.Precision.HIGHEST)
    time_term = jnp.sum(block_weights[:, None, None, None] * all_blocks, axis=0)
    return (iterate.astype(jnp.bfloat16), data_term + space_term + time_term)


def weights():
    now = HALF_WIDTH / CENTER
    steps = []
    for _ in range(ITERS - 1):
        new = 1.0 / (2.0 * CENTER / HALF_WIDTH - now)
        steps.append((new * now, 2.0 * new / HALF_WIDTH))
        now = new
    return steps


def after(x, axis):
    return pltpu.roll(x, x.shape[axis] - 1, axis)


def before(x, axis):
    return pltpu.roll(x, 1, axis)


def inner(shape, axis):
    return lax.broadcasted_iota(jnp.int32, shape, axis) < shape[axis] - 1


def face_prod(field, other, axis):
    return (field - after(field, axis)) * (other - after(other, axis))


def tile_of(position):
    return (position + 1) & 1


def survey_of(position):
    return ((position + 1) >> 1) & (SURVEYS - 1)


def inject(order, residual, electrodes, out, weights):
    position = lax.axis_index("space")
    tile = tile_of(position)
    surveys = order.shape[0]
    ranks = []
    for place in [position, position ^ 1] + [position ^ (4 * k) for k in range(4)]:
        found = 0
        for i in range(surveys):
            found = found + jnp.where(order[i] == survey_of(place), i, 0)
        ranks.append(found)
    for k in range(4):
        a = ranks[2 + k]
        ends = jnp.where(a == 0, 1, 0) + jnp.where(a == surveys - 1, 1, 0)
        for m in range(2):
            b = ranks[m]
            value = jnp.where(a == b, 2 - ends, jnp.where(jnp.abs(a - b) == 1, -1, 0))
            weights[2 * k + m] = value.astype(jnp.float32)
    sources, _, rows_y, rows_z = out.shape
    half = residual.shape[1] // 2
    cells = out.shape[1] * rows_y * rows_z
    where_cell = lax.rem(electrodes[...] + tile * (cells // 2), cells)
    row = where_cell // rows_z
    lane = lax.rem(where_cell, rows_z)
    count = row.shape[1]
    rows = cells // rows_z
    at_row = lax.broadcasted_iota(jnp.int32, (rows, count), 0) == row
    at_row = jnp.where(at_row, 1.0, 0.0).astype(jnp.bfloat16)
    at_lane = lax.broadcasted_iota(jnp.int32, (rows_z, count), 0) == lane
    mine = residual[survey_of(position)]
    mine = jnp.where(tile == 0, mine[:half], mine[half:])
    total = None
    for _ in range(3):
        part = mine.astype(jnp.bfloat16).astype(jnp.float32)
        mine = mine - part
        right = jnp.concatenate(
            [jnp.where(at_lane, part[q : q + 1], 0.0) for q in range(sources)], axis=0
        ).astype(jnp.bfloat16)
        term = lax.dot_general(
            at_row, right, (((1,), (1,)), ((), ())), preferred_element_type=jnp.float32
        )
        total = term if total is None else total + term
    for q in range(sources):
        out[q] = total[:, q * rows_z : (q + 1) * rows_z].reshape(out.shape[1:])


def prepare(model, other, warm, forward, coefs, second, sigma):
    tile = tile_of(lax.axis_index("space"))
    half = warm.shape[0] // 2
    count, layers = half // 2, model.shape[0]
    theirs = half * (1 - tile)
    face = (layers - 1) * (1 - tile)
    for q in range(count):
        second[layers * q : layers * (q + 1)] = warm[theirs + count + q].astype(jnp.float32)
    for q in range(half):
        second[count * layers + q] = forward[theirs + q, face].astype(jnp.float32)
    full = 2 * layers
    shape = model.shape[1:]
    for i in range(layers):
        sigma[i] = jnp.exp(model[i])
        sigma[layers + i] = jnp.exp(other[i])
    in_y, in_z = inner(shape, 0), inner(shape, 1)
    middle = jnp.where(tile == 0, 1.0, 0.0)
    for i in range(full):
        mine = sigma[i]
        up = 0.5 * (mine + sigma[(i + 1) % full])
        down = 0.5 * (mine + sigma[(i - 1) % full])
        if i == layers - 1:
            up = up * middle
        if i == full - 1:
            up = up * (1.0 - middle)
        if i == layers:
            down = down * middle
        if i == 0:
            down = down * (1.0 - middle)
        right_y = jnp.where(in_y, 0.5 * (mine + after(mine, 0)), 0.0)
        right_z = jnp.where(in_z, 0.5 * (mine + after(mine, 1)), 0.0)
        left_y = before(right_y, 0)
        left_z = before(right_z, 1)
        scale = 1.0 / (up + down + right_y + left_y + right_z + left_z + GROUND * mine)
        for k, face in enumerate((up, down, right_y, left_y, right_z, left_z)):
            coefs[k, i] = face * scale
        coefs[6, i] = scale


def sweeps(coefs, rhs, base, start, rest, lam, mine):
    count, full = start.shape[:2]

    def around(field, q, i, weight):
        here = field[q, i]
        total = weight[0] * field[q, (i + 1) % full] + weight[1] * field[q, (i + full - 1) % full]
        total = total + (weight[2] * after(here, 0) + weight[3] * before(here, 0))
        total = total + (weight[4] * after(here, 1) + weight[5] * before(here, 1))
        return here, total

    def first(i, carry):
        weight = [coefs[k, i] for k in range(7)]
        for q in range(count):
            here, total = around(start, q, i, weight)
            step = rhs[base + q, i] * weight[6] - here + total
            mine[0, q, i] = step
            lam[q, i] = here + step
        return carry

    lax.fori_loop(0, full, first, 0, unroll=full)
    for index, (keep, gain) in enumerate(weights()):
        source, target = mine.at[index % 2], mine.at[1 - index % 2]
        last = index == ITERS - 2

        def later(i, carry):
            weight = [coefs[k, i] for k in range(6)]
            for q in range(count):
                here, total = around(source, q, i, weight)
                if index > 0:
                    total = rest[q, i] - here + total
                step = keep * here + gain * total
                if not last:
                    rest[q, i] = total
                    target[q, i] = step
                lam[q, i] = lam[q, i] + step
            return carry

        lax.fori_loop(0, full, later, 0, unroll=full)


def load_start(warm, source, got, start):
    count, full = start.shape[:2]
    layers = full // 2
    for q in range(count):
        start[q, :layers] = warm[source + q].astype(jnp.float32)
        start[q, layers:] = got[q] if len(got.shape) == 4 else got[layers * q : layers * (q + 1)]


def solve_first(coefs, got, warm, rhs, other, own, sent, relay, start, rest, lam, mine):
    count, layers = own.shape[:2]
    relay[...] = other[...]
    load_start(warm, 2 * count * tile_of(lax.axis_index("space")), got, start)
    sweeps(coefs, rhs, 0, start, rest, lam, mine)
    for q in range(count):
        own[q] = lam[q, :layers]
        sent[layers * q : layers * (q + 1)] = lam[q, layers:]


def solve_second(weights, model, beside, coefs, got, warm, rhs, forward, own_first, sent_first, own, sent, times, part_a, part_b, part_c, start, rest, lam, mine):
    count, layers = own.shape[:2]
    tile = tile_of(lax.axis_index("space"))
    for k, out in enumerate((times, part_a, part_b, part_c)):
        out[...] = weights[2 * k] * model[...] + weights[2 * k + 1] * beside[...]
    source = 2 * count * tile
    load_start(warm, source + count, got, start)
    sweeps(coefs, rhs, count, start, rest, lam, mine)
    near = (layers - 1) * (1 - tile)
    far = (layers - 1) * tile
    total = None
    for q in range(2 * count):
        slope = forward[source + q, near].astype(jnp.float32) - got[count * layers + q]
        if q < count:
            drop = own_first[q, near] - sent_first[layers * q + far]
        else:
            drop = lam[q - count, near] - lam[q - count, layers + far]
        total = slope * drop if total is None else total + slope * drop
    for q in range(count):
        own[q] = lam[q, :layers]
        sent[layers * q : layers * (q + 1)] = lam[q, layers:]
    sent[count * layers] = total


def data_sums(pairs, layers, along_x, along_y, along_z, mass):
    def add(ref, i, value, first):
        ref[i] = value if first else ref[i] + value

    for i in range(layers):
        totals = [None] * 4
        for forward, lam in pairs:
            here, other = forward(i), lam(i)
            terms = [None, face_prod(here, other, 0), face_prod(here, other, 1), here * other]
            if i + 1 < layers:
                terms[0] = (here - forward(i + 1)) * (other - lam(i + 1))
            totals = [t if a is None else (a if t is None else a + t) for a, t in zip(totals, terms)]
        if i + 1 < layers:
            along_x[i] = along_x[i] + totals[0]
        along_y[i] = along_y[i] + totals[1]
        along_z[i] = along_z[i] + totals[2]
        mass[i] = mass[i] + totals[3]


def gather_terms(forward, own_first, own_second, back, sums, adjoint, rounded, sems):
    count, layers = own_first.shape[:2]
    tile = tile_of(lax.axis_index("space"))
    mine, theirs = 2 * count * tile, 2 * count * (1 - tile)
    for q in range(count):
        rounded[q] = own_first[q].astype(jnp.bfloat16)
        rounded[count + q] = own_second[q].astype(jnp.bfloat16)
        rounded[2 * count + q] = back[layers * q : layers * (q + 1)].astype(jnp.bfloat16)
    copies = [
        pltpu.make_async_copy(rounded.at[: 2 * count], adjoint.at[pl.ds(mine, 2 * count)], sems.at[0]),
        pltpu.make_async_copy(rounded.at[2 * count :], adjoint.at[pl.ds(theirs, count)], sems.at[1]),
    ]
    for copy in copies:
        copy.start()
    sums[...] = jnp.zeros(sums.shape, jnp.float32)
    pairs = []
    for q in range(count):
        pairs.append((mine + q, lambda i, q=q: own_first[q, i]))
        pairs.append((mine + count + q, lambda i, q=q: own_second[q, i]))
        pairs.append((theirs + q, lambda i, q=q: back[layers * q + i]))
    pairs = [(lambda i, s=s: forward[s, i].astype(jnp.float32), lam) for s, lam in pairs]
    data_sums(pairs, layers, sums.at[0], sums.at[1], sums.at[2], sums.at[3])
    for copy in copies:
        copy.wait()


def finish(sums, back, sent, forward, model, other, times, near_a, near_b, near_c, kept, adjoint, gradient, rounded, result, sems):
    tile = tile_of(lax.axis_index("space"))
    count, layers = rounded.shape[:2]
    theirs = 2 * count * (1 - tile) + count
    for q in range(count):
        rounded[q] = back[layers * q : layers * (q + 1)].astype(jnp.bfloat16)
    copies = [pltpu.make_async_copy(rounded, adjoint.at[pl.ds(theirs, count)], sems.at[layers])]
    copies[0].start()
    shape = model.shape[1:]
    pairs = []
    for q in range(count):
        pairs.append((
            lambda i, q=q: forward[theirs + q, i].astype(jnp.float32),
            lambda i, q=q: back[layers * q + i],
        ))
    in_y, in_z = inner(shape, 0), inner(shape, 1)
    low = jnp.where(tile == 0, 0.0, 1.0)
    high = 1.0 - low
    cross = back[count * layers] + sent[count * layers]
    bridge = other[(layers - 1) * tile]
    products, falls = [low * cross], [low * (bridge - model[0])]
    for i in range(layers):
        if i + 1 < layers:
            total = sums[0, i]
            for f, l in pairs:
                total = total + (f(i) - f(i + 1)) * (l(i) - l(i + 1))
            products.append(total)
            falls.append(model[i] - model[i + 1])
        else:
            products.append(high * cross)
            falls.append(high * (model[i] - bridge))
    for i in range(layers):
        total_y, total_z, mass = sums[1, i], sums[2, i], sums[3, i]
        for f, l in pairs:
            here, there = f(i), l(i)
            total_y = total_y + face_prod(here, there, 0)
            total_z = total_z + face_prod(here, there, 1)
            mass = mass + here * there
        total_y = jnp.where(in_y, total_y, 0.0)
        total_z = jnp.where(in_z, total_z, 0.0)
        terms = products[i] + products[i + 1]
        terms = terms + (total_y + before(total_y, 0)) + (total_z + before(total_z, 1))
        value = model[i]
        fall_y = jnp.where(in_y, value - after(value, 0), 0.0)
        fall_z = jnp.where(in_z, value - after(value, 1), 0.0)
        space = falls[i + 1] - falls[i] + (fall_y - before(fall_y, 0)) + (fall_z - before(fall_z, 1))
        time = (times[i] + near_a[i]) + (near_b[i] + near_c[i])
        result[i] = space + time - jnp.exp(value) * (0.5 * terms + GROUND * mass)
        copies.append(pltpu.make_async_copy(result.at[i], gradient.at[i], sems.at[i]))
        copies[-1].start()
    for copy in copies:
        copy.wait()


V, S, H = pltpu.VMEM, pltpu.SMEM, pltpu.HBM


def call(kernel, operands, spaces, out_shapes, out_spaces=None, scratch=(), aliases=None, micros=1, room=16):
    several = len(out_shapes) > 1
    specs = [pl.BlockSpec(memory_space=m) for m in spaces]
    out_specs = [pl.BlockSpec(memory_space=m) for m in out_spaces or [V] * len(out_shapes)]
    return pl.pallas_call(
        kernel,
        out_shape=out_shapes if several else out_shapes[0],
        in_specs=specs,
        out_specs=out_specs if several else out_specs[0],
        scratch_shapes=list(scratch),
        input_output_aliases=aliases or {},
        compiler_params=pltpu.CompilerParams(vmem_limit_bytes=room * 2**20),
        cost_estimate=pl.CostEstimate(
            flops=micros * 10**9, bytes_accessed=micros * 3 * 10**6, transcendentals=0
        ),
    )(*operands)


def f32(*shape):
    return jax.ShapeDtypeStruct(shape, jnp.float32)


def bf16(*shape):
    return jax.ShapeDtypeStruct(shape, jnp.bfloat16)


def paired(model, forward, warm_start, residual_data, electrodes, survey_order):
    sources, layers, ny, nz = forward.shape
    half, count = sources // 2, sources // 4
    full = 2 * layers
    devices = lax.axis_size("space")
    position = lax.axis_index("space")
    pairs = []
    for p in range(1, devices, 2):
        pairs += [(p, (p + 1) % devices), ((p + 1) % devices, p)]

    def swap(x, mask=None):
        links = pairs if mask is None else [(p, p ^ mask) for p in range(devices)]
        return lax.ppermute(x, "space", links)

    dma = pltpu.SemaphoreType.DMA
    slab = (layers, ny, nz)
    other = swap(model)
    first = lax.dynamic_slice_in_dim(warm_start, half * (1 - tile_of(position)), count, 0)
    got_first = swap(first.astype(jnp.float32))
    rhs, weights_time = call(
        inject,
        (survey_order, residual_data, electrodes.reshape(1, -1)),
        (S, V, V),
        [f32(half, full, ny, nz), f32(8)],
        [V, S],
    )
    coefs, second = call(
        prepare,
        (model, other, warm_start, forward),
        (V, V, V, V),
        [f32(7, full, ny, nz), f32(count * layers + half, ny, nz)],
        scratch=[V((full, ny, nz), jnp.float32)],
    )
    got_second = swap(second)
    field = V((count, full, ny, nz), jnp.float32)
    fields = [field, field, field, V((2, count, full, ny, nz), jnp.float32)]
    block = f32(count, *slab)
    own_first, sent_first, relay = call(
        solve_first,
        (coefs, got_first, warm_start, rhs, other),
        (V, V, V, V, V),
        [block, f32(count * layers, ny, nz), f32(*slab)],
        scratch=fields,
        micros=3,
    )
    back_first = swap(sent_first)
    beside = swap(relay, 1)
    own_second, sent_second, times, *parts = call(
        solve_second,
        (weights_time, model, beside, coefs, got_second, warm_start, rhs, forward, own_first, sent_first),
        (S, V, V, V, V, V, V, V, V, V),
        [block, f32(count * layers + 1, ny, nz)] + [f32(*slab)] * 4,
        scratch=fields,
        micros=3,
    )
    back_second = swap(sent_second)
    near = [swap(part, 4 * (k + 1)) for k, part in enumerate(parts)]
    sums, kept = call(
        gather_terms,
        (forward, own_first, own_second, back_first),
        (V, V, V, V),
        [f32(4, *slab), bf16(*forward.shape)],
        [V, H],
        scratch=[V((3 * count, *slab), jnp.bfloat16), dma((2,))],
        micros=2,
    )
    adjoint, gradient = call(
        finish,
        (sums, back_second, sent_second, forward, model, other, times, *near, kept),
        (V, V, V, V, V, V, V, V, V, V, H),
        [bf16(*forward.shape), f32(*slab)],
        [H, H],
        scratch=[V((count, *slab), jnp.bfloat16), V(slab, jnp.float32), dma((layers + 1,))],
        aliases={10: 0},
    )
    return adjoint, gradient


def solution(mesh):
    body = paired if mesh.shape["space"] == 2 * SURVEYS else layered
    in_specs = (
        P(("groups", "space"), None, None),
        P(None, ("groups", "space"), None, None),
        P(None, ("groups", "space"), None, None),
        P("groups", None, None),
        P("groups"),
        P("groups"),
    )
    out_specs = (P(None, ("groups", "space"), None, None), P(("groups", "space"), None, None))
    return jax.shard_map(body, mesh=mesh, in_specs=in_specs, out_specs=out_specs, check_vma=False)
```

```python
import jax
import jax.numpy as jnp
from jax import lax
from jax.experimental import pallas as pl
from jax.experimental.pallas import tpu as pltpu
from jax.sharding import PartitionSpec as P

SURVEYS = 8
ITERS = 4


GROUND = 0.5
CENTER = 1.0
HALF_WIDTH = 0.99


def padded(shard, sides, width):
    for axis, dim in sides:
        devices, length = (lax.axis_size(axis), shard.shape[dim])
        up = [(i, (i + 1) % devices) for i in range(devices)]
        down = [(j, i) for i, j in up]
        last = lax.slice_in_dim(shard, length - width, length, axis=dim)
        leading = lax.slice_in_dim(shard, 0, width, axis=dim)
        before = lax.ppermute(last, axis, up)
        after = lax.ppermute(leading, axis, down)
        shard = jnp.concatenate([before, shard, after], axis=dim)
    return shard


def swapped(value, axis, bit):
    mask = 2**bit
    pairs = [(source, source ^ mask) for source in range(lax.axis_size(axis))]
    return lax.ppermute(value, axis, pairs)


def face_diff(field, axis):
    count = field.shape[axis]
    return lax.slice_in_dim(field, 0, count - 1, axis=axis) - lax.slice_in_dim(
        field, 1, count, axis=axis
    )


def edge_zeros(field, axis):
    shape = list(field.shape)
    shape[axis] = 1
    return jnp.zeros(shape, jnp.float32)


def pad_diff(faces, axis):
    zeros = edge_zeros(faces, axis)
    return jnp.concatenate([faces, zeros], axis=axis) - jnp.concatenate([zeros, faces], axis=axis)


def pad_sum(faces, axis):
    zeros = edge_zeros(faces, axis)
    return jnp.concatenate([faces, zeros], axis=axis) + jnp.concatenate([zeros, faces], axis=axis)


def extend(field):
    return padded(field, (("space", 1),), 1)


def layered(model, forward, warm_start, residual_data, electrodes, survey_order):
    sources, layers, rows_y, rows_z = forward.shape
    position = lax.axis_index("space")
    devices = lax.axis_size("space")
    tiles = devices // SURVEYS
    half_tiles = tiles // 2
    shifted = position + half_tiles
    tile = shifted % tiles
    survey = shifted // tiles % SURVEYS
    block = position // tiles
    rotation = jnp.where(position % tiles >= half_tiles, 1, 0).astype(jnp.int32)
    valid = jnp.ones((layers + 1,), jnp.float32)
    valid = valid.at[0].set(jnp.where(tile == 0, 0.0, 1.0))
    valid = valid.at[layers].set(jnp.where(tile == tiles - 1, 0.0, 1.0))
    valid_faces = valid[:, None, None]
    model_pad = padded(model, (("space", 0),), 1)
    sigma_pad = jnp.exp(model_pad)
    sigma = sigma_pad[1:-1]
    conduct_x = 0.5 * (sigma_pad[:-1] + sigma_pad[1:]) * valid_faces
    conduct_y = 0.5 * (sigma[:, :-1] + sigma[:, 1:])
    conduct_z = 0.5 * (sigma[:, :, :-1] + sigma[:, :, 1:])
    diagonal = (
        conduct_x[1:]
        + conduct_x[:-1]
        + pad_sum(conduct_y, 1)
        + pad_sum(conduct_z, 2)
        + GROUND * sigma
    )
    inverse_diag = (1.0 / diagonal)[None]

    def operate(field_pad):
        field = field_pad[:, 1:-1]
        flux_x = conduct_x[None] * (field_pad[:, :-1] - field_pad[:, 1:])
        total = flux_x[:, 1:] - flux_x[:, :-1]
        total = total + pad_diff(conduct_y[None] * face_diff(field, 2), 2)
        total = total + pad_diff(conduct_z[None] * face_diff(field, 3), 3)
        return total + GROUND * sigma[None] * field

    cells = layers * rows_y * rows_z
    residual = lax.dynamic_index_in_dim(residual_data, survey, 0, keepdims=False)
    local_index = electrodes - tile * cells
    inside = (local_index >= 0) & (local_index < cells)
    target = jnp.where(inside, local_index, 0)
    amount = jnp.where(inside[None, :], residual, 0.0)
    rhs = jnp.zeros((sources, cells), jnp.float32).at[:, target].add(amount)
    rhs = rhs.reshape(sources, layers, rows_y, rows_z)
    iterate = warm_start.astype(jnp.float32)
    remain = rhs - operate(extend(iterate))
    direction = remain * inverse_diag / CENTER
    weight_now = HALF_WIDTH / CENTER
    for sweep_index in range(ITERS):
        iterate = iterate + direction
        if sweep_index + 1 < ITERS:
            remain = remain - operate(extend(direction))
            weight_new = 1.0 / (2.0 * CENTER / HALF_WIDTH - weight_now)
            direction = weight_new * weight_now * direction + 2.0 * weight_new / HALF_WIDTH * (
                remain * inverse_diag
            )
            weight_now = weight_new
    both = padded(
        jnp.concatenate([forward.astype(jnp.float32), iterate], axis=0), (("space", 1),), 1
    )
    forward_pad = both[:sources]
    adjoint_pad = both[sources:]
    potential = forward_pad[:, 1:-1]
    product_x = (
        jnp.sum(
            (forward_pad[:, :-1] - forward_pad[:, 1:]) * (adjoint_pad[:, :-1] - adjoint_pad[:, 1:]),
            axis=0,
        )
        * valid_faces
    )
    terms = product_x[1:] + product_x[:-1]
    terms = terms + pad_sum(jnp.sum(face_diff(potential, 2) * face_diff(iterate, 2), axis=0), 1)
    terms = terms + pad_sum(jnp.sum(face_diff(potential, 3) * face_diff(iterate, 3), axis=0), 2)
    data_term = -sigma * (0.5 * terms + GROUND * jnp.sum(potential * iterate, axis=0))
    model_x = (model_pad[:-1] - model_pad[1:]) * valid_faces
    space_term = (
        model_x[1:]
        - model_x[:-1]
        + pad_diff(face_diff(model, 1), 1)
        + pad_diff(face_diff(model, 2), 2)
    )
    base_bit = tiles.bit_length() - 1
    collected = model
    for level in range(SURVEYS.bit_length() - 1):
        partner = swapped(collected, "space", base_bit + level)
        upper = block >> level & 1 == 1
        lower_half = jnp.where(upper, partner, collected)
        upper_half = jnp.where(upper, collected, partner)
        collected = jnp.concatenate([lower_half, upper_half], axis=0)
    all_blocks = collected.reshape(SURVEYS, layers, rows_y, rows_z)
    ranks = jnp.arange(SURVEYS, dtype=jnp.int32)
    placed = (survey_order[:, None] == ranks[None, :]).astype(jnp.float32)
    apart = jnp.abs(ranks[:, None] - ranks[None, :])
    degree = jnp.where((ranks == 0) | (ranks == SURVEYS - 1), 1.0, 2.0)
    path = jnp.where(apart == 0, degree[:, None], 0.0) - jnp.where(apart == 1, 1.0, 0.0)
    coupling = jnp.dot(
        placed.T,
        jnp.dot(path, placed, precision=lax.Precision.HIGHEST),
        precision=lax.Precision.HIGHEST,
    )
    row_weights = lax.dynamic_index_in_dim(coupling, survey, 0, keepdims=False)
    block_survey = (ranks + rotation) % SURVEYS
    picker = (block_survey[:, None] == ranks[None, :]).astype(jnp.float32)
    block_weights = jnp.dot(picker, row_weights, precision=lax.Precision.HIGHEST)
    time_term = jnp.sum(block_weights[:, None, None, None] * all_blocks, axis=0)
    return (iterate.astype(jnp.bfloat16), data_term + space_term + time_term)


def weights():
    now = HALF_WIDTH / CENTER
    steps = []
    for _ in range(ITERS - 1):
        new = 1.0 / (2.0 * CENTER / HALF_WIDTH - now)
        steps.append((new * now, 2.0 * new / HALF_WIDTH))
        now = new
    return steps


def after(x, axis):
    return pltpu.roll(x, x.shape[axis] - 1, axis)


def before(x, axis):
    return pltpu.roll(x, 1, axis)


def inner(shape, axis):
    return lax.broadcasted_iota(jnp.int32, shape, axis) < shape[axis] - 1


def face_prod(field, other, axis):
    return (field - after(field, axis)) * (other - after(other, axis))


def tile_of(position):
    return (position + 1) & 1


def survey_of(position):
    return ((position + 1) >> 1) & (SURVEYS - 1)


def pack(warm, first):
    tile = tile_of(lax.axis_index("space"))
    count = first.shape[0]
    for q in range(count):
        first[q] = warm[2 * count * (1 - tile) + q].astype(jnp.float32)


def inject(order, residual, electrodes, out, weights):
    position = lax.axis_index("space")
    tile = tile_of(position)
    surveys = order.shape[0]
    ranks = []
    for place in [position, position ^ 1] + [position ^ (4 * k) for k in range(4)]:
        found = 0
        for i in range(surveys):
            found = found + jnp.where(order[i] == survey_of(place), i, 0)
        ranks.append(found)
    for k in range(4):
        a = ranks[2 + k]
        ends = jnp.where(a == 0, 1, 0) + jnp.where(a == surveys - 1, 1, 0)
        for m in range(2):
            b = ranks[m]
            value = jnp.where(a == b, 2 - ends, jnp.where(jnp.abs(a - b) == 1, -1, 0))
            weights[2 * k + m] = value.astype(jnp.float32)
    sources, _, rows_y, rows_z = out.shape
    half = residual.shape[1] // 2
    cells = out.shape[1] * rows_y * rows_z
    where_cell = lax.rem(electrodes[...] + tile * (cells // 2), cells)
    row = where_cell // rows_z
    lane = lax.rem(where_cell, rows_z)
    count = row.shape[1]
    rows = cells // rows_z
    at_row = lax.broadcasted_iota(jnp.int32, (rows, count), 0) == row
    at_row = jnp.where(at_row, 1.0, 0.0).astype(jnp.bfloat16)
    at_lane = lax.broadcasted_iota(jnp.int32, (rows_z, count), 0) == lane
    mine = residual[survey_of(position)]
    mine = jnp.where(tile == 0, mine[:half], mine[half:])
    total = None
    for _ in range(3):
        part = mine.astype(jnp.bfloat16).astype(jnp.float32)
        mine = mine - part
        right = jnp.concatenate(
            [jnp.where(at_lane, part[q : q + 1], 0.0) for q in range(sources)], axis=0
        ).astype(jnp.bfloat16)
        term = lax.dot_general(
            at_row, right, (((1,), (1,)), ((), ())), preferred_element_type=jnp.float32
        )
        total = term if total is None else total + term
    for q in range(sources):
        out[q] = total[:, q * rows_z : (q + 1) * rows_z].reshape(out.shape[1:])


def prepare(model, other, warm, forward, coefs, second, sigma):
    tile = tile_of(lax.axis_index("space"))
    half = warm.shape[0] // 2
    count, layers = half // 2, model.shape[0]
    theirs = half * (1 - tile)
    face = (layers - 1) * (1 - tile)
    for q in range(count):
        second[layers * q : layers * (q + 1)] = warm[theirs + count + q].astype(jnp.float32)
    for q in range(half):
        second[count * layers + q] = forward[theirs + q, face].astype(jnp.float32)
    full = 2 * layers
    shape = model.shape[1:]
    for i in range(layers):
        sigma[i] = jnp.exp(model[i])
        sigma[layers + i] = jnp.exp(other[i])
    in_y, in_z = inner(shape, 0), inner(shape, 1)
    middle = jnp.where(tile == 0, 1.0, 0.0)
    for i in range(full):
        mine = sigma[i]
        up = 0.5 * (mine + sigma[(i + 1) % full])
        down = 0.5 * (mine + sigma[(i - 1) % full])
        if i == layers - 1:
            up = up * middle
        if i == full - 1:
            up = up * (1.0 - middle)
        if i == layers:
            down = down * middle
        if i == 0:
            down = down * (1.0 - middle)
        right_y = jnp.where(in_y, 0.5 * (mine + after(mine, 0)), 0.0)
        right_z = jnp.where(in_z, 0.5 * (mine + after(mine, 1)), 0.0)
        left_y = before(right_y, 0)
        left_z = before(right_z, 1)
        scale = 1.0 / (up + down + right_y + left_y + right_z + left_z + GROUND * mine)
        for k, face in enumerate((up, down, right_y, left_y, right_z, left_z)):
            coefs[k, i] = face * scale
        coefs[6, i] = scale


def sweeps(coefs, rhs, base, start, rest, lam, mine):
    count, full = start.shape[:2]

    def around(field, q, i, weight):
        here = field[q, i]
        total = weight[0] * field[q, (i + 1) % full] + weight[1] * field[q, (i + full - 1) % full]
        total = total + (weight[2] * after(here, 0) + weight[3] * before(here, 0))
        total = total + (weight[4] * after(here, 1) + weight[5] * before(here, 1))
        return here, total

    def first(i, carry):
        weight = [coefs[k, i] for k in range(7)]
        for q in range(count):
            here, total = around(start, q, i, weight)
            step = rhs[base + q, i] * weight[6] - here + total
            mine[0, q, i] = step
            lam[q, i] = here + step
        return carry

    lax.fori_loop(0, full, first, 0, unroll=full)
    for index, (keep, gain) in enumerate(weights()):
        source, target = mine.at[index % 2], mine.at[1 - index % 2]
        last = index == ITERS - 2

        def later(i, carry):
            weight = [coefs[k, i] for k in range(6)]
            for q in range(count):
                here, total = around(source, q, i, weight)
                if index > 0:
                    total = rest[q, i] - here + total
                step = keep * here + gain * total
                if not last:
                    rest[q, i] = total
                    target[q, i] = step
                lam[q, i] = lam[q, i] + step
            return carry

        lax.fori_loop(0, full, later, 0, unroll=full)


def load_start(warm, source, got, start):
    count, full = start.shape[:2]
    layers = full // 2
    for q in range(count):
        start[q, :layers] = warm[source + q].astype(jnp.float32)
        start[q, layers:] = got[q] if len(got.shape) == 4 else got[layers * q : layers * (q + 1)]


def solve_first(weights, model, beside, coefs, got, warm, rhs, own, sent, time, opposite, parts, start, rest, lam, mine):
    count, layers = own.shape[:2]
    here, there = model[...], beside[...]
    time[...] = weights[0] * here + weights[1] * there
    parts[:layers] = weights[2] * here + weights[3] * there
    opposite[...] = weights[4] * here + weights[5] * there
    parts[layers:] = weights[6] * here + weights[7] * there
    load_start(warm, 2 * count * tile_of(lax.axis_index("space")), got, start)
    sweeps(coefs, rhs, 0, start, rest, lam, mine)
    for q in range(count):
        own[q] = lam[q, :layers]
        sent[layers * q : layers * (q + 1)] = lam[q, layers:]


def solve_second(time, opposite, near, coefs, got, warm, rhs, forward, own_first, sent_first, own, sent, times, joined, start, rest, lam, mine):
    count, layers = own.shape[:2]
    tile = tile_of(lax.axis_index("space"))
    times[...] = time[...] + near[:layers]
    joined[...] = opposite[...] + near[layers:]
    source = 2 * count * tile
    load_start(warm, source + count, got, start)
    sweeps(coefs, rhs, count, start, rest, lam, mine)
    near = (layers - 1) * (1 - tile)
    far = (layers - 1) * tile
    total = None
    for q in range(2 * count):
        slope = forward[source + q, near].astype(jnp.float32) - got[count * layers + q]
        if q < count:
            drop = own_first[q, near] - sent_first[layers * q + far]
        else:
            drop = lam[q - count, near] - lam[q - count, layers + far]
        total = slope * drop if total is None else total + slope * drop
    for q in range(count):
        own[q] = lam[q, :layers]
        sent[layers * q : layers * (q + 1)] = lam[q, layers:]
    sent[count * layers] = total


def data_sums(pairs, layers, along_x, along_y, along_z, mass):
    def add(ref, i, value, first):
        ref[i] = value if first else ref[i] + value

    for i in range(layers):
        totals = [None] * 4
        for forward, lam in pairs:
            here, other = forward(i), lam(i)
            terms = [None, face_prod(here, other, 0), face_prod(here, other, 1), here * other]
            if i + 1 < layers:
                terms[0] = (here - forward(i + 1)) * (other - lam(i + 1))
            totals = [t if a is None else (a if t is None else a + t) for a, t in zip(totals, terms)]
        if i + 1 < layers:
            along_x[i] = along_x[i] + totals[0]
        along_y[i] = along_y[i] + totals[1]
        along_z[i] = along_z[i] + totals[2]
        mass[i] = mass[i] + totals[3]


def gather_terms(forward, own_first, own_second, back, sums, adjoint, rounded, sems):
    count, layers = own_first.shape[:2]
    tile = tile_of(lax.axis_index("space"))
    mine, theirs = 2 * count * tile, 2 * count * (1 - tile)
    for q in range(count):
        rounded[q] = own_first[q].astype(jnp.bfloat16)
        rounded[count + q] = own_second[q].astype(jnp.bfloat16)
        rounded[2 * count + q] = back[layers * q : layers * (q + 1)].astype(jnp.bfloat16)
    copies = [
        pltpu.make_async_copy(rounded.at[: 2 * count], adjoint.at[pl.ds(mine, 2 * count)], sems.at[0]),
        pltpu.make_async_copy(rounded.at[2 * count :], adjoint.at[pl.ds(theirs, count)], sems.at[1]),
    ]
    for copy in copies:
        copy.start()
    sums[...] = jnp.zeros(sums.shape, jnp.float32)
    pairs = []
    for q in range(count):
        pairs.append((mine + q, lambda i, q=q: own_first[q, i]))
        pairs.append((mine + count + q, lambda i, q=q: own_second[q, i]))
        pairs.append((theirs + q, lambda i, q=q: back[layers * q + i]))
    pairs = [(lambda i, s=s: forward[s, i].astype(jnp.float32), lam) for s, lam in pairs]
    data_sums(pairs, layers, sums.at[0], sums.at[1], sums.at[2], sums.at[3])
    for copy in copies:
        copy.wait()


def finish(sums, back, sent, forward, model, other, times, far, kept, adjoint, gradient, rounded, result, sems):
    tile = tile_of(lax.axis_index("space"))
    count, layers = rounded.shape[:2]
    theirs = 2 * count * (1 - tile) + count
    for q in range(count):
        rounded[q] = back[layers * q : layers * (q + 1)].astype(jnp.bfloat16)
    copies = [pltpu.make_async_copy(rounded, adjoint.at[pl.ds(theirs, count)], sems.at[layers])]
    copies[0].start()
    shape = model.shape[1:]
    pairs = []
    for q in range(count):
        pairs.append((
            lambda i, q=q: forward[theirs + q, i].astype(jnp.float32),
            lambda i, q=q: back[layers * q + i],
        ))
    in_y, in_z = inner(shape, 0), inner(shape, 1)
    low = jnp.where(tile == 0, 0.0, 1.0)
    high = 1.0 - low
    cross = back[count * layers] + sent[count * layers]
    bridge = other[(layers - 1) * tile]
    products, falls = [low * cross], [low * (bridge - model[0])]
    for i in range(layers):
        if i + 1 < layers:
            total = sums[0, i]
            for f, l in pairs:
                total = total + (f(i) - f(i + 1)) * (l(i) - l(i + 1))
            products.append(total)
            falls.append(model[i] - model[i + 1])
        else:
            products.append(high * cross)
            falls.append(high * (model[i] - bridge))
    for i in range(layers):
        total_y, total_z, mass = sums[1, i], sums[2, i], sums[3, i]
        for f, l in pairs:
            here, there = f(i), l(i)
            total_y = total_y + face_prod(here, there, 0)
            total_z = total_z + face_prod(here, there, 1)
            mass = mass + here * there
        total_y = jnp.where(in_y, total_y, 0.0)
        total_z = jnp.where(in_z, total_z, 0.0)
        terms = products[i] + products[i + 1]
        terms = terms + (total_y + before(total_y, 0)) + (total_z + before(total_z, 1))
        value = model[i]
        fall_y = jnp.where(in_y, value - after(value, 0), 0.0)
        fall_z = jnp.where(in_z, value - after(value, 1), 0.0)
        space = falls[i + 1] - falls[i] + (fall_y - before(fall_y, 0)) + (fall_z - before(fall_z, 1))
        result[i] = space + (times[i] + far[i]) - jnp.exp(value) * (0.5 * terms + GROUND * mass)
        copies.append(pltpu.make_async_copy(result.at[i], gradient.at[i], sems.at[i]))
        copies[-1].start()
    for copy in copies:
        copy.wait()


V, S, H = pltpu.VMEM, pltpu.SMEM, pltpu.HBM


def call(kernel, operands, spaces, out_shapes, out_spaces=None, scratch=(), aliases=None, micros=1, room=16):
    several = len(out_shapes) > 1
    specs = [pl.BlockSpec(memory_space=m) for m in spaces]
    out_specs = [pl.BlockSpec(memory_space=m) for m in out_spaces or [V] * len(out_shapes)]
    return pl.pallas_call(
        kernel,
        out_shape=out_shapes if several else out_shapes[0],
        in_specs=specs,
        out_specs=out_specs if several else out_specs[0],
        scratch_shapes=list(scratch),
        input_output_aliases=aliases or {},
        compiler_params=pltpu.CompilerParams(vmem_limit_bytes=room * 2**20),
        cost_estimate=pl.CostEstimate(
            flops=micros * 10**9, bytes_accessed=micros * 3 * 10**6, transcendentals=0
        ),
    )(*operands)


def f32(*shape):
    return jax.ShapeDtypeStruct(shape, jnp.float32)


def bf16(*shape):
    return jax.ShapeDtypeStruct(shape, jnp.bfloat16)


def paired(model, forward, warm_start, residual_data, electrodes, survey_order):
    sources, layers, ny, nz = forward.shape
    half, count = sources // 2, sources // 4
    full = 2 * layers
    devices = lax.axis_size("space")
    pairs = []
    for p in range(1, devices, 2):
        pairs += [(p, (p + 1) % devices), ((p + 1) % devices, p)]

    def swap(x, mask=None):
        links = pairs if mask is None else [(p, p ^ mask) for p in range(devices)]
        return lax.ppermute(x, "space", links)

    dma = pltpu.SemaphoreType.DMA
    slab = (layers, ny, nz)
    other = swap(model)
    first = call(pack, (warm_start,), (V,), [f32(count, *slab)], micros=2)
    got_first = swap(first)
    beside = swap(other, 1)
    rhs, weights_time = call(
        inject,
        (survey_order, residual_data, electrodes.reshape(1, -1)),
        (S, V, V),
        [f32(half, full, ny, nz), f32(8)],
        [V, S],
    )
    coefs, second = call(
        prepare,
        (model, other, warm_start, forward),
        (V, V, V, V),
        [f32(7, full, ny, nz), f32(count * layers + half, ny, nz)],
        scratch=[V((full, ny, nz), jnp.float32)],
    )
    got_second = swap(second)
    field = V((count, full, ny, nz), jnp.float32)
    fields = [field, field, field, V((2, count, full, ny, nz), jnp.float32)]
    block = f32(count, *slab)
    own_first, sent_first, time, opposite, parts = call(
        solve_first,
        (weights_time, model, beside, coefs, got_first, warm_start, rhs),
        (S, V, V, V, V, V, V),
        [block, f32(count * layers, ny, nz), f32(*slab), f32(*slab), f32(2 * layers, ny, nz)],
        scratch=fields,
        micros=3,
    )
    back_first = swap(sent_first)
    near = swap(parts, 4)
    own_second, sent_second, times, joined = call(
        solve_second,
        (time, opposite, near, coefs, got_second, warm_start, rhs, forward, own_first, sent_first),
        (V, V, V, V, V, V, V, V, V, V),
        [block, f32(count * layers + 1, ny, nz), f32(*slab), f32(*slab)],
        scratch=fields,
        micros=3,
    )
    back_second = swap(sent_second)
    far = swap(joined, 8)
    sums, kept = call(
        gather_terms,
        (forward, own_first, own_second, back_first),
        (V, V, V, V),
        [f32(4, *slab), bf16(*forward.shape)],
        [V, H],
        scratch=[V((3 * count, *slab), jnp.bfloat16), dma((2,))],
        micros=2,
    )
    adjoint, gradient = call(
        finish,
        (sums, back_second, sent_second, forward, model, other, times, far, kept),
        (V, V, V, V, V, V, V, V, H),
        [bf16(*forward.shape), f32(*slab)],
        [H, H],
        scratch=[V((count, *slab), jnp.bfloat16), V(slab, jnp.float32), dma((layers + 1,))],
        aliases={8: 0},
    )
    return adjoint, gradient


def solution(mesh):
    body = paired if mesh.shape["space"] == 2 * SURVEYS else layered
    in_specs = (
        P(("groups", "space"), None, None),
        P(None, ("groups", "space"), None, None),
        P(None, ("groups", "space"), None, None),
        P("groups", None, None),
        P("groups"),
        P("groups"),
    )
    out_specs = (P(None, ("groups", "space"), None, None), P(("groups", "space"), None, None))
    return jax.shard_map(body, mesh=mesh, in_specs=in_specs, out_specs=out_specs, check_vma=False)
```

```python
import jax
import jax.numpy as jnp
from jax import lax
from jax.experimental import pallas as pl
from jax.experimental.pallas import tpu as pltpu
from jax.sharding import PartitionSpec as P

SURVEYS = 8
ITERS = 4


GROUND = 0.5
CENTER = 1.0
HALF_WIDTH = 0.99


def padded(shard, sides, width):
    for axis, dim in sides:
        devices, length = (lax.axis_size(axis), shard.shape[dim])
        up = [(i, (i + 1) % devices) for i in range(devices)]
        down = [(j, i) for i, j in up]
        last = lax.slice_in_dim(shard, length - width, length, axis=dim)
        leading = lax.slice_in_dim(shard, 0, width, axis=dim)
        before = lax.ppermute(last, axis, up)
        after = lax.ppermute(leading, axis, down)
        shard = jnp.concatenate([before, shard, after], axis=dim)
    return shard


def swapped(value, axis, bit):
    mask = 2**bit
    pairs = [(source, source ^ mask) for source in range(lax.axis_size(axis))]
    return lax.ppermute(value, axis, pairs)


def face_diff(field, axis):
    count = field.shape[axis]
    return lax.slice_in_dim(field, 0, count - 1, axis=axis) - lax.slice_in_dim(
        field, 1, count, axis=axis
    )


def edge_zeros(field, axis):
    shape = list(field.shape)
    shape[axis] = 1
    return jnp.zeros(shape, jnp.float32)


def pad_diff(faces, axis):
    zeros = edge_zeros(faces, axis)
    return jnp.concatenate([faces, zeros], axis=axis) - jnp.concatenate([zeros, faces], axis=axis)


def pad_sum(faces, axis):
    zeros = edge_zeros(faces, axis)
    return jnp.concatenate([faces, zeros], axis=axis) + jnp.concatenate([zeros, faces], axis=axis)


def extend(field):
    return padded(field, (("space", 1),), 1)


def layered(model, forward, warm_start, residual_data, electrodes, survey_order):
    sources, layers, rows_y, rows_z = forward.shape
    position = lax.axis_index("space")
    devices = lax.axis_size("space")
    tiles = devices // SURVEYS
    half_tiles = tiles // 2
    shifted = position + half_tiles
    tile = shifted % tiles
    survey = shifted // tiles % SURVEYS
    block = position // tiles
    rotation = jnp.where(position % tiles >= half_tiles, 1, 0).astype(jnp.int32)
    valid = jnp.ones((layers + 1,), jnp.float32)
    valid = valid.at[0].set(jnp.where(tile == 0, 0.0, 1.0))
    valid = valid.at[layers].set(jnp.where(tile == tiles - 1, 0.0, 1.0))
    valid_faces = valid[:, None, None]
    model_pad = padded(model, (("space", 0),), 1)
    sigma_pad = jnp.exp(model_pad)
    sigma = sigma_pad[1:-1]
    conduct_x = 0.5 * (sigma_pad[:-1] + sigma_pad[1:]) * valid_faces
    conduct_y = 0.5 * (sigma[:, :-1] + sigma[:, 1:])
    conduct_z = 0.5 * (sigma[:, :, :-1] + sigma[:, :, 1:])
    diagonal = (
        conduct_x[1:]
        + conduct_x[:-1]
        + pad_sum(conduct_y, 1)
        + pad_sum(conduct_z, 2)
        + GROUND * sigma
    )
    inverse_diag = (1.0 / diagonal)[None]

    def operate(field_pad):
        field = field_pad[:, 1:-1]
        flux_x = conduct_x[None] * (field_pad[:, :-1] - field_pad[:, 1:])
        total = flux_x[:, 1:] - flux_x[:, :-1]
        total = total + pad_diff(conduct_y[None] * face_diff(field, 2), 2)
        total = total + pad_diff(conduct_z[None] * face_diff(field, 3), 3)
        return total + GROUND * sigma[None] * field

    cells = layers * rows_y * rows_z
    residual = lax.dynamic_index_in_dim(residual_data, survey, 0, keepdims=False)
    local_index = electrodes - tile * cells
    inside = (local_index >= 0) & (local_index < cells)
    target = jnp.where(inside, local_index, 0)
    amount = jnp.where(inside[None, :], residual, 0.0)
    rhs = jnp.zeros((sources, cells), jnp.float32).at[:, target].add(amount)
    rhs = rhs.reshape(sources, layers, rows_y, rows_z)
    iterate = warm_start.astype(jnp.float32)
    remain = rhs - operate(extend(iterate))
    direction = remain * inverse_diag / CENTER
    weight_now = HALF_WIDTH / CENTER
    for sweep_index in range(ITERS):
        iterate = iterate + direction
        if sweep_index + 1 < ITERS:
            remain = remain - operate(extend(direction))
            weight_new = 1.0 / (2.0 * CENTER / HALF_WIDTH - weight_now)
            direction = weight_new * weight_now * direction + 2.0 * weight_new / HALF_WIDTH * (
                remain * inverse_diag
            )
            weight_now = weight_new
    both = padded(
        jnp.concatenate([forward.astype(jnp.float32), iterate], axis=0), (("space", 1),), 1
    )
    forward_pad = both[:sources]
    adjoint_pad = both[sources:]
    potential = forward_pad[:, 1:-1]
    product_x = (
        jnp.sum(
            (forward_pad[:, :-1] - forward_pad[:, 1:]) * (adjoint_pad[:, :-1] - adjoint_pad[:, 1:]),
            axis=0,
        )
        * valid_faces
    )
    terms = product_x[1:] + product_x[:-1]
    terms = terms + pad_sum(jnp.sum(face_diff(potential, 2) * face_diff(iterate, 2), axis=0), 1)
    terms = terms + pad_sum(jnp.sum(face_diff(potential, 3) * face_diff(iterate, 3), axis=0), 2)
    data_term = -sigma * (0.5 * terms + GROUND * jnp.sum(potential * iterate, axis=0))
    model_x = (model_pad[:-1] - model_pad[1:]) * valid_faces
    space_term = (
        model_x[1:]
        - model_x[:-1]
        + pad_diff(face_diff(model, 1), 1)
        + pad_diff(face_diff(model, 2), 2)
    )
    base_bit = tiles.bit_length() - 1
    collected = model
    for level in range(SURVEYS.bit_length() - 1):
        partner = swapped(collected, "space", base_bit + level)
        upper = block >> level & 1 == 1
        lower_half = jnp.where(upper, partner, collected)
        upper_half = jnp.where(upper, collected, partner)
        collected = jnp.concatenate([lower_half, upper_half], axis=0)
    all_blocks = collected.reshape(SURVEYS, layers, rows_y, rows_z)
    ranks = jnp.arange(SURVEYS, dtype=jnp.int32)
    placed = (survey_order[:, None] == ranks[None, :]).astype(jnp.float32)
    apart = jnp.abs(ranks[:, None] - ranks[None, :])
    degree = jnp.where((ranks == 0) | (ranks == SURVEYS - 1), 1.0, 2.0)
    path = jnp.where(apart == 0, degree[:, None], 0.0) - jnp.where(apart == 1, 1.0, 0.0)
    coupling = jnp.dot(
        placed.T,
        jnp.dot(path, placed, precision=lax.Precision.HIGHEST),
        precision=lax.Precision.HIGHEST,
    )
    row_weights = lax.dynamic_index_in_dim(coupling, survey, 0, keepdims=False)
    block_survey = (ranks + rotation) % SURVEYS
    picker = (block_survey[:, None] == ranks[None, :]).astype(jnp.float32)
    block_weights = jnp.dot(picker, row_weights, precision=lax.Precision.HIGHEST)
    time_term = jnp.sum(block_weights[:, None, None, None] * all_blocks, axis=0)
    return (iterate.astype(jnp.bfloat16), data_term + space_term + time_term)


def weights():
    now = HALF_WIDTH / CENTER
    steps = []
    for _ in range(ITERS - 1):
        new = 1.0 / (2.0 * CENTER / HALF_WIDTH - now)
        steps.append((new * now, 2.0 * new / HALF_WIDTH))
        now = new
    return steps


def after(x, axis):
    return pltpu.roll(x, x.shape[axis] - 1, axis)


def before(x, axis):
    return pltpu.roll(x, 1, axis)


def inner(shape, axis):
    return lax.broadcasted_iota(jnp.int32, shape, axis) < shape[axis] - 1


def face_prod(field, other, axis):
    return (field - after(field, axis)) * (other - after(other, axis))


def tile_of(position):
    return (position + 1) & 1


def survey_of(position):
    return ((position + 1) >> 1) & (SURVEYS - 1)


def pack(warm, first):
    tile = tile_of(lax.axis_index("space"))
    count = first.shape[0]
    for q in range(count):
        first[q] = warm[2 * count * (1 - tile) + q].astype(jnp.float32)


def inject(order, residual, electrodes, out, weights):
    position = lax.axis_index("space")
    tile = tile_of(position)
    surveys = order.shape[0]
    ranks = []
    for place in [position, position ^ 1] + [position ^ (4 * k) for k in range(4)]:
        found = 0
        for i in range(surveys):
            found = found + jnp.where(order[i] == survey_of(place), i, 0)
        ranks.append(found)
    for k in range(4):
        a = ranks[2 + k]
        ends = jnp.where(a == 0, 1, 0) + jnp.where(a == surveys - 1, 1, 0)
        for m in range(2):
            b = ranks[m]
            value = jnp.where(a == b, 2 - ends, jnp.where(jnp.abs(a - b) == 1, -1, 0))
            weights[2 * k + m] = value.astype(jnp.float32)
    sources, _, rows_y, rows_z = out.shape
    half = residual.shape[1] // 2
    cells = out.shape[1] * rows_y * rows_z
    where_cell = lax.rem(electrodes[...] + tile * (cells // 2), cells)
    row = where_cell // rows_z
    lane = lax.rem(where_cell, rows_z)
    count = row.shape[1]
    rows = cells // rows_z
    at_row = lax.broadcasted_iota(jnp.int32, (rows, count), 0) == row
    at_row = jnp.where(at_row, 1.0, 0.0).astype(jnp.bfloat16)
    at_lane = lax.broadcasted_iota(jnp.int32, (rows_z, count), 0) == lane
    mine = residual[survey_of(position)]
    mine = jnp.where(tile == 0, mine[:half], mine[half:])
    total = None
    for _ in range(3):
        part = mine.astype(jnp.bfloat16).astype(jnp.float32)
        mine = mine - part
        right = jnp.concatenate(
            [jnp.where(at_lane, part[q : q + 1], 0.0) for q in range(sources)], axis=0
        ).astype(jnp.bfloat16)
        term = lax.dot_general(
            at_row, right, (((1,), (1,)), ((), ())), preferred_element_type=jnp.float32
        )
        total = term if total is None else total + term
    for q in range(sources):
        out[q] = total[:, q * rows_z : (q + 1) * rows_z].reshape(out.shape[1:])


def prepare(model, other, warm, forward, coefs, second, sigma):
    tile = tile_of(lax.axis_index("space"))
    half = warm.shape[0] // 2
    count, layers = half // 2, model.shape[0]
    theirs = half * (1 - tile)
    face = (layers - 1) * (1 - tile)
    for q in range(count):
        second[layers * q : layers * (q + 1)] = warm[theirs + count + q].astype(jnp.float32)
    for q in range(half):
        second[count * layers + q] = forward[theirs + q, face].astype(jnp.float32)
    full = 2 * layers
    shape = model.shape[1:]
    for i in range(layers):
        sigma[i] = jnp.exp(model[i])
        sigma[layers + i] = jnp.exp(other[i])
    in_y, in_z = inner(shape, 0), inner(shape, 1)
    middle = jnp.where(tile == 0, 1.0, 0.0)
    for i in range(full):
        mine = sigma[i]
        up = 0.5 * (mine + sigma[(i + 1) % full])
        down = 0.5 * (mine + sigma[(i - 1) % full])
        if i == layers - 1:
            up = up * middle
        if i == full - 1:
            up = up * (1.0 - middle)
        if i == layers:
            down = down * middle
        if i == 0:
            down = down * (1.0 - middle)
        right_y = jnp.where(in_y, 0.5 * (mine + after(mine, 0)), 0.0)
        right_z = jnp.where(in_z, 0.5 * (mine + after(mine, 1)), 0.0)
        left_y = before(right_y, 0)
        left_z = before(right_z, 1)
        scale = 1.0 / (up + down + right_y + left_y + right_z + left_z + GROUND * mine)
        for k, face in enumerate((up, down, right_y, left_y, right_z, left_z)):
            coefs[k, i] = face * scale
        coefs[6, i] = scale


def sweeps(coefs, rhs, base, start, rest, lam, mine):
    count, full = start.shape[:2]

    def around(field, q, i, weight):
        here = field[q, i]
        total = weight[0] * field[q, (i + 1) % full] + weight[1] * field[q, (i + full - 1) % full]
        total = total + (weight[2] * after(here, 0) + weight[3] * before(here, 0))
        total = total + (weight[4] * after(here, 1) + weight[5] * before(here, 1))
        return here, total

    def first(i, carry):
        weight = [coefs[k, i] for k in range(7)]
        for q in range(count):
            here, total = around(start, q, i, weight)
            step = rhs[base + q, i] * weight[6] - here + total
            mine[0, q, i] = step
            lam[q, i] = here + step
        return carry

    lax.fori_loop(0, full, first, 0, unroll=full)
    for index, (keep, gain) in enumerate(weights()):
        source, target = mine.at[index % 2], mine.at[1 - index % 2]
        last = index == ITERS - 2

        def later(i, carry):
            weight = [coefs[k, i] for k in range(6)]
            for q in range(count):
                here, total = around(source, q, i, weight)
                if index > 0:
                    total = rest[q, i] - here + total
                step = keep * here + gain * total
                if not last:
                    rest[q, i] = total
                    target[q, i] = step
                lam[q, i] = lam[q, i] + step
            return carry

        lax.fori_loop(0, full, later, 0, unroll=full)


def load_start(warm, source, got, start):
    count, full = start.shape[:2]
    layers = full // 2
    for q in range(count):
        start[q, :layers] = warm[source + q].astype(jnp.float32)
        start[q, layers:] = got[q] if len(got.shape) == 4 else got[layers * q : layers * (q + 1)]


def split_time(weights, model, beside, time, opposite, parts):
    layers = model.shape[0]
    here, there = model[...], beside[...]
    time[...] = weights[0] * here + weights[1] * there
    parts[:layers] = weights[2] * here + weights[3] * there
    opposite[...] = weights[4] * here + weights[5] * there
    parts[layers:] = weights[6] * here + weights[7] * there


def join_time(time, opposite, near, times, joined):
    layers = time.shape[0]
    times[...] = time[...] + near[:layers]
    joined[...] = opposite[...] + near[layers:]


def solve_first(coefs, got, warm, rhs, own, sent, start, rest, lam, mine):
    count, layers = own.shape[:2]
    load_start(warm, 2 * count * tile_of(lax.axis_index("space")), got, start)
    sweeps(coefs, rhs, 0, start, rest, lam, mine)
    for q in range(count):
        own[q] = lam[q, :layers]
        sent[layers * q : layers * (q + 1)] = lam[q, layers:]


def solve_second(times, coefs, got, warm, rhs, forward, own_first, sent_first, own, sent, start, rest, lam, mine):
    count, layers = own.shape[:2]
    tile = tile_of(lax.axis_index("space"))
    source = 2 * count * tile
    load_start(warm, source + count, got, start)
    sweeps(coefs, rhs, count, start, rest, lam, mine)
    near = (layers - 1) * (1 - tile)
    far = (layers - 1) * tile
    total = None
    for q in range(2 * count):
        slope = forward[source + q, near].astype(jnp.float32) - got[count * layers + q]
        if q < count:
            drop = own_first[q, near] - sent_first[layers * q + far]
        else:
            drop = lam[q - count, near] - lam[q - count, layers + far]
        total = slope * drop if total is None else total + slope * drop
    for q in range(count):
        own[q] = lam[q, :layers]
        sent[layers * q : layers * (q + 1)] = lam[q, layers:]
    sent[count * layers] = total


def data_sums(pairs, layers, along_x, along_y, along_z, mass):
    def add(ref, i, value, first):
        ref[i] = value if first else ref[i] + value

    for i in range(layers):
        totals = [None] * 4
        for forward, lam in pairs:
            here, other = forward(i), lam(i)
            terms = [None, face_prod(here, other, 0), face_prod(here, other, 1), here * other]
            if i + 1 < layers:
                terms[0] = (here - forward(i + 1)) * (other - lam(i + 1))
            totals = [t if a is None else (a if t is None else a + t) for a, t in zip(totals, terms)]
        if i + 1 < layers:
            along_x[i] = along_x[i] + totals[0]
        along_y[i] = along_y[i] + totals[1]
        along_z[i] = along_z[i] + totals[2]
        mass[i] = mass[i] + totals[3]


def gather_terms(forward, own_first, own_second, back, times, far, sums, adjoint, time, rounded, sems):
    count, layers = own_first.shape[:2]
    time[...] = times[...] + far[...]
    tile = tile_of(lax.axis_index("space"))
    mine, theirs = 2 * count * tile, 2 * count * (1 - tile)
    for q in range(count):
        rounded[q] = own_first[q].astype(jnp.bfloat16)
        rounded[count + q] = own_second[q].astype(jnp.bfloat16)
        rounded[2 * count + q] = back[layers * q : layers * (q + 1)].astype(jnp.bfloat16)
    copies = [
        pltpu.make_async_copy(rounded.at[: 2 * count], adjoint.at[pl.ds(mine, 2 * count)], sems.at[0]),
        pltpu.make_async_copy(rounded.at[2 * count :], adjoint.at[pl.ds(theirs, count)], sems.at[1]),
    ]
    for copy in copies:
        copy.start()
    sums[...] = jnp.zeros(sums.shape, jnp.float32)
    pairs = []
    for q in range(count):
        pairs.append((mine + q, lambda i, q=q: own_first[q, i]))
        pairs.append((mine + count + q, lambda i, q=q: own_second[q, i]))
        pairs.append((theirs + q, lambda i, q=q: back[layers * q + i]))
    pairs = [(lambda i, s=s: forward[s, i].astype(jnp.float32), lam) for s, lam in pairs]
    data_sums(pairs, layers, sums.at[0], sums.at[1], sums.at[2], sums.at[3])
    for copy in copies:
        copy.wait()


def finish(sums, back, sent, forward, model, other, times, kept, adjoint, gradient, rounded, result, sems):
    tile = tile_of(lax.axis_index("space"))
    count, layers = rounded.shape[:2]
    theirs = 2 * count * (1 - tile) + count
    for q in range(count):
        rounded[q] = back[layers * q : layers * (q + 1)].astype(jnp.bfloat16)
    copies = [pltpu.make_async_copy(rounded, adjoint.at[pl.ds(theirs, count)], sems.at[layers])]
    copies[0].start()
    shape = model.shape[1:]
    pairs = []
    for q in range(count):
        pairs.append((
            lambda i, q=q: forward[theirs + q, i].astype(jnp.float32),
            lambda i, q=q: back[layers * q + i],
        ))
    in_y, in_z = inner(shape, 0), inner(shape, 1)
    low = jnp.where(tile == 0, 0.0, 1.0)
    high = 1.0 - low
    cross = back[count * layers] + sent[count * layers]
    bridge = other[(layers - 1) * tile]
    products, falls = [low * cross], [low * (bridge - model[0])]
    for i in range(layers):
        if i + 1 < layers:
            total = sums[0, i]
            for f, l in pairs:
                total = total + (f(i) - f(i + 1)) * (l(i) - l(i + 1))
            products.append(total)
            falls.append(model[i] - model[i + 1])
        else:
            products.append(high * cross)
            falls.append(high * (model[i] - bridge))
    for i in range(layers):
        total_y, total_z, mass = sums[1, i], sums[2, i], sums[3, i]
        for f, l in pairs:
            here, there = f(i), l(i)
            total_y = total_y + face_prod(here, there, 0)
            total_z = total_z + face_prod(here, there, 1)
            mass = mass + here * there
        total_y = jnp.where(in_y, total_y, 0.0)
        total_z = jnp.where(in_z, total_z, 0.0)
        terms = products[i] + products[i + 1]
        terms = terms + (total_y + before(total_y, 0)) + (total_z + before(total_z, 1))
        value = model[i]
        fall_y = jnp.where(in_y, value - after(value, 0), 0.0)
        fall_z = jnp.where(in_z, value - after(value, 1), 0.0)
        space = falls[i + 1] - falls[i] + (fall_y - before(fall_y, 0)) + (fall_z - before(fall_z, 1))
        result[i] = space + times[i] - jnp.exp(value) * (0.5 * terms + GROUND * mass)
        copies.append(pltpu.make_async_copy(result.at[i], gradient.at[i], sems.at[i]))
        copies[-1].start()
    for copy in copies:
        copy.wait()


V, S, H = pltpu.VMEM, pltpu.SMEM, pltpu.HBM


def call(kernel, operands, spaces, out_shapes, out_spaces=None, scratch=(), aliases=None, micros=1, room=16):
    several = len(out_shapes) > 1
    specs = [pl.BlockSpec(memory_space=m) for m in spaces]
    out_specs = [pl.BlockSpec(memory_space=m) for m in out_spaces or [V] * len(out_shapes)]
    return pl.pallas_call(
        kernel,
        out_shape=out_shapes if several else out_shapes[0],
        in_specs=specs,
        out_specs=out_specs if several else out_specs[0],
        scratch_shapes=list(scratch),
        input_output_aliases=aliases or {},
        compiler_params=pltpu.CompilerParams(vmem_limit_bytes=room * 2**20),
        cost_estimate=pl.CostEstimate(
            flops=micros * 10**9, bytes_accessed=micros * 3 * 10**6, transcendentals=0
        ),
    )(*operands)


def f32(*shape):
    return jax.ShapeDtypeStruct(shape, jnp.float32)


def bf16(*shape):
    return jax.ShapeDtypeStruct(shape, jnp.bfloat16)


def paired(model, forward, warm_start, residual_data, electrodes, survey_order):
    sources, layers, ny, nz = forward.shape
    half, count = sources // 2, sources // 4
    full = 2 * layers
    devices = lax.axis_size("space")
    pairs = []
    for p in range(1, devices, 2):
        pairs += [(p, (p + 1) % devices), ((p + 1) % devices, p)]

    def swap(x, mask=None):
        links = pairs if mask is None else [(p, p ^ mask) for p in range(devices)]
        return lax.ppermute(x, "space", links)

    dma = pltpu.SemaphoreType.DMA
    slab = (layers, ny, nz)
    other = swap(model)
    first = call(pack, (warm_start,), (V,), [f32(count, *slab)])
    got_first = swap(first)
    beside = swap(other, 1)
    rhs, weights_time = call(
        inject,
        (survey_order, residual_data, electrodes.reshape(1, -1)),
        (S, V, V),
        [f32(half, full, ny, nz), f32(8)],
        [V, S],
    )
    coefs, second = call(
        prepare,
        (model, other, warm_start, forward),
        (V, V, V, V),
        [f32(7, full, ny, nz), f32(count * layers + half, ny, nz)],
        scratch=[V((full, ny, nz), jnp.float32)],
    )
    got_second = swap(second)
    field = V((count, full, ny, nz), jnp.float32)
    fields = [field, field, field, V((2, count, full, ny, nz), jnp.float32)]
    block = f32(count, *slab)
    time, opposite, parts = call(
        split_time,
        (weights_time, model, beside),
        (S, V, V),
        [f32(*slab), f32(*slab), f32(2 * layers, ny, nz)],
    )
    near = swap(parts, 4)
    own_first, sent_first = call(
        solve_first,
        (coefs, got_first, warm_start, rhs),
        (V, V, V, V),
        [block, f32(count * layers, ny, nz)],
        scratch=fields,
        micros=3,
    )
    back_first = swap(sent_first)
    times, joined = call(join_time, (time, opposite, near), (V, V, V), [f32(*slab), f32(*slab)])
    far = swap(joined, 8)
    own_second, sent_second = call(
        solve_second,
        (times, coefs, got_second, warm_start, rhs, forward, own_first, sent_first),
        (V, V, V, V, V, V, V, V),
        [block, f32(count * layers + 1, ny, nz)],
        scratch=fields,
        micros=3,
    )
    back_second = swap(sent_second)
    sums, kept, time = call(
        gather_terms,
        (forward, own_first, own_second, back_first, times, far),
        (V, V, V, V, V, V),
        [f32(4, *slab), bf16(*forward.shape), f32(*slab)],
        [V, H, V],
        scratch=[V((3 * count, *slab), jnp.bfloat16), dma((2,))],
        micros=2,
    )
    adjoint, gradient = call(
        finish,
        (sums, back_second, sent_second, forward, model, other, time, kept),
        (V, V, V, V, V, V, V, H),
        [bf16(*forward.shape), f32(*slab)],
        [H, H],
        scratch=[V((count, *slab), jnp.bfloat16), V(slab, jnp.float32), dma((layers + 1,))],
        aliases={7: 0},
    )
    return adjoint, gradient


def solution(mesh):
    body = paired if mesh.shape["space"] == 2 * SURVEYS else layered
    in_specs = (
        P(("groups", "space"), None, None),
        P(None, ("groups", "space"), None, None),
        P(None, ("groups", "space"), None, None),
        P("groups", None, None),
        P("groups"),
        P("groups"),
    )
    out_specs = (P(None, ("groups", "space"), None, None), P(("groups", "space"), None, None))
    return jax.shard_map(body, mesh=mesh, in_specs=in_specs, out_specs=out_specs, check_vma=False)
```

```python
import jax
import jax.numpy as jnp
from jax import lax
from jax.experimental import pallas as pl
from jax.experimental.pallas import tpu as pltpu
from jax.sharding import PartitionSpec as P

SURVEYS = 8
ITERS = 4


GROUND = 0.5
CENTER = 1.0
HALF_WIDTH = 0.99


def padded(shard, sides, width):
    for axis, dim in sides:
        devices, length = (lax.axis_size(axis), shard.shape[dim])
        up = [(i, (i + 1) % devices) for i in range(devices)]
        down = [(j, i) for i, j in up]
        last = lax.slice_in_dim(shard, length - width, length, axis=dim)
        leading = lax.slice_in_dim(shard, 0, width, axis=dim)
        before = lax.ppermute(last, axis, up)
        after = lax.ppermute(leading, axis, down)
        shard = jnp.concatenate([before, shard, after], axis=dim)
    return shard


def swapped(value, axis, bit):
    mask = 2**bit
    pairs = [(source, source ^ mask) for source in range(lax.axis_size(axis))]
    return lax.ppermute(value, axis, pairs)


def face_diff(field, axis):
    count = field.shape[axis]
    return lax.slice_in_dim(field, 0, count - 1, axis=axis) - lax.slice_in_dim(
        field, 1, count, axis=axis
    )


def edge_zeros(field, axis):
    shape = list(field.shape)
    shape[axis] = 1
    return jnp.zeros(shape, jnp.float32)


def pad_diff(faces, axis):
    zeros = edge_zeros(faces, axis)
    return jnp.concatenate([faces, zeros], axis=axis) - jnp.concatenate([zeros, faces], axis=axis)


def pad_sum(faces, axis):
    zeros = edge_zeros(faces, axis)
    return jnp.concatenate([faces, zeros], axis=axis) + jnp.concatenate([zeros, faces], axis=axis)


def extend(field):
    return padded(field, (("space", 1),), 1)


def layered(model, forward, warm_start, residual_data, electrodes, survey_order):
    sources, layers, rows_y, rows_z = forward.shape
    position = lax.axis_index("space")
    devices = lax.axis_size("space")
    tiles = devices // SURVEYS
    half_tiles = tiles // 2
    shifted = position + half_tiles
    tile = shifted % tiles
    survey = shifted // tiles % SURVEYS
    block = position // tiles
    rotation = jnp.where(position % tiles >= half_tiles, 1, 0).astype(jnp.int32)
    valid = jnp.ones((layers + 1,), jnp.float32)
    valid = valid.at[0].set(jnp.where(tile == 0, 0.0, 1.0))
    valid = valid.at[layers].set(jnp.where(tile == tiles - 1, 0.0, 1.0))
    valid_faces = valid[:, None, None]
    model_pad = padded(model, (("space", 0),), 1)
    sigma_pad = jnp.exp(model_pad)
    sigma = sigma_pad[1:-1]
    conduct_x = 0.5 * (sigma_pad[:-1] + sigma_pad[1:]) * valid_faces
    conduct_y = 0.5 * (sigma[:, :-1] + sigma[:, 1:])
    conduct_z = 0.5 * (sigma[:, :, :-1] + sigma[:, :, 1:])
    diagonal = (
        conduct_x[1:]
        + conduct_x[:-1]
        + pad_sum(conduct_y, 1)
        + pad_sum(conduct_z, 2)
        + GROUND * sigma
    )
    inverse_diag = (1.0 / diagonal)[None]

    def operate(field_pad):
        field = field_pad[:, 1:-1]
        flux_x = conduct_x[None] * (field_pad[:, :-1] - field_pad[:, 1:])
        total = flux_x[:, 1:] - flux_x[:, :-1]
        total = total + pad_diff(conduct_y[None] * face_diff(field, 2), 2)
        total = total + pad_diff(conduct_z[None] * face_diff(field, 3), 3)
        return total + GROUND * sigma[None] * field

    cells = layers * rows_y * rows_z
    residual = lax.dynamic_index_in_dim(residual_data, survey, 0, keepdims=False)
    local_index = electrodes - tile * cells
    inside = (local_index >= 0) & (local_index < cells)
    target = jnp.where(inside, local_index, 0)
    amount = jnp.where(inside[None, :], residual, 0.0)
    rhs = jnp.zeros((sources, cells), jnp.float32).at[:, target].add(amount)
    rhs = rhs.reshape(sources, layers, rows_y, rows_z)
    iterate = warm_start.astype(jnp.float32)
    remain = rhs - operate(extend(iterate))
    direction = remain * inverse_diag / CENTER
    weight_now = HALF_WIDTH / CENTER
    for sweep_index in range(ITERS):
        iterate = iterate + direction
        if sweep_index + 1 < ITERS:
            remain = remain - operate(extend(direction))
            weight_new = 1.0 / (2.0 * CENTER / HALF_WIDTH - weight_now)
            direction = weight_new * weight_now * direction + 2.0 * weight_new / HALF_WIDTH * (
                remain * inverse_diag
            )
            weight_now = weight_new
    both = padded(
        jnp.concatenate([forward.astype(jnp.float32), iterate], axis=0), (("space", 1),), 1
    )
    forward_pad = both[:sources]
    adjoint_pad = both[sources:]
    potential = forward_pad[:, 1:-1]
    product_x = (
        jnp.sum(
            (forward_pad[:, :-1] - forward_pad[:, 1:]) * (adjoint_pad[:, :-1] - adjoint_pad[:, 1:]),
            axis=0,
        )
        * valid_faces
    )
    terms = product_x[1:] + product_x[:-1]
    terms = terms + pad_sum(jnp.sum(face_diff(potential, 2) * face_diff(iterate, 2), axis=0), 1)
    terms = terms + pad_sum(jnp.sum(face_diff(potential, 3) * face_diff(iterate, 3), axis=0), 2)
    data_term = -sigma * (0.5 * terms + GROUND * jnp.sum(potential * iterate, axis=0))
    model_x = (model_pad[:-1] - model_pad[1:]) * valid_faces
    space_term = (
        model_x[1:]
        - model_x[:-1]
        + pad_diff(face_diff(model, 1), 1)
        + pad_diff(face_diff(model, 2), 2)
    )
    base_bit = tiles.bit_length() - 1
    collected = model
    for level in range(SURVEYS.bit_length() - 1):
        partner = swapped(collected, "space", base_bit + level)
        upper = block >> level & 1 == 1
        lower_half = jnp.where(upper, partner, collected)
        upper_half = jnp.where(upper, collected, partner)
        collected = jnp.concatenate([lower_half, upper_half], axis=0)
    all_blocks = collected.reshape(SURVEYS, layers, rows_y, rows_z)
    ranks = jnp.arange(SURVEYS, dtype=jnp.int32)
    placed = (survey_order[:, None] == ranks[None, :]).astype(jnp.float32)
    apart = jnp.abs(ranks[:, None] - ranks[None, :])
    degree = jnp.where((ranks == 0) | (ranks == SURVEYS - 1), 1.0, 2.0)
    path = jnp.where(apart == 0, degree[:, None], 0.0) - jnp.where(apart == 1, 1.0, 0.0)
    coupling = jnp.dot(
        placed.T,
        jnp.dot(path, placed, precision=lax.Precision.HIGHEST),
        precision=lax.Precision.HIGHEST,
    )
    row_weights = lax.dynamic_index_in_dim(coupling, survey, 0, keepdims=False)
    block_survey = (ranks + rotation) % SURVEYS
    picker = (block_survey[:, None] == ranks[None, :]).astype(jnp.float32)
    block_weights = jnp.dot(picker, row_weights, precision=lax.Precision.HIGHEST)
    time_term = jnp.sum(block_weights[:, None, None, None] * all_blocks, axis=0)
    return (iterate.astype(jnp.bfloat16), data_term + space_term + time_term)


def weights():
    now = HALF_WIDTH / CENTER
    steps = []
    for _ in range(ITERS - 1):
        new = 1.0 / (2.0 * CENTER / HALF_WIDTH - now)
        steps.append((new * now, 2.0 * new / HALF_WIDTH))
        now = new
    return steps


def after(x, axis):
    return pltpu.roll(x, x.shape[axis] - 1, axis)


def before(x, axis):
    return pltpu.roll(x, 1, axis)


def inner(shape, axis):
    return lax.broadcasted_iota(jnp.int32, shape, axis) < shape[axis] - 1


def face_prod(field, other, axis):
    return (field - after(field, axis)) * (other - after(other, axis))


def tile_of(position):
    return (position + 1) & 1


def survey_of(position):
    return ((position + 1) >> 1) & (SURVEYS - 1)


def pack(warm, first):
    tile = tile_of(lax.axis_index("space"))
    count = first.shape[0]
    for q in range(count):
        first[q] = warm[2 * count * (1 - tile) + q].astype(jnp.float32)


def inject(order, residual, electrodes, coefs, out, weights):
    position = lax.axis_index("space")
    tile = tile_of(position)
    surveys = order.shape[0]
    ranks = []
    for place in [position, position ^ 1] + [position ^ (4 * k) for k in range(4)]:
        found = 0
        for i in range(surveys):
            found = found + jnp.where(order[i] == survey_of(place), i, 0)
        ranks.append(found)
    for k in range(4):
        a = ranks[2 + k]
        ends = jnp.where(a == 0, 1, 0) + jnp.where(a == surveys - 1, 1, 0)
        for m in range(2):
            b = ranks[m]
            value = jnp.where(a == b, 2 - ends, jnp.where(jnp.abs(a - b) == 1, -1, 0))
            weights[2 * k + m] = value.astype(jnp.float32)
    sources, _, rows_y, rows_z = out.shape
    half = residual.shape[1] // 2
    cells = out.shape[1] * rows_y * rows_z
    where_cell = lax.rem(electrodes[...] + tile * (cells // 2), cells)
    row = where_cell // rows_z
    lane = lax.rem(where_cell, rows_z)
    count = row.shape[1]
    rows = cells // rows_z
    at_row = lax.broadcasted_iota(jnp.int32, (rows, count), 0) == row
    at_row = jnp.where(at_row, 1.0, 0.0).astype(jnp.bfloat16)
    at_lane = lax.broadcasted_iota(jnp.int32, (rows_z, count), 0) == lane
    mine = residual[survey_of(position)]
    mine = jnp.where(tile == 0, mine[:half], mine[half:])
    total = None
    for _ in range(3):
        part = mine.astype(jnp.bfloat16).astype(jnp.float32)
        mine = mine - part
        right = jnp.concatenate(
            [jnp.where(at_lane, part[q : q + 1], 0.0) for q in range(sources)], axis=0
        ).astype(jnp.bfloat16)
        term = lax.dot_general(
            at_row, right, (((1,), (1,)), ((), ())), preferred_element_type=jnp.float32
        )
        total = term if total is None else total + term
    for q in range(sources):
        out[q] = coefs[6] * total[:, q * rows_z : (q + 1) * rows_z].reshape(out.shape[1:])


def prepare(model, other, warm, forward, coefs, second, sigma):
    tile = tile_of(lax.axis_index("space"))
    half = warm.shape[0] // 2
    count, layers = half // 2, model.shape[0]
    theirs = half * (1 - tile)
    face = (layers - 1) * (1 - tile)
    for q in range(count):
        second[layers * q : layers * (q + 1)] = warm[theirs + count + q].astype(jnp.float32)
    for q in range(half):
        second[count * layers + q] = forward[theirs + q, face].astype(jnp.float32)
    full = 2 * layers
    shape = model.shape[1:]
    for i in range(layers):
        sigma[i] = jnp.exp(model[i])
        sigma[layers + i] = jnp.exp(other[i])
    in_y, in_z = inner(shape, 0), inner(shape, 1)
    middle = jnp.where(tile == 0, 1.0, 0.0)
    for i in range(full):
        mine = sigma[i]
        up = 0.5 * (mine + sigma[(i + 1) % full])
        down = 0.5 * (mine + sigma[(i - 1) % full])
        if i == layers - 1:
            up = up * middle
        if i == full - 1:
            up = up * (1.0 - middle)
        if i == layers:
            down = down * middle
        if i == 0:
            down = down * (1.0 - middle)
        right_y = jnp.where(in_y, 0.5 * (mine + after(mine, 0)), 0.0)
        right_z = jnp.where(in_z, 0.5 * (mine + after(mine, 1)), 0.0)
        left_y = before(right_y, 0)
        left_z = before(right_z, 1)
        scale = 1.0 / (up + down + right_y + left_y + right_z + left_z + GROUND * mine)
        for k, face in enumerate((up, down, right_y, left_y, right_z, left_z)):
            coefs[k, i] = face * scale
        coefs[6, i] = scale


def sweeps(coefs, rhs, base, start, rest, lam, mine):
    count, full = start.shape[:2]

    def around(field, q, i, weight):
        here = field[q, i]
        total = weight[0] * field[q, (i + 1) % full] + weight[1] * field[q, (i + full - 1) % full]
        total = total + (weight[2] * after(here, 0) + weight[3] * before(here, 0))
        total = total + (weight[4] * after(here, 1) + weight[5] * before(here, 1))
        return here, total

    def first(i, carry):
        weight = [coefs[k, i] for k in range(6)]
        for q in range(count):
            here, total = around(start, q, i, weight)
            step = rhs[base + q, i] - here + total
            mine[0, q, i] = step
            lam[q, i] = here + step
        return carry

    lax.fori_loop(0, full, first, 0, unroll=full)
    for index, (keep, gain) in enumerate(weights()):
        source, target = mine.at[index % 2], mine.at[1 - index % 2]
        last = index == ITERS - 2

        def later(i, carry):
            weight = [coefs[k, i] for k in range(6)]
            for q in range(count):
                here, total = around(source, q, i, weight)
                if index > 0:
                    total = rest[q, i] - here + total
                step = keep * here + gain * total
                if not last:
                    rest[q, i] = total
                    target[q, i] = step
                lam[q, i] = lam[q, i] + step
            return carry

        lax.fori_loop(0, full, later, 0, unroll=full)


def load_start(warm, source, got, start):
    count, full = start.shape[:2]
    layers = full // 2
    for q in range(count):
        start[q, :layers] = warm[source + q].astype(jnp.float32)
        start[q, layers:] = got[q] if len(got.shape) == 4 else got[layers * q : layers * (q + 1)]


def split_time(weights, model, beside, time, opposite, parts):
    layers = model.shape[0]
    here, there = model[...], beside[...]
    time[...] = weights[0] * here + weights[1] * there
    parts[:layers] = weights[2] * here + weights[3] * there
    opposite[...] = weights[4] * here + weights[5] * there
    parts[layers:] = weights[6] * here + weights[7] * there


def join_time(time, opposite, near, solved, times, joined):
    layers = time.shape[0]
    times[...] = time[...] + near[:layers]
    joined[...] = opposite[...] + near[layers:]


def solve_first(coefs, got, warm, rhs, own, sent, start, rest, lam, mine):
    count, layers = own.shape[:2]
    load_start(warm, 2 * count * tile_of(lax.axis_index("space")), got, start)
    sweeps(coefs, rhs, 0, start, rest, lam, mine)
    for q in range(count):
        own[q] = lam[q, :layers]
        sent[layers * q : layers * (q + 1)] = lam[q, layers:]


def solve_second(coefs, got, warm, rhs, forward, own_first, sent_first, own, sent, start, rest, lam, mine):
    count, layers = own.shape[:2]
    tile = tile_of(lax.axis_index("space"))
    source = 2 * count * tile
    load_start(warm, source + count, got, start)
    sweeps(coefs, rhs, count, start, rest, lam, mine)
    near = (layers - 1) * (1 - tile)
    far = (layers - 1) * tile
    total = None
    for q in range(2 * count):
        slope = forward[source + q, near].astype(jnp.float32) - got[count * layers + q]
        if q < count:
            drop = own_first[q, near] - sent_first[layers * q + far]
        else:
            drop = lam[q - count, near] - lam[q - count, layers + far]
        total = slope * drop if total is None else total + slope * drop
    for q in range(count):
        own[q] = lam[q, :layers]
        sent[layers * q : layers * (q + 1)] = lam[q, layers:]
    sent[count * layers] = total


def data_sums(pairs, layers, along_x, along_y, along_z, mass):
    def add(ref, i, value, first):
        ref[i] = value if first else ref[i] + value

    for i in range(layers):
        totals = [None] * 4
        for forward, lam in pairs:
            here, other = forward(i), lam(i)
            terms = [None, face_prod(here, other, 0), face_prod(here, other, 1), here * other]
            if i + 1 < layers:
                terms[0] = (here - forward(i + 1)) * (other - lam(i + 1))
            totals = [t if a is None else (a if t is None else a + t) for a, t in zip(totals, terms)]
        if i + 1 < layers:
            along_x[i] = along_x[i] + totals[0]
        along_y[i] = along_y[i] + totals[1]
        along_z[i] = along_z[i] + totals[2]
        mass[i] = mass[i] + totals[3]


def gather_terms(forward, own_first, own_second, back, sums, adjoint, rounded, sems):
    count, layers = own_first.shape[:2]
    tile = tile_of(lax.axis_index("space"))
    mine, theirs = 2 * count * tile, 2 * count * (1 - tile)
    for q in range(count):
        rounded[q] = own_first[q].astype(jnp.bfloat16)
        rounded[count + q] = own_second[q].astype(jnp.bfloat16)
        rounded[2 * count + q] = back[layers * q : layers * (q + 1)].astype(jnp.bfloat16)
    copies = [
        pltpu.make_async_copy(rounded.at[: 2 * count], adjoint.at[pl.ds(mine, 2 * count)], sems.at[0]),
        pltpu.make_async_copy(rounded.at[2 * count :], adjoint.at[pl.ds(theirs, count)], sems.at[1]),
    ]
    for copy in copies:
        copy.start()
    sums[...] = jnp.zeros(sums.shape, jnp.float32)
    pairs = []
    for q in range(count):
        pairs.append((mine + q, lambda i, q=q: own_first[q, i]))
        pairs.append((mine + count + q, lambda i, q=q: own_second[q, i]))
        pairs.append((theirs + q, lambda i, q=q: back[layers * q + i]))
    pairs = [(lambda i, s=s: forward[s, i].astype(jnp.float32), lam) for s, lam in pairs]
    data_sums(pairs, layers, sums.at[0], sums.at[1], sums.at[2], sums.at[3])
    for copy in copies:
        copy.wait()


def finish(sums, back, sent, forward, model, other, times, far, kept, adjoint, gradient, rounded, result, sems):
    tile = tile_of(lax.axis_index("space"))
    count, layers = rounded.shape[:2]
    theirs = 2 * count * (1 - tile) + count
    for q in range(count):
        rounded[q] = back[layers * q : layers * (q + 1)].astype(jnp.bfloat16)
    copies = [pltpu.make_async_copy(rounded, adjoint.at[pl.ds(theirs, count)], sems.at[layers])]
    copies[0].start()
    shape = model.shape[1:]
    pairs = []
    for q in range(count):
        pairs.append((
            lambda i, q=q: forward[theirs + q, i].astype(jnp.float32),
            lambda i, q=q: back[layers * q + i],
        ))
    in_y, in_z = inner(shape, 0), inner(shape, 1)
    low = jnp.where(tile == 0, 0.0, 1.0)
    high = 1.0 - low
    cross = back[count * layers] + sent[count * layers]
    bridge = other[(layers - 1) * tile]
    products, falls = [low * cross], [low * (bridge - model[0])]
    for i in range(layers):
        if i + 1 < layers:
            total = sums[0, i]
            for f, l in pairs:
                total = total + (f(i) - f(i + 1)) * (l(i) - l(i + 1))
            products.append(total)
            falls.append(model[i] - model[i + 1])
        else:
            products.append(high * cross)
            falls.append(high * (model[i] - bridge))
    for i in range(layers):
        total_y, total_z, mass = sums[1, i], sums[2, i], sums[3, i]
        for f, l in pairs:
            here, there = f(i), l(i)
            total_y = total_y + face_prod(here, there, 0)
            total_z = total_z + face_prod(here, there, 1)
            mass = mass + here * there
        total_y = jnp.where(in_y, total_y, 0.0)
        total_z = jnp.where(in_z, total_z, 0.0)
        terms = products[i] + products[i + 1]
        terms = terms + (total_y + before(total_y, 0)) + (total_z + before(total_z, 1))
        value = model[i]
        fall_y = jnp.where(in_y, value - after(value, 0), 0.0)
        fall_z = jnp.where(in_z, value - after(value, 1), 0.0)
        space = falls[i + 1] - falls[i] + (fall_y - before(fall_y, 0)) + (fall_z - before(fall_z, 1))
        result[i] = space + (times[i] + far[i]) - jnp.exp(value) * (0.5 * terms + GROUND * mass)
        copies.append(pltpu.make_async_copy(result.at[i], gradient.at[i], sems.at[i]))
        copies[-1].start()
    for copy in copies:
        copy.wait()


V, S, H = pltpu.VMEM, pltpu.SMEM, pltpu.HBM


def call(kernel, operands, spaces, out_shapes, out_spaces=None, scratch=(), aliases=None, micros=1, room=16):
    several = len(out_shapes) > 1
    specs = [pl.BlockSpec(memory_space=m) for m in spaces]
    out_specs = [pl.BlockSpec(memory_space=m) for m in out_spaces or [V] * len(out_shapes)]
    return pl.pallas_call(
        kernel,
        out_shape=out_shapes if several else out_shapes[0],
        in_specs=specs,
        out_specs=out_specs if several else out_specs[0],
        scratch_shapes=list(scratch),
        input_output_aliases=aliases or {},
        compiler_params=pltpu.CompilerParams(vmem_limit_bytes=room * 2**20),
        cost_estimate=pl.CostEstimate(
            flops=micros * 10**9, bytes_accessed=micros * 3 * 10**6, transcendentals=0
        ),
    )(*operands)


def f32(*shape):
    return jax.ShapeDtypeStruct(shape, jnp.float32)


def bf16(*shape):
    return jax.ShapeDtypeStruct(shape, jnp.bfloat16)


def paired(model, forward, warm_start, residual_data, electrodes, survey_order):
    sources, layers, ny, nz = forward.shape
    half, count = sources // 2, sources // 4
    full = 2 * layers
    devices = lax.axis_size("space")
    pairs = []
    for p in range(1, devices, 2):
        pairs += [(p, (p + 1) % devices), ((p + 1) % devices, p)]

    def swap(x, mask=None):
        links = pairs if mask is None else [(p, p ^ mask) for p in range(devices)]
        return lax.ppermute(x, "space", links)

    dma = pltpu.SemaphoreType.DMA
    slab = (layers, ny, nz)
    other = swap(model)
    first = call(pack, (warm_start,), (V,), [f32(count, *slab)])
    got_first = swap(first)
    beside = swap(other, 1)
    coefs, second = call(
        prepare,
        (model, other, warm_start, forward),
        (V, V, V, V),
        [f32(7, full, ny, nz), f32(count * layers + half, ny, nz)],
        scratch=[V((full, ny, nz), jnp.float32)],
    )
    rhs, weights_time = call(
        inject,
        (survey_order, residual_data, electrodes.reshape(1, -1), coefs),
        (S, V, V, V),
        [f32(half, full, ny, nz), f32(8)],
        [V, S],
    )
    got_second = swap(second)
    field = V((count, full, ny, nz), jnp.float32)
    fields = [field, field, field, V((2, count, full, ny, nz), jnp.float32)]
    block = f32(count, *slab)
    time, opposite, parts = call(
        split_time,
        (weights_time, model, beside),
        (S, V, V),
        [f32(*slab), f32(*slab), f32(2 * layers, ny, nz)],
    )
    near = swap(parts, 4)
    own_first, sent_first = call(
        solve_first,
        (coefs, got_first, warm_start, rhs),
        (V, V, V, V),
        [block, f32(count * layers, ny, nz)],
        scratch=fields,
        micros=3,
    )
    back_first = swap(sent_first)
    own_second, sent_second = call(
        solve_second,
        (coefs, got_second, warm_start, rhs, forward, own_first, sent_first),
        (V, V, V, V, V, V, V),
        [block, f32(count * layers + 1, ny, nz)],
        scratch=fields,
        micros=3,
    )
    back_second = swap(sent_second)
    times, joined = call(join_time, (time, opposite, near, own_second), (V, V, V, V), [f32(*slab), f32(*slab)])
    far = swap(joined, 8)
    sums, kept = call(
        gather_terms,
        (forward, own_first, own_second, back_first),
        (V, V, V, V),
        [f32(4, *slab), bf16(*forward.shape)],
        [V, H],
        scratch=[V((3 * count, *slab), jnp.bfloat16), dma((2,))],
        micros=2,
    )
    adjoint, gradient = call(
        finish,
        (sums, back_second, sent_second, forward, model, other, times, far, kept),
        (V, V, V, V, V, V, V, V, H),
        [bf16(*forward.shape), f32(*slab)],
        [H, H],
        scratch=[V((count, *slab), jnp.bfloat16), V(slab, jnp.float32), dma((layers + 1,))],
        aliases={8: 0},
    )
    return adjoint, gradient


def solution(mesh):
    body = paired if mesh.shape["space"] == 2 * SURVEYS else layered
    in_specs = (
        P(("groups", "space"), None, None),
        P(None, ("groups", "space"), None, None),
        P(None, ("groups", "space"), None, None),
        P("groups", None, None),
        P("groups"),
        P("groups"),
    )
    out_specs = (P(None, ("groups", "space"), None, None), P(("groups", "space"), None, None))
    return jax.shard_map(body, mesh=mesh, in_specs=in_specs, out_specs=out_specs, check_vma=False)
```

```python
import jax
import jax.numpy as jnp
from jax import lax
from jax.experimental import pallas as pl
from jax.experimental.pallas import tpu as pltpu
from jax.sharding import PartitionSpec as P

SURVEYS = 8
ITERS = 4


GROUND = 0.5
CENTER = 1.0
HALF_WIDTH = 0.99


def padded(shard, sides, width):
    for axis, dim in sides:
        devices, length = (lax.axis_size(axis), shard.shape[dim])
        up = [(i, (i + 1) % devices) for i in range(devices)]
        down = [(j, i) for i, j in up]
        last = lax.slice_in_dim(shard, length - width, length, axis=dim)
        leading = lax.slice_in_dim(shard, 0, width, axis=dim)
        before = lax.ppermute(last, axis, up)
        after = lax.ppermute(leading, axis, down)
        shard = jnp.concatenate([before, shard, after], axis=dim)
    return shard


def swapped(value, axis, bit):
    mask = 2**bit
    pairs = [(source, source ^ mask) for source in range(lax.axis_size(axis))]
    return lax.ppermute(value, axis, pairs)


def face_diff(field, axis):
    count = field.shape[axis]
    return lax.slice_in_dim(field, 0, count - 1, axis=axis) - lax.slice_in_dim(
        field, 1, count, axis=axis
    )


def edge_zeros(field, axis):
    shape = list(field.shape)
    shape[axis] = 1
    return jnp.zeros(shape, jnp.float32)


def pad_diff(faces, axis):
    zeros = edge_zeros(faces, axis)
    return jnp.concatenate([faces, zeros], axis=axis) - jnp.concatenate([zeros, faces], axis=axis)


def pad_sum(faces, axis):
    zeros = edge_zeros(faces, axis)
    return jnp.concatenate([faces, zeros], axis=axis) + jnp.concatenate([zeros, faces], axis=axis)


def extend(field):
    return padded(field, (("space", 1),), 1)


def layered(model, forward, warm_start, residual_data, electrodes, survey_order):
    sources, layers, rows_y, rows_z = forward.shape
    position = lax.axis_index("space")
    devices = lax.axis_size("space")
    tiles = devices // SURVEYS
    half_tiles = tiles // 2
    shifted = position + half_tiles
    tile = shifted % tiles
    survey = shifted // tiles % SURVEYS
    block = position // tiles
    rotation = jnp.where(position % tiles >= half_tiles, 1, 0).astype(jnp.int32)
    valid = jnp.ones((layers + 1,), jnp.float32)
    valid = valid.at[0].set(jnp.where(tile == 0, 0.0, 1.0))
    valid = valid.at[layers].set(jnp.where(tile == tiles - 1, 0.0, 1.0))
    valid_faces = valid[:, None, None]
    model_pad = padded(model, (("space", 0),), 1)
    sigma_pad = jnp.exp(model_pad)
    sigma = sigma_pad[1:-1]
    conduct_x = 0.5 * (sigma_pad[:-1] + sigma_pad[1:]) * valid_faces
    conduct_y = 0.5 * (sigma[:, :-1] + sigma[:, 1:])
    conduct_z = 0.5 * (sigma[:, :, :-1] + sigma[:, :, 1:])
    diagonal = (
        conduct_x[1:]
        + conduct_x[:-1]
        + pad_sum(conduct_y, 1)
        + pad_sum(conduct_z, 2)
        + GROUND * sigma
    )
    inverse_diag = (1.0 / diagonal)[None]

    def operate(field_pad):
        field = field_pad[:, 1:-1]
        flux_x = conduct_x[None] * (field_pad[:, :-1] - field_pad[:, 1:])
        total = flux_x[:, 1:] - flux_x[:, :-1]
        total = total + pad_diff(conduct_y[None] * face_diff(field, 2), 2)
        total = total + pad_diff(conduct_z[None] * face_diff(field, 3), 3)
        return total + GROUND * sigma[None] * field

    cells = layers * rows_y * rows_z
    residual = lax.dynamic_index_in_dim(residual_data, survey, 0, keepdims=False)
    local_index = electrodes - tile * cells
    inside = (local_index >= 0) & (local_index < cells)
    target = jnp.where(inside, local_index, 0)
    amount = jnp.where(inside[None, :], residual, 0.0)
    rhs = jnp.zeros((sources, cells), jnp.float32).at[:, target].add(amount)
    rhs = rhs.reshape(sources, layers, rows_y, rows_z)
    iterate = warm_start.astype(jnp.float32)
    remain = rhs - operate(extend(iterate))
    direction = remain * inverse_diag / CENTER
    weight_now = HALF_WIDTH / CENTER
    for sweep_index in range(ITERS):
        iterate = iterate + direction
        if sweep_index + 1 < ITERS:
            remain = remain - operate(extend(direction))
            weight_new = 1.0 / (2.0 * CENTER / HALF_WIDTH - weight_now)
            direction = weight_new * weight_now * direction + 2.0 * weight_new / HALF_WIDTH * (
                remain * inverse_diag
            )
            weight_now = weight_new
    both = padded(
        jnp.concatenate([forward.astype(jnp.float32), iterate], axis=0), (("space", 1),), 1
    )
    forward_pad = both[:sources]
    adjoint_pad = both[sources:]
    potential = forward_pad[:, 1:-1]
    product_x = (
        jnp.sum(
            (forward_pad[:, :-1] - forward_pad[:, 1:]) * (adjoint_pad[:, :-1] - adjoint_pad[:, 1:]),
            axis=0,
        )
        * valid_faces
    )
    terms = product_x[1:] + product_x[:-1]
    terms = terms + pad_sum(jnp.sum(face_diff(potential, 2) * face_diff(iterate, 2), axis=0), 1)
    terms = terms + pad_sum(jnp.sum(face_diff(potential, 3) * face_diff(iterate, 3), axis=0), 2)
    data_term = -sigma * (0.5 * terms + GROUND * jnp.sum(potential * iterate, axis=0))
    model_x = (model_pad[:-1] - model_pad[1:]) * valid_faces
    space_term = (
        model_x[1:]
        - model_x[:-1]
        + pad_diff(face_diff(model, 1), 1)
        + pad_diff(face_diff(model, 2), 2)
    )
    base_bit = tiles.bit_length() - 1
    collected = model
    for level in range(SURVEYS.bit_length() - 1):
        partner = swapped(collected, "space", base_bit + level)
        upper = block >> level & 1 == 1
        lower_half = jnp.where(upper, partner, collected)
        upper_half = jnp.where(upper, collected, partner)
        collected = jnp.concatenate([lower_half, upper_half], axis=0)
    all_blocks = collected.reshape(SURVEYS, layers, rows_y, rows_z)
    ranks = jnp.arange(SURVEYS, dtype=jnp.int32)
    placed = (survey_order[:, None] == ranks[None, :]).astype(jnp.float32)
    apart = jnp.abs(ranks[:, None] - ranks[None, :])
    degree = jnp.where((ranks == 0) | (ranks == SURVEYS - 1), 1.0, 2.0)
    path = jnp.where(apart == 0, degree[:, None], 0.0) - jnp.where(apart == 1, 1.0, 0.0)
    coupling = jnp.dot(
        placed.T,
        jnp.dot(path, placed, precision=lax.Precision.HIGHEST),
        precision=lax.Precision.HIGHEST,
    )
    row_weights = lax.dynamic_index_in_dim(coupling, survey, 0, keepdims=False)
    block_survey = (ranks + rotation) % SURVEYS
    picker = (block_survey[:, None] == ranks[None, :]).astype(jnp.float32)
    block_weights = jnp.dot(picker, row_weights, precision=lax.Precision.HIGHEST)
    time_term = jnp.sum(block_weights[:, None, None, None] * all_blocks, axis=0)
    return (iterate.astype(jnp.bfloat16), data_term + space_term + time_term)


def weights():
    now = HALF_WIDTH / CENTER
    steps = []
    for _ in range(ITERS - 1):
        new = 1.0 / (2.0 * CENTER / HALF_WIDTH - now)
        steps.append((new * now, 2.0 * new / HALF_WIDTH))
        now = new
    return steps


def after(x, axis):
    return pltpu.roll(x, x.shape[axis] - 1, axis)


def before(x, axis):
    return pltpu.roll(x, 1, axis)


def inner(shape, axis):
    return lax.broadcasted_iota(jnp.int32, shape, axis) < shape[axis] - 1


def face_prod(field, other, axis):
    return (field - after(field, axis)) * (other - after(other, axis))


def tile_of(position):
    return (position + 1) & 1


def survey_of(position):
    return ((position + 1) >> 1) & (SURVEYS - 1)


def pack(warm, first):
    tile = tile_of(lax.axis_index("space"))
    half = warm.shape[0] // 2
    for q in range(first.shape[0]):
        first[q] = warm[half * (1 - tile) + q].astype(jnp.float32)


def pack_second(warm, forward, parts, second):
    tile = tile_of(lax.axis_index("space"))
    half, layers = warm.shape[0] // 2, warm.shape[1]
    count = (second.shape[0] - half) // layers
    theirs = half * (1 - tile)
    face = (layers - 1) * (1 - tile)
    for q in range(count):
        source = theirs + half - count + q
        second[layers * q : layers * (q + 1)] = warm[source].astype(jnp.float32)
    for q in range(half):
        second[count * layers + q] = forward[theirs + q, face].astype(jnp.float32)


def inject(order, residual, electrodes, coefs, out, weights):
    position = lax.axis_index("space")
    tile = tile_of(position)
    surveys = order.shape[0]
    ranks = []
    for place in [position, position ^ 1] + [position ^ (4 * k) for k in range(4)]:
        found = 0
        for i in range(surveys):
            found = found + jnp.where(order[i] == survey_of(place), i, 0)
        ranks.append(found)
    for k in range(4):
        a = ranks[2 + k]
        ends = jnp.where(a == 0, 1, 0) + jnp.where(a == surveys - 1, 1, 0)
        for m in range(2):
            b = ranks[m]
            value = jnp.where(a == b, 2 - ends, jnp.where(jnp.abs(a - b) == 1, -1, 0))
            weights[2 * k + m] = value.astype(jnp.float32)
    sources, _, rows_y, rows_z = out.shape
    half = residual.shape[1] // 2
    cells = out.shape[1] * rows_y * rows_z
    where_cell = lax.rem(electrodes[...] + tile * (cells // 2), cells)
    row = where_cell // rows_z
    lane = lax.rem(where_cell, rows_z)
    count = row.shape[1]
    rows = cells // rows_z
    at_row = lax.broadcasted_iota(jnp.int32, (rows, count), 0) == row
    at_row = jnp.where(at_row, 1.0, 0.0).astype(jnp.bfloat16)
    at_lane = lax.broadcasted_iota(jnp.int32, (rows_z, count), 0) == lane
    mine = residual[survey_of(position)]
    mine = jnp.where(tile == 0, mine[:half], mine[half:])
    total = None
    for _ in range(3):
        part = mine.astype(jnp.bfloat16).astype(jnp.float32)
        mine = mine - part
        right = jnp.concatenate(
            [jnp.where(at_lane, part[q : q + 1], 0.0) for q in range(sources)], axis=0
        ).astype(jnp.bfloat16)
        term = lax.dot_general(
            at_row, right, (((1,), (1,)), ((), ())), preferred_element_type=jnp.float32
        )
        total = term if total is None else total + term
    for q in range(sources):
        out[q] = coefs[6] * total[:, q * rows_z : (q + 1) * rows_z].reshape(out.shape[1:])


def prepare(model, other, coefs, sigma):
    tile = tile_of(lax.axis_index("space"))
    layers = model.shape[0]
    full = 2 * layers
    shape = model.shape[1:]
    for i in range(layers):
        sigma[i] = jnp.exp(model[i])
        sigma[layers + i] = jnp.exp(other[i])
    in_y, in_z = inner(shape, 0), inner(shape, 1)
    middle = jnp.where(tile == 0, 1.0, 0.0)
    for i in range(full):
        mine = sigma[i]
        up = 0.5 * (mine + sigma[(i + 1) % full])
        down = 0.5 * (mine + sigma[(i - 1) % full])
        if i == layers - 1:
            up = up * middle
        if i == full - 1:
            up = up * (1.0 - middle)
        if i == layers:
            down = down * middle
        if i == 0:
            down = down * (1.0 - middle)
        right_y = jnp.where(in_y, 0.5 * (mine + after(mine, 0)), 0.0)
        right_z = jnp.where(in_z, 0.5 * (mine + after(mine, 1)), 0.0)
        left_y = before(right_y, 0)
        left_z = before(right_z, 1)
        scale = 1.0 / (up + down + right_y + left_y + right_z + left_z + GROUND * mine)
        for k, face in enumerate((up, down, right_y, left_y, right_z, left_z)):
            coefs[k, i] = face * scale
        coefs[6, i] = scale


def sweeps(coefs, rhs, base, start, rest, lam, mine):
    count, full = start.shape[:2]

    def around(field, q, i, weight):
        here = field[q, i]
        total = weight[0] * field[q, (i + 1) % full] + weight[1] * field[q, (i + full - 1) % full]
        total = total + (weight[2] * after(here, 0) + weight[3] * before(here, 0))
        total = total + (weight[4] * after(here, 1) + weight[5] * before(here, 1))
        return here, total

    def first(i, carry):
        weight = [coefs[k, i] for k in range(6)]
        for q in range(count):
            here, total = around(start, q, i, weight)
            step = rhs[base + q, i] - here + total
            mine[0, q, i] = step
            lam[q, i] = here + step
        return carry

    lax.fori_loop(0, full, first, 0, unroll=full)
    for index, (keep, gain) in enumerate(weights()):
        source, target = mine.at[index % 2], mine.at[1 - index % 2]
        last = index == ITERS - 2

        def later(i, carry):
            weight = [coefs[k, i] for k in range(6)]
            for q in range(count):
                here, total = around(source, q, i, weight)
                if index > 0:
                    total = rest[q, i] - here + total
                step = keep * here + gain * total
                if not last:
                    rest[q, i] = total
                    target[q, i] = step
                lam[q, i] = lam[q, i] + step
            return carry

        lax.fori_loop(0, full, later, 0, unroll=full)


def load_start(warm, source, got, start):
    count, full = start.shape[:2]
    layers = full // 2
    for q in range(count):
        start[q, :layers] = warm[source + q].astype(jnp.float32)
        start[q, layers:] = got[q] if len(got.shape) == 4 else got[layers * q : layers * (q + 1)]


def split_time(weights, model, beside, time, opposite, parts):
    layers = model.shape[0]
    here, there = model[...], beside[...]
    time[...] = weights[0] * here + weights[1] * there
    parts[:layers] = weights[2] * here + weights[3] * there
    opposite[...] = weights[4] * here + weights[5] * there
    parts[layers:] = weights[6] * here + weights[7] * there


def join_time(time, opposite, near, solved, times, joined):
    layers = time.shape[0]
    times[...] = time[...] + near[:layers]
    joined[...] = opposite[...] + near[layers:]


def solve_first(coefs, got, warm, rhs, own, sent, start, rest, lam, mine):
    count, layers = own.shape[:2]
    half = warm.shape[0] // 2
    load_start(warm, half * tile_of(lax.axis_index("space")), got, start)
    sweeps(coefs, rhs, 0, start, rest, lam, mine)
    for q in range(count):
        own[q] = lam[q, :layers]
        sent[layers * q : layers * (q + 1)] = lam[q, layers:]


def solve_second(coefs, got, warm, rhs, forward, own_first, sent_first, own, sent, start, rest, lam, mine):
    count, layers = own.shape[:2]
    tile = tile_of(lax.axis_index("space"))
    half = warm.shape[0] // 2
    early, source = half - count, half * tile
    load_start(warm, source + early, got, start)
    sweeps(coefs, rhs, early, start, rest, lam, mine)
    near = (layers - 1) * (1 - tile)
    far = (layers - 1) * tile
    total = None
    for q in range(half):
        slope = forward[source + q, near].astype(jnp.float32) - got[count * layers + q]
        if q < early:
            drop = own_first[q, near] - sent_first[layers * q + far]
        else:
            drop = lam[q - early, near] - lam[q - early, layers + far]
        total = slope * drop if total is None else total + slope * drop
    for q in range(count):
        own[q] = lam[q, :layers]
        sent[layers * q : layers * (q + 1)] = lam[q, layers:]
    sent[count * layers] = total


def data_sums(pairs, layers, along_x, along_y, along_z, mass):
    def add(ref, i, value, first):
        ref[i] = value if first else ref[i] + value

    for i in range(layers):
        totals = [None] * 4
        for forward, lam in pairs:
            here, other = forward(i), lam(i)
            terms = [None, face_prod(here, other, 0), face_prod(here, other, 1), here * other]
            if i + 1 < layers:
                terms[0] = (here - forward(i + 1)) * (other - lam(i + 1))
            totals = [t if a is None else (a if t is None else a + t) for a, t in zip(totals, terms)]
        if i + 1 < layers:
            along_x[i] = along_x[i] + totals[0]
        along_y[i] = along_y[i] + totals[1]
        along_z[i] = along_z[i] + totals[2]
        mass[i] = mass[i] + totals[3]


def gather_terms(forward, own_first, own_second, back, sums, adjoint, rounded, sems):
    early, layers = own_first.shape[:2]
    half = early + own_second.shape[0]
    tile = tile_of(lax.axis_index("space"))
    mine, theirs = half * tile, half * (1 - tile)
    rounded[:early] = own_first[...].astype(jnp.bfloat16)
    rounded[early:half] = own_second[...].astype(jnp.bfloat16)
    for q in range(early):
        rounded[half + q] = back[layers * q : layers * (q + 1)].astype(jnp.bfloat16)
    copies = [
        pltpu.make_async_copy(rounded.at[:half], adjoint.at[pl.ds(mine, half)], sems.at[0]),
        pltpu.make_async_copy(rounded.at[half:], adjoint.at[pl.ds(theirs, early)], sems.at[1]),
    ]
    for copy in copies:
        copy.start()
    sums[...] = jnp.zeros(sums.shape, jnp.float32)
    pairs = []
    for q in range(half):
        if q < early:
            pairs.append((mine + q, lambda i, q=q: own_first[q, i]))
            pairs.append((theirs + q, lambda i, q=q: back[layers * q + i]))
        else:
            pairs.append((mine + q, lambda i, q=q: own_second[q - early, i]))
    pairs = [(lambda i, s=s: forward[s, i].astype(jnp.float32), lam) for s, lam in pairs]
    data_sums(pairs, layers, sums.at[0], sums.at[1], sums.at[2], sums.at[3])
    for copy in copies:
        copy.wait()


def finish(sums, back, sent, forward, model, other, times, far, kept, adjoint, gradient, rounded, result, sems):
    tile = tile_of(lax.axis_index("space"))
    count, layers = rounded.shape[:2]
    half = forward.shape[0] // 2
    theirs = half * (1 - tile) + half - count
    for q in range(count):
        rounded[q] = back[layers * q : layers * (q + 1)].astype(jnp.bfloat16)
    copies = [pltpu.make_async_copy(rounded, adjoint.at[pl.ds(theirs, count)], sems.at[layers])]
    copies[0].start()
    shape = model.shape[1:]
    pairs = []
    for q in range(count):
        pairs.append((
            lambda i, q=q: forward[theirs + q, i].astype(jnp.float32),
            lambda i, q=q: back[layers * q + i],
        ))
    in_y, in_z = inner(shape, 0), inner(shape, 1)
    low = jnp.where(tile == 0, 0.0, 1.0)
    high = 1.0 - low
    cross = back[count * layers] + sent[count * layers]
    bridge = other[(layers - 1) * tile]
    products, falls = [low * cross], [low * (bridge - model[0])]
    for i in range(layers):
        if i + 1 < layers:
            total = sums[0, i]
            for f, l in pairs:
                total = total + (f(i) - f(i + 1)) * (l(i) - l(i + 1))
            products.append(total)
            falls.append(model[i] - model[i + 1])
        else:
            products.append(high * cross)
            falls.append(high * (model[i] - bridge))
    for i in range(layers):
        total_y, total_z, mass = sums[1, i], sums[2, i], sums[3, i]
        for f, l in pairs:
            here, there = f(i), l(i)
            total_y = total_y + face_prod(here, there, 0)
            total_z = total_z + face_prod(here, there, 1)
            mass = mass + here * there
        total_y = jnp.where(in_y, total_y, 0.0)
        total_z = jnp.where(in_z, total_z, 0.0)
        terms = products[i] + products[i + 1]
        terms = terms + (total_y + before(total_y, 0)) + (total_z + before(total_z, 1))
        value = model[i]
        fall_y = jnp.where(in_y, value - after(value, 0), 0.0)
        fall_z = jnp.where(in_z, value - after(value, 1), 0.0)
        space = falls[i + 1] - falls[i] + (fall_y - before(fall_y, 0)) + (fall_z - before(fall_z, 1))
        result[i] = space + (times[i] + far[i]) - jnp.exp(value) * (0.5 * terms + GROUND * mass)
        copies.append(pltpu.make_async_copy(result.at[i], gradient.at[i], sems.at[i]))
        copies[-1].start()
    for copy in copies:
        copy.wait()


V, S, H = pltpu.VMEM, pltpu.SMEM, pltpu.HBM


def call(kernel, operands, spaces, out_shapes, out_spaces=None, scratch=(), aliases=None, micros=1, room=16):
    several = len(out_shapes) > 1
    specs = [pl.BlockSpec(memory_space=m) for m in spaces]
    out_specs = [pl.BlockSpec(memory_space=m) for m in out_spaces or [V] * len(out_shapes)]
    return pl.pallas_call(
        kernel,
        out_shape=out_shapes if several else out_shapes[0],
        in_specs=specs,
        out_specs=out_specs if several else out_specs[0],
        scratch_shapes=list(scratch),
        input_output_aliases=aliases or {},
        compiler_params=pltpu.CompilerParams(vmem_limit_bytes=room * 2**20),
        cost_estimate=pl.CostEstimate(
            flops=micros * 10**9, bytes_accessed=micros * 3 * 10**6, transcendentals=0
        ),
    )(*operands)


def f32(*shape):
    return jax.ShapeDtypeStruct(shape, jnp.float32)


def bf16(*shape):
    return jax.ShapeDtypeStruct(shape, jnp.bfloat16)


def paired(model, forward, warm_start, residual_data, electrodes, survey_order):
    sources, layers, ny, nz = forward.shape
    half = sources // 2
    late = (half + 3) // 4
    early = half - late
    full = 2 * layers
    devices = lax.axis_size("space")
    pairs = []
    for p in range(1, devices, 2):
        pairs += [(p, (p + 1) % devices), ((p + 1) % devices, p)]

    def swap(x, mask=None):
        links = pairs if mask is None else [(p, p ^ mask) for p in range(devices)]
        return lax.ppermute(x, "space", links)

    dma = pltpu.SemaphoreType.DMA
    slab = (layers, ny, nz)
    other = swap(model)
    first = call(pack, (warm_start,), (V,), [f32(early, *slab)])
    got_first = swap(first)
    beside = swap(other, 1)
    coefs = call(
        prepare,
        (model, other),
        (V, V),
        [f32(7, full, ny, nz)],
        scratch=[V((full, ny, nz), jnp.float32)],
    )
    rhs, weights_time = call(
        inject,
        (survey_order, residual_data, electrodes.reshape(1, -1), coefs),
        (S, V, V, V),
        [f32(half, full, ny, nz), f32(8)],
        [V, S],
    )

    def fields(count):
        field = V((count, full, ny, nz), jnp.float32)
        return [field, field, field, V((2, count, full, ny, nz), jnp.float32)]

    time, opposite, parts = call(
        split_time,
        (weights_time, model, beside),
        (S, V, V),
        [f32(*slab), f32(*slab), f32(2 * layers, ny, nz)],
    )
    near = swap(parts, 4)
    second = call(
        pack_second, (warm_start, forward, parts), (V, V, V), [f32(late * layers + half, ny, nz)]
    )
    got_second = swap(second)
    own_first, sent_first = call(
        solve_first,
        (coefs, got_first, warm_start, rhs),
        (V, V, V, V),
        [f32(early, *slab), f32(early * layers, ny, nz)],
        scratch=fields(early),
        micros=3,
    )
    back_first = swap(sent_first)
    own_second, sent_second = call(
        solve_second,
        (coefs, got_second, warm_start, rhs, forward, own_first, sent_first),
        (V, V, V, V, V, V, V),
        [f32(late, *slab), f32(late * layers + 1, ny, nz)],
        scratch=fields(late),
        micros=3,
    )
    back_second = swap(sent_second)
    times, joined = call(join_time, (time, opposite, near, own_second), (V, V, V, V), [f32(*slab), f32(*slab)])
    far = swap(joined, 8)
    sums, kept = call(
        gather_terms,
        (forward, own_first, own_second, back_first),
        (V, V, V, V),
        [f32(4, *slab), bf16(*forward.shape)],
        [V, H],
        scratch=[V((half + early, *slab), jnp.bfloat16), dma((2,))],
        micros=1,
    )
    adjoint, gradient = call(
        finish,
        (sums, back_second, sent_second, forward, model, other, times, far, kept),
        (V, V, V, V, V, V, V, V, H),
        [bf16(*forward.shape), f32(*slab)],
        [H, H],
        scratch=[V((late, *slab), jnp.bfloat16), V(slab, jnp.float32), dma((layers + 1,))],
        aliases={8: 0},
    )
    return adjoint, gradient


def solution(mesh):
    body = paired if mesh.shape["space"] == 2 * SURVEYS else layered
    in_specs = (
        P(("groups", "space"), None, None),
        P(None, ("groups", "space"), None, None),
        P(None, ("groups", "space"), None, None),
        P("groups", None, None),
        P("groups"),
        P("groups"),
    )
    out_specs = (P(None, ("groups", "space"), None, None), P(("groups", "space"), None, None))
    return jax.shard_map(body, mesh=mesh, in_specs=in_specs, out_specs=out_specs, check_vma=False)
```

```python
import jax
import jax.numpy as jnp
from jax import lax
from jax.experimental import pallas as pl
from jax.experimental.pallas import tpu as pltpu
from jax.sharding import PartitionSpec as P

SURVEYS = 8
ITERS = 4


GROUND = 0.5
CENTER = 1.0
HALF_WIDTH = 0.99


def padded(shard, sides, width):
    for axis, dim in sides:
        devices, length = (lax.axis_size(axis), shard.shape[dim])
        up = [(i, (i + 1) % devices) for i in range(devices)]
        down = [(j, i) for i, j in up]
        last = lax.slice_in_dim(shard, length - width, length, axis=dim)
        leading = lax.slice_in_dim(shard, 0, width, axis=dim)
        before = lax.ppermute(last, axis, up)
        after = lax.ppermute(leading, axis, down)
        shard = jnp.concatenate([before, shard, after], axis=dim)
    return shard


def swapped(value, axis, bit):
    mask = 2**bit
    pairs = [(source, source ^ mask) for source in range(lax.axis_size(axis))]
    return lax.ppermute(value, axis, pairs)


def face_diff(field, axis):
    count = field.shape[axis]
    return lax.slice_in_dim(field, 0, count - 1, axis=axis) - lax.slice_in_dim(
        field, 1, count, axis=axis
    )


def edge_zeros(field, axis):
    shape = list(field.shape)
    shape[axis] = 1
    return jnp.zeros(shape, jnp.float32)


def pad_diff(faces, axis):
    zeros = edge_zeros(faces, axis)
    return jnp.concatenate([faces, zeros], axis=axis) - jnp.concatenate([zeros, faces], axis=axis)


def pad_sum(faces, axis):
    zeros = edge_zeros(faces, axis)
    return jnp.concatenate([faces, zeros], axis=axis) + jnp.concatenate([zeros, faces], axis=axis)


def extend(field):
    return padded(field, (("space", 1),), 1)


def layered(model, forward, warm_start, residual_data, electrodes, survey_order):
    sources, layers, rows_y, rows_z = forward.shape
    position = lax.axis_index("space")
    devices = lax.axis_size("space")
    tiles = devices // SURVEYS
    half_tiles = tiles // 2
    shifted = position + half_tiles
    tile = shifted % tiles
    survey = shifted // tiles % SURVEYS
    block = position // tiles
    rotation = jnp.where(position % tiles >= half_tiles, 1, 0).astype(jnp.int32)
    valid = jnp.ones((layers + 1,), jnp.float32)
    valid = valid.at[0].set(jnp.where(tile == 0, 0.0, 1.0))
    valid = valid.at[layers].set(jnp.where(tile == tiles - 1, 0.0, 1.0))
    valid_faces = valid[:, None, None]
    model_pad = padded(model, (("space", 0),), 1)
    sigma_pad = jnp.exp(model_pad)
    sigma = sigma_pad[1:-1]
    conduct_x = 0.5 * (sigma_pad[:-1] + sigma_pad[1:]) * valid_faces
    conduct_y = 0.5 * (sigma[:, :-1] + sigma[:, 1:])
    conduct_z = 0.5 * (sigma[:, :, :-1] + sigma[:, :, 1:])
    diagonal = (
        conduct_x[1:]
        + conduct_x[:-1]
        + pad_sum(conduct_y, 1)
        + pad_sum(conduct_z, 2)
        + GROUND * sigma
    )
    inverse_diag = (1.0 / diagonal)[None]

    def operate(field_pad):
        field = field_pad[:, 1:-1]
        flux_x = conduct_x[None] * (field_pad[:, :-1] - field_pad[:, 1:])
        total = flux_x[:, 1:] - flux_x[:, :-1]
        total = total + pad_diff(conduct_y[None] * face_diff(field, 2), 2)
        total = total + pad_diff(conduct_z[None] * face_diff(field, 3), 3)
        return total + GROUND * sigma[None] * field

    cells = layers * rows_y * rows_z
    residual = lax.dynamic_index_in_dim(residual_data, survey, 0, keepdims=False)
    local_index = electrodes - tile * cells
    inside = (local_index >= 0) & (local_index < cells)
    target = jnp.where(inside, local_index, 0)
    amount = jnp.where(inside[None, :], residual, 0.0)
    rhs = jnp.zeros((sources, cells), jnp.float32).at[:, target].add(amount)
    rhs = rhs.reshape(sources, layers, rows_y, rows_z)
    iterate = warm_start.astype(jnp.float32)
    remain = rhs - operate(extend(iterate))
    direction = remain * inverse_diag / CENTER
    weight_now = HALF_WIDTH / CENTER
    for sweep_index in range(ITERS):
        iterate = iterate + direction
        if sweep_index + 1 < ITERS:
            remain = remain - operate(extend(direction))
            weight_new = 1.0 / (2.0 * CENTER / HALF_WIDTH - weight_now)
            direction = weight_new * weight_now * direction + 2.0 * weight_new / HALF_WIDTH * (
                remain * inverse_diag
            )
            weight_now = weight_new
    both = padded(
        jnp.concatenate([forward.astype(jnp.float32), iterate], axis=0), (("space", 1),), 1
    )
    forward_pad = both[:sources]
    adjoint_pad = both[sources:]
    potential = forward_pad[:, 1:-1]
    product_x = (
        jnp.sum(
            (forward_pad[:, :-1] - forward_pad[:, 1:]) * (adjoint_pad[:, :-1] - adjoint_pad[:, 1:]),
            axis=0,
        )
        * valid_faces
    )
    terms = product_x[1:] + product_x[:-1]
    terms = terms + pad_sum(jnp.sum(face_diff(potential, 2) * face_diff(iterate, 2), axis=0), 1)
    terms = terms + pad_sum(jnp.sum(face_diff(potential, 3) * face_diff(iterate, 3), axis=0), 2)
    data_term = -sigma * (0.5 * terms + GROUND * jnp.sum(potential * iterate, axis=0))
    model_x = (model_pad[:-1] - model_pad[1:]) * valid_faces
    space_term = (
        model_x[1:]
        - model_x[:-1]
        + pad_diff(face_diff(model, 1), 1)
        + pad_diff(face_diff(model, 2), 2)
    )
    base_bit = tiles.bit_length() - 1
    collected = model
    for level in range(SURVEYS.bit_length() - 1):
        partner = swapped(collected, "space", base_bit + level)
        upper = block >> level & 1 == 1
        lower_half = jnp.where(upper, partner, collected)
        upper_half = jnp.where(upper, collected, partner)
        collected = jnp.concatenate([lower_half, upper_half], axis=0)
    all_blocks = collected.reshape(SURVEYS, layers, rows_y, rows_z)
    ranks = jnp.arange(SURVEYS, dtype=jnp.int32)
    placed = (survey_order[:, None] == ranks[None, :]).astype(jnp.float32)
    apart = jnp.abs(ranks[:, None] - ranks[None, :])
    degree = jnp.where((ranks == 0) | (ranks == SURVEYS - 1), 1.0, 2.0)
    path = jnp.where(apart == 0, degree[:, None], 0.0) - jnp.where(apart == 1, 1.0, 0.0)
    coupling = jnp.dot(
        placed.T,
        jnp.dot(path, placed, precision=lax.Precision.HIGHEST),
        precision=lax.Precision.HIGHEST,
    )
    row_weights = lax.dynamic_index_in_dim(coupling, survey, 0, keepdims=False)
    block_survey = (ranks + rotation) % SURVEYS
    picker = (block_survey[:, None] == ranks[None, :]).astype(jnp.float32)
    block_weights = jnp.dot(picker, row_weights, precision=lax.Precision.HIGHEST)
    time_term = jnp.sum(block_weights[:, None, None, None] * all_blocks, axis=0)
    return (iterate.astype(jnp.bfloat16), data_term + space_term + time_term)


def weights():
    now = HALF_WIDTH / CENTER
    steps = []
    for _ in range(ITERS - 1):
        new = 1.0 / (2.0 * CENTER / HALF_WIDTH - now)
        steps.append((new * now, 2.0 * new / HALF_WIDTH))
        now = new
    return steps


def after(x, axis):
    return pltpu.roll(x, x.shape[axis] - 1, axis)


def before(x, axis):
    return pltpu.roll(x, 1, axis)


def inner(shape, axis):
    return lax.broadcasted_iota(jnp.int32, shape, axis) < shape[axis] - 1


def face_prod(field, other, axis):
    return (field - after(field, axis)) * (other - after(other, axis))


def tile_of(position):
    return (position + 1) & 1


def survey_of(position):
    return ((position + 1) >> 1) & (SURVEYS - 1)


def pack(warm, first):
    tile = tile_of(lax.axis_index("space"))
    half = warm.shape[0] // 2
    for q in range(first.shape[0]):
        first[q] = warm[half * (1 - tile) + q].astype(jnp.float32)


def pack_second(warm, forward, parts, second):
    tile = tile_of(lax.axis_index("space"))
    half, layers = warm.shape[0] // 2, warm.shape[1]
    count = (second.shape[0] - half) // layers
    theirs = half * (1 - tile)
    face = (layers - 1) * (1 - tile)
    for q in range(count):
        source = theirs + half - count + q
        second[layers * q : layers * (q + 1)] = warm[source].astype(jnp.float32)
    for q in range(half):
        second[count * layers + q] = forward[theirs + q, face].astype(jnp.float32)


def inject(order, residual, electrodes, coefs, out, weights):
    position = lax.axis_index("space")
    tile = tile_of(position)
    surveys = order.shape[0]
    ranks = []
    for place in [position, position ^ 1] + [position ^ (4 * k) for k in range(4)]:
        found = 0
        for i in range(surveys):
            found = found + jnp.where(order[i] == survey_of(place), i, 0)
        ranks.append(found)
    for k in range(4):
        a = ranks[2 + k]
        ends = jnp.where(a == 0, 1, 0) + jnp.where(a == surveys - 1, 1, 0)
        for m in range(2):
            b = ranks[m]
            value = jnp.where(a == b, 2 - ends, jnp.where(jnp.abs(a - b) == 1, -1, 0))
            weights[2 * k + m] = value.astype(jnp.float32)
    sources, _, rows_y, rows_z = out.shape
    half = residual.shape[1] // 2
    cells = out.shape[1] * rows_y * rows_z
    where_cell = lax.rem(electrodes[...] + tile * (cells // 2), cells)
    row = where_cell // rows_z
    lane = lax.rem(where_cell, rows_z)
    count = row.shape[1]
    rows = cells // rows_z
    at_row = lax.broadcasted_iota(jnp.int32, (rows, count), 0) == row
    at_row = jnp.where(at_row, 1.0, 0.0).astype(jnp.bfloat16)
    at_lane = lax.broadcasted_iota(jnp.int32, (rows_z, count), 0) == lane
    mine = residual[survey_of(position)]
    mine = jnp.where(tile == 0, mine[:half], mine[half:])
    total = None
    for _ in range(3):
        part = mine.astype(jnp.bfloat16).astype(jnp.float32)
        mine = mine - part
        right = jnp.concatenate(
            [jnp.where(at_lane, part[q : q + 1], 0.0) for q in range(sources)], axis=0
        ).astype(jnp.bfloat16)
        term = lax.dot_general(
            at_row, right, (((1,), (1,)), ((), ())), preferred_element_type=jnp.float32
        )
        total = term if total is None else total + term
    for q in range(sources):
        out[q] = coefs[6] * total[:, q * rows_z : (q + 1) * rows_z].reshape(out.shape[1:])


def prepare(model, other, coefs, sigma):
    tile = tile_of(lax.axis_index("space"))
    layers = model.shape[0]
    full = 2 * layers
    shape = model.shape[1:]
    for i in range(layers):
        sigma[i] = jnp.exp(model[i])
        sigma[layers + i] = jnp.exp(other[i])
    in_y, in_z = inner(shape, 0), inner(shape, 1)
    middle = jnp.where(tile == 0, 1.0, 0.0)
    for i in range(full):
        mine = sigma[i]
        up = 0.5 * (mine + sigma[(i + 1) % full])
        down = 0.5 * (mine + sigma[(i - 1) % full])
        if i == layers - 1:
            up = up * middle
        if i == full - 1:
            up = up * (1.0 - middle)
        if i == layers:
            down = down * middle
        if i == 0:
            down = down * (1.0 - middle)
        right_y = jnp.where(in_y, 0.5 * (mine + after(mine, 0)), 0.0)
        right_z = jnp.where(in_z, 0.5 * (mine + after(mine, 1)), 0.0)
        left_y = before(right_y, 0)
        left_z = before(right_z, 1)
        scale = 1.0 / (up + down + right_y + left_y + right_z + left_z + GROUND * mine)
        for k, face in enumerate((up, down, right_y, left_y, right_z, left_z)):
            coefs[k, i] = face * scale
        coefs[6, i] = scale


def sweeps(coefs, rhs, base, start, rest, lam, mine):
    count, full = start.shape[:2]

    def around(field, q, i, weight):
        here = field[q, i]
        total = weight[0] * field[q, (i + 1) % full] + weight[1] * field[q, (i + full - 1) % full]
        total = total + (weight[2] * after(here, 0) + weight[3] * before(here, 0))
        total = total + (weight[4] * after(here, 1) + weight[5] * before(here, 1))
        return here, total

    def first(i, carry):
        weight = [coefs[k, i] for k in range(6)]
        for q in range(count):
            here, total = around(start, q, i, weight)
            step = rhs[base + q, i] - here + total
            mine[0, q, i] = step
            lam[q, i] = here + step
        return carry

    lax.fori_loop(0, full, first, 0, unroll=full)
    for index, (keep, gain) in enumerate(weights()):
        source, target = mine.at[index % 2], mine.at[1 - index % 2]
        last = index == ITERS - 2

        def later(i, carry):
            weight = [coefs[k, i] for k in range(6)]
            for q in range(count):
                here, total = around(source, q, i, weight)
                if index > 0:
                    total = rest[q, i] - here + total
                step = keep * here + gain * total
                if not last:
                    rest[q, i] = total
                    target[q, i] = step
                lam[q, i] = lam[q, i] + step
            return carry

        lax.fori_loop(0, full, later, 0, unroll=full)


def load_start(warm, source, got, start):
    count, full = start.shape[:2]
    layers = full // 2
    for q in range(count):
        start[q, :layers] = warm[source + q].astype(jnp.float32)
        start[q, layers:] = got[q] if len(got.shape) == 4 else got[layers * q : layers * (q + 1)]


def split_time(weights, model, beside, time, opposite, parts):
    layers = model.shape[0]
    here, there = model[...], beside[...]
    time[...] = weights[0] * here + weights[1] * there
    parts[:layers] = weights[2] * here + weights[3] * there
    opposite[...] = weights[4] * here + weights[5] * there
    parts[layers:] = weights[6] * here + weights[7] * there


def join_time(time, opposite, near, times, joined):
    layers = time.shape[0]
    times[...] = time[...] + near[:layers]
    joined[...] = opposite[...] + near[layers:]


def solve_first(coefs, got, warm, rhs, own, sent, start, rest, lam, mine):
    count, layers = own.shape[:2]
    half = warm.shape[0] // 2
    load_start(warm, half * tile_of(lax.axis_index("space")), got, start)
    sweeps(coefs, rhs, 0, start, rest, lam, mine)
    for q in range(count):
        own[q] = lam[q, :layers]
        sent[layers * q : layers * (q + 1)] = lam[q, layers:]


def solve_second(coefs, got, warm, rhs, forward, own_first, sent_first, own, sent, start, rest, lam, mine):
    count, layers = own.shape[:2]
    tile = tile_of(lax.axis_index("space"))
    half = warm.shape[0] // 2
    early, source = half - count, half * tile
    load_start(warm, source + early, got, start)
    sweeps(coefs, rhs, early, start, rest, lam, mine)
    near = (layers - 1) * (1 - tile)
    far = (layers - 1) * tile
    total = None
    for q in range(half):
        slope = forward[source + q, near].astype(jnp.float32) - got[count * layers + q]
        if q < early:
            drop = own_first[q, near] - sent_first[layers * q + far]
        else:
            drop = lam[q - early, near] - lam[q - early, layers + far]
        total = slope * drop if total is None else total + slope * drop
    for q in range(count):
        own[q] = lam[q, :layers]
        sent[layers * q : layers * (q + 1)] = lam[q, layers:]
    sent[count * layers] = total


def data_sums(pairs, layers, along_x, along_y, along_z, mass):
    def add(ref, i, value, first):
        ref[i] = value if first else ref[i] + value

    for i in range(layers):
        totals = [None] * 4
        for forward, lam in pairs:
            here, other = forward(i), lam(i)
            terms = [None, face_prod(here, other, 0), face_prod(here, other, 1), here * other]
            if i + 1 < layers:
                terms[0] = (here - forward(i + 1)) * (other - lam(i + 1))
            totals = [t if a is None else (a if t is None else a + t) for a, t in zip(totals, terms)]
        if i + 1 < layers:
            along_x[i] = along_x[i] + totals[0]
        along_y[i] = along_y[i] + totals[1]
        along_z[i] = along_z[i] + totals[2]
        mass[i] = mass[i] + totals[3]


def gather_terms(forward, own_first, own_second, back, times, far, sums, adjoint, time, rounded, sems):
    time[...] = times[...] + far[...]
    early, layers = own_first.shape[:2]
    half = early + own_second.shape[0]
    tile = tile_of(lax.axis_index("space"))
    mine, theirs = half * tile, half * (1 - tile)
    rounded[:early] = own_first[...].astype(jnp.bfloat16)
    rounded[early:half] = own_second[...].astype(jnp.bfloat16)
    for q in range(early):
        rounded[half + q] = back[layers * q : layers * (q + 1)].astype(jnp.bfloat16)
    copies = [
        pltpu.make_async_copy(rounded.at[:half], adjoint.at[pl.ds(mine, half)], sems.at[0]),
        pltpu.make_async_copy(rounded.at[half:], adjoint.at[pl.ds(theirs, early)], sems.at[1]),
    ]
    for copy in copies:
        copy.start()
    sums[...] = jnp.zeros(sums.shape, jnp.float32)
    pairs = []
    for q in range(half):
        if q < early:
            pairs.append((mine + q, lambda i, q=q: own_first[q, i]))
            pairs.append((theirs + q, lambda i, q=q: back[layers * q + i]))
        else:
            pairs.append((mine + q, lambda i, q=q: own_second[q - early, i]))
    pairs = [(lambda i, s=s: forward[s, i].astype(jnp.float32), lam) for s, lam in pairs]
    data_sums(pairs, layers, sums.at[0], sums.at[1], sums.at[2], sums.at[3])
    for copy in copies:
        copy.wait()


def finish(sums, back, sent, forward, model, other, times, kept, adjoint, gradient, rounded, result, sems):
    tile = tile_of(lax.axis_index("space"))
    count, layers = rounded.shape[:2]
    half = forward.shape[0] // 2
    theirs = half * (1 - tile) + half - count
    for q in range(count):
        rounded[q] = back[layers * q : layers * (q + 1)].astype(jnp.bfloat16)
    copies = [pltpu.make_async_copy(rounded, adjoint.at[pl.ds(theirs, count)], sems.at[layers])]
    copies[0].start()
    shape = model.shape[1:]
    pairs = []
    for q in range(count):
        pairs.append((
            lambda i, q=q: forward[theirs + q, i].astype(jnp.float32),
            lambda i, q=q: back[layers * q + i],
        ))
    in_y, in_z = inner(shape, 0), inner(shape, 1)
    low = jnp.where(tile == 0, 0.0, 1.0)
    high = 1.0 - low
    cross = back[count * layers] + sent[count * layers]
    bridge = other[(layers - 1) * tile]
    products, falls = [low * cross], [low * (bridge - model[0])]
    for i in range(layers):
        if i + 1 < layers:
            total = sums[0, i]
            for f, l in pairs:
                total = total + (f(i) - f(i + 1)) * (l(i) - l(i + 1))
            products.append(total)
            falls.append(model[i] - model[i + 1])
        else:
            products.append(high * cross)
            falls.append(high * (model[i] - bridge))
    for i in range(layers):
        total_y, total_z, mass = sums[1, i], sums[2, i], sums[3, i]
        for f, l in pairs:
            here, there = f(i), l(i)
            total_y = total_y + face_prod(here, there, 0)
            total_z = total_z + face_prod(here, there, 1)
            mass = mass + here * there
        total_y = jnp.where(in_y, total_y, 0.0)
        total_z = jnp.where(in_z, total_z, 0.0)
        terms = products[i] + products[i + 1]
        terms = terms + (total_y + before(total_y, 0)) + (total_z + before(total_z, 1))
        value = model[i]
        fall_y = jnp.where(in_y, value - after(value, 0), 0.0)
        fall_z = jnp.where(in_z, value - after(value, 1), 0.0)
        space = falls[i + 1] - falls[i] + (fall_y - before(fall_y, 0)) + (fall_z - before(fall_z, 1))
        result[i] = space + times[i] - jnp.exp(value) * (0.5 * terms + GROUND * mass)
        copies.append(pltpu.make_async_copy(result.at[i], gradient.at[i], sems.at[i]))
        copies[-1].start()
    for copy in copies:
        copy.wait()


V, S, H = pltpu.VMEM, pltpu.SMEM, pltpu.HBM


def call(kernel, operands, spaces, out_shapes, out_spaces=None, scratch=(), aliases=None, micros=1, room=16):
    several = len(out_shapes) > 1
    specs = [pl.BlockSpec(memory_space=m) for m in spaces]
    out_specs = [pl.BlockSpec(memory_space=m) for m in out_spaces or [V] * len(out_shapes)]
    return pl.pallas_call(
        kernel,
        out_shape=out_shapes if several else out_shapes[0],
        in_specs=specs,
        out_specs=out_specs if several else out_specs[0],
        scratch_shapes=list(scratch),
        input_output_aliases=aliases or {},
        compiler_params=pltpu.CompilerParams(vmem_limit_bytes=room * 2**20),
        cost_estimate=pl.CostEstimate(
            flops=micros * 10**9, bytes_accessed=micros * 3 * 10**6, transcendentals=0
        ),
    )(*operands)


def f32(*shape):
    return jax.ShapeDtypeStruct(shape, jnp.float32)


def bf16(*shape):
    return jax.ShapeDtypeStruct(shape, jnp.bfloat16)


def paired(model, forward, warm_start, residual_data, electrodes, survey_order):
    sources, layers, ny, nz = forward.shape
    half = sources // 2
    late = (half + 3) // 4
    early = half - late
    full = 2 * layers
    devices = lax.axis_size("space")
    pairs = []
    for p in range(1, devices, 2):
        pairs += [(p, (p + 1) % devices), ((p + 1) % devices, p)]

    def swap(x, mask=None):
        links = pairs if mask is None else [(p, p ^ mask) for p in range(devices)]
        return lax.ppermute(x, "space", links)

    dma = pltpu.SemaphoreType.DMA
    slab = (layers, ny, nz)
    other = swap(model)
    first = call(pack, (warm_start,), (V,), [f32(early, *slab)])
    got_first = swap(first)
    beside = swap(other, 1)
    coefs = call(
        prepare,
        (model, other),
        (V, V),
        [f32(7, full, ny, nz)],
        scratch=[V((full, ny, nz), jnp.float32)],
    )
    rhs, weights_time = call(
        inject,
        (survey_order, residual_data, electrodes.reshape(1, -1), coefs),
        (S, V, V, V),
        [f32(half, full, ny, nz), f32(8)],
        [V, S],
    )

    def fields(count):
        field = V((count, full, ny, nz), jnp.float32)
        return [field, field, field, V((2, count, full, ny, nz), jnp.float32)]

    time, opposite, parts = call(
        split_time,
        (weights_time, model, beside),
        (S, V, V),
        [f32(*slab), f32(*slab), f32(2 * layers, ny, nz)],
    )
    near = swap(parts, 4)
    second = call(
        pack_second, (warm_start, forward, parts), (V, V, V), [f32(late * layers + half, ny, nz)]
    )
    got_second = swap(second)
    own_first, sent_first = call(
        solve_first,
        (coefs, got_first, warm_start, rhs),
        (V, V, V, V),
        [f32(early, *slab), f32(early * layers, ny, nz)],
        scratch=fields(early),
        micros=3,
    )
    back_first = swap(sent_first)
    times, joined = call(join_time, (time, opposite, near), (V, V, V), [f32(*slab), f32(*slab)], micros=1)
    far = swap(joined, 8)
    own_second, sent_second = call(
        solve_second,
        (coefs, got_second, warm_start, rhs, forward, own_first, sent_first),
        (V, V, V, V, V, V, V),
        [f32(late, *slab), f32(late * layers + 1, ny, nz)],
        scratch=fields(late),
        micros=3,
    )
    back_second = swap(sent_second)
    sums, kept, time = call(
        gather_terms,
        (forward, own_first, own_second, back_first, times, far),
        (V, V, V, V, V, V),
        [f32(4, *slab), bf16(*forward.shape), f32(*slab)],
        [V, H, V],
        scratch=[V((half + early, *slab), jnp.bfloat16), dma((2,))],
        micros=1,
    )
    adjoint, gradient = call(
        finish,
        (sums, back_second, sent_second, forward, model, other, time, kept),
        (V, V, V, V, V, V, V, H),
        [bf16(*forward.shape), f32(*slab)],
        [H, H],
        scratch=[V((late, *slab), jnp.bfloat16), V(slab, jnp.float32), dma((layers + 1,))],
        aliases={7: 0},
    )
    return adjoint, gradient


def solution(mesh):
    body = paired if mesh.shape["space"] == 2 * SURVEYS else layered
    in_specs = (
        P(("groups", "space"), None, None),
        P(None, ("groups", "space"), None, None),
        P(None, ("groups", "space"), None, None),
        P("groups", None, None),
        P("groups"),
        P("groups"),
    )
    out_specs = (P(None, ("groups", "space"), None, None), P(("groups", "space"), None, None))
    return jax.shard_map(body, mesh=mesh, in_specs=in_specs, out_specs=out_specs, check_vma=False)
```

```python
import jax
import jax.numpy as jnp
from jax import lax
from jax.experimental import pallas as pl
from jax.experimental.pallas import tpu as pltpu
from jax.sharding import PartitionSpec as P

SURVEYS = 8
ITERS = 4


GROUND = 0.5
CENTER = 1.0
HALF_WIDTH = 0.99


def padded(shard, sides, width):
    for axis, dim in sides:
        devices, length = (lax.axis_size(axis), shard.shape[dim])
        up = [(i, (i + 1) % devices) for i in range(devices)]
        down = [(j, i) for i, j in up]
        last = lax.slice_in_dim(shard, length - width, length, axis=dim)
        leading = lax.slice_in_dim(shard, 0, width, axis=dim)
        before = lax.ppermute(last, axis, up)
        after = lax.ppermute(leading, axis, down)
        shard = jnp.concatenate([before, shard, after], axis=dim)
    return shard


def swapped(value, axis, bit):
    mask = 2**bit
    pairs = [(source, source ^ mask) for source in range(lax.axis_size(axis))]
    return lax.ppermute(value, axis, pairs)


def face_diff(field, axis):
    count = field.shape[axis]
    return lax.slice_in_dim(field, 0, count - 1, axis=axis) - lax.slice_in_dim(
        field, 1, count, axis=axis
    )


def edge_zeros(field, axis):
    shape = list(field.shape)
    shape[axis] = 1
    return jnp.zeros(shape, jnp.float32)


def pad_diff(faces, axis):
    zeros = edge_zeros(faces, axis)
    return jnp.concatenate([faces, zeros], axis=axis) - jnp.concatenate([zeros, faces], axis=axis)


def pad_sum(faces, axis):
    zeros = edge_zeros(faces, axis)
    return jnp.concatenate([faces, zeros], axis=axis) + jnp.concatenate([zeros, faces], axis=axis)


def extend(field):
    return padded(field, (("space", 1),), 1)


def layered(model, forward, warm_start, residual_data, electrodes, survey_order):
    sources, layers, rows_y, rows_z = forward.shape
    position = lax.axis_index("space")
    devices = lax.axis_size("space")
    tiles = devices // SURVEYS
    half_tiles = tiles // 2
    shifted = position + half_tiles
    tile = shifted % tiles
    survey = shifted // tiles % SURVEYS
    block = position // tiles
    rotation = jnp.where(position % tiles >= half_tiles, 1, 0).astype(jnp.int32)
    valid = jnp.ones((layers + 1,), jnp.float32)
    valid = valid.at[0].set(jnp.where(tile == 0, 0.0, 1.0))
    valid = valid.at[layers].set(jnp.where(tile == tiles - 1, 0.0, 1.0))
    valid_faces = valid[:, None, None]
    model_pad = padded(model, (("space", 0),), 1)
    sigma_pad = jnp.exp(model_pad)
    sigma = sigma_pad[1:-1]
    conduct_x = 0.5 * (sigma_pad[:-1] + sigma_pad[1:]) * valid_faces
    conduct_y = 0.5 * (sigma[:, :-1] + sigma[:, 1:])
    conduct_z = 0.5 * (sigma[:, :, :-1] + sigma[:, :, 1:])
    diagonal = (
        conduct_x[1:]
        + conduct_x[:-1]
        + pad_sum(conduct_y, 1)
        + pad_sum(conduct_z, 2)
        + GROUND * sigma
    )
    inverse_diag = (1.0 / diagonal)[None]

    def operate(field_pad):
        field = field_pad[:, 1:-1]
        flux_x = conduct_x[None] * (field_pad[:, :-1] - field_pad[:, 1:])
        total = flux_x[:, 1:] - flux_x[:, :-1]
        total = total + pad_diff(conduct_y[None] * face_diff(field, 2), 2)
        total = total + pad_diff(conduct_z[None] * face_diff(field, 3), 3)
        return total + GROUND * sigma[None] * field

    cells = layers * rows_y * rows_z
    residual = lax.dynamic_index_in_dim(residual_data, survey, 0, keepdims=False)
    local_index = electrodes - tile * cells
    inside = (local_index >= 0) & (local_index < cells)
    target = jnp.where(inside, local_index, 0)
    amount = jnp.where(inside[None, :], residual, 0.0)
    rhs = jnp.zeros((sources, cells), jnp.float32).at[:, target].add(amount)
    rhs = rhs.reshape(sources, layers, rows_y, rows_z)
    iterate = warm_start.astype(jnp.float32)
    remain = rhs - operate(extend(iterate))
    direction = remain * inverse_diag / CENTER
    weight_now = HALF_WIDTH / CENTER
    for sweep_index in range(ITERS):
        iterate = iterate + direction
        if sweep_index + 1 < ITERS:
            remain = remain - operate(extend(direction))
            weight_new = 1.0 / (2.0 * CENTER / HALF_WIDTH - weight_now)
            direction = weight_new * weight_now * direction + 2.0 * weight_new / HALF_WIDTH * (
                remain * inverse_diag
            )
            weight_now = weight_new
    both = padded(
        jnp.concatenate([forward.astype(jnp.float32), iterate], axis=0), (("space", 1),), 1
    )
    forward_pad = both[:sources]
    adjoint_pad = both[sources:]
    potential = forward_pad[:, 1:-1]
    product_x = (
        jnp.sum(
            (forward_pad[:, :-1] - forward_pad[:, 1:]) * (adjoint_pad[:, :-1] - adjoint_pad[:, 1:]),
            axis=0,
        )
        * valid_faces
    )
    terms = product_x[1:] + product_x[:-1]
    terms = terms + pad_sum(jnp.sum(face_diff(potential, 2) * face_diff(iterate, 2), axis=0), 1)
    terms = terms + pad_sum(jnp.sum(face_diff(potential, 3) * face_diff(iterate, 3), axis=0), 2)
    data_term = -sigma * (0.5 * terms + GROUND * jnp.sum(potential * iterate, axis=0))
    model_x = (model_pad[:-1] - model_pad[1:]) * valid_faces
    space_term = (
        model_x[1:]
        - model_x[:-1]
        + pad_diff(face_diff(model, 1), 1)
        + pad_diff(face_diff(model, 2), 2)
    )
    base_bit = tiles.bit_length() - 1
    collected = model
    for level in range(SURVEYS.bit_length() - 1):
        partner = swapped(collected, "space", base_bit + level)
        upper = block >> level & 1 == 1
        lower_half = jnp.where(upper, partner, collected)
        upper_half = jnp.where(upper, collected, partner)
        collected = jnp.concatenate([lower_half, upper_half], axis=0)
    all_blocks = collected.reshape(SURVEYS, layers, rows_y, rows_z)
    ranks = jnp.arange(SURVEYS, dtype=jnp.int32)
    placed = (survey_order[:, None] == ranks[None, :]).astype(jnp.float32)
    apart = jnp.abs(ranks[:, None] - ranks[None, :])
    degree = jnp.where((ranks == 0) | (ranks == SURVEYS - 1), 1.0, 2.0)
    path = jnp.where(apart == 0, degree[:, None], 0.0) - jnp.where(apart == 1, 1.0, 0.0)
    coupling = jnp.dot(
        placed.T,
        jnp.dot(path, placed, precision=lax.Precision.HIGHEST),
        precision=lax.Precision.HIGHEST,
    )
    row_weights = lax.dynamic_index_in_dim(coupling, survey, 0, keepdims=False)
    block_survey = (ranks + rotation) % SURVEYS
    picker = (block_survey[:, None] == ranks[None, :]).astype(jnp.float32)
    block_weights = jnp.dot(picker, row_weights, precision=lax.Precision.HIGHEST)
    time_term = jnp.sum(block_weights[:, None, None, None] * all_blocks, axis=0)
    return (iterate.astype(jnp.bfloat16), data_term + space_term + time_term)


def weights():
    now = HALF_WIDTH / CENTER
    steps = []
    for _ in range(ITERS - 1):
        new = 1.0 / (2.0 * CENTER / HALF_WIDTH - now)
        steps.append((new * now, 2.0 * new / HALF_WIDTH))
        now = new
    return steps


def after(x, axis):
    return pltpu.roll(x, x.shape[axis] - 1, axis)


def before(x, axis):
    return pltpu.roll(x, 1, axis)


def inner(shape, axis):
    return lax.broadcasted_iota(jnp.int32, shape, axis) < shape[axis] - 1


def face_prod(field, other, axis):
    return (field - after(field, axis)) * (other - after(other, axis))


def tile_of(position):
    return (position + 1) & 1


def survey_of(position):
    return ((position + 1) >> 1) & (SURVEYS - 1)


def pack(warm, first):
    tile = tile_of(lax.axis_index("space"))
    half = warm.shape[0] // 2
    for q in range(first.shape[0]):
        first[q] = warm[half * (1 - tile) + q].astype(jnp.float32)


def pack_second(warm, forward, parts, second):
    tile = tile_of(lax.axis_index("space"))
    half, layers = warm.shape[0] // 2, warm.shape[1]
    count = (second.shape[0] - half) // layers
    theirs = half * (1 - tile)
    face = (layers - 1) * (1 - tile)
    for q in range(count):
        source = theirs + half - count + q
        second[layers * q : layers * (q + 1)] = warm[source].astype(jnp.float32)
    for q in range(half):
        second[count * layers + q] = forward[theirs + q, face].astype(jnp.float32)


def inject(order, residual, electrodes, coefs, out, weights):
    position = lax.axis_index("space")
    tile = tile_of(position)
    surveys = order.shape[0]
    ranks = []
    for place in [position, position ^ 1] + [position ^ (4 * k) for k in range(4)]:
        found = 0
        for i in range(surveys):
            found = found + jnp.where(order[i] == survey_of(place), i, 0)
        ranks.append(found)
    for k in range(4):
        a = ranks[2 + k]
        ends = jnp.where(a == 0, 1, 0) + jnp.where(a == surveys - 1, 1, 0)
        for m in range(2):
            b = ranks[m]
            value = jnp.where(a == b, 2 - ends, jnp.where(jnp.abs(a - b) == 1, -1, 0))
            weights[2 * k + m] = value.astype(jnp.float32)
    sources, _, rows_y, rows_z = out.shape
    half = residual.shape[1] // 2
    cells = out.shape[1] * rows_y * rows_z
    where_cell = lax.rem(electrodes[...] + tile * (cells // 2), cells)
    row = where_cell // rows_z
    lane = lax.rem(where_cell, rows_z)
    count = row.shape[1]
    rows = cells // rows_z
    at_row = lax.broadcasted_iota(jnp.int32, (rows, count), 0) == row
    at_row = jnp.where(at_row, 1.0, 0.0).astype(jnp.bfloat16)
    at_lane = lax.broadcasted_iota(jnp.int32, (rows_z, count), 0) == lane
    mine = residual[survey_of(position)]
    mine = jnp.where(tile == 0, mine[:half], mine[half:])
    total = None
    for _ in range(3):
        part = mine.astype(jnp.bfloat16).astype(jnp.float32)
        mine = mine - part
        right = jnp.concatenate(
            [jnp.where(at_lane, part[q : q + 1], 0.0) for q in range(sources)], axis=0
        ).astype(jnp.bfloat16)
        term = lax.dot_general(
            at_row, right, (((1,), (1,)), ((), ())), preferred_element_type=jnp.float32
        )
        total = term if total is None else total + term
    for q in range(sources):
        out[q] = coefs[6] * total[:, q * rows_z : (q + 1) * rows_z].reshape(out.shape[1:])


def prepare(model, other, coefs, sigma):
    tile = tile_of(lax.axis_index("space"))
    layers = model.shape[0]
    full = 2 * layers
    shape = model.shape[1:]
    for i in range(layers):
        sigma[i] = jnp.exp(model[i])
        sigma[layers + i] = jnp.exp(other[i])
    in_y, in_z = inner(shape, 0), inner(shape, 1)
    middle = jnp.where(tile == 0, 1.0, 0.0)
    for i in range(full):
        mine = sigma[i]
        up = 0.5 * (mine + sigma[(i + 1) % full])
        down = 0.5 * (mine + sigma[(i - 1) % full])
        if i == layers - 1:
            up = up * middle
        if i == full - 1:
            up = up * (1.0 - middle)
        if i == layers:
            down = down * middle
        if i == 0:
            down = down * (1.0 - middle)
        right_y = jnp.where(in_y, 0.5 * (mine + after(mine, 0)), 0.0)
        right_z = jnp.where(in_z, 0.5 * (mine + after(mine, 1)), 0.0)
        left_y = before(right_y, 0)
        left_z = before(right_z, 1)
        scale = 1.0 / (up + down + right_y + left_y + right_z + left_z + GROUND * mine)
        for k, face in enumerate((up, down, right_y, left_y, right_z, left_z)):
            coefs[k, i] = face * scale
        coefs[6, i] = scale


def sweeps(coefs, rhs, base, start, rest, lam, mine):
    count, full = start.shape[:2]

    def around(field, q, i, weight):
        here = field[q, i]
        total = weight[0] * field[q, (i + 1) % full] + weight[1] * field[q, (i + full - 1) % full]
        total = total + (weight[2] * after(here, 0) + weight[3] * before(here, 0))
        total = total + (weight[4] * after(here, 1) + weight[5] * before(here, 1))
        return here, total

    def first(i, carry):
        weight = [coefs[k, i] for k in range(6)]
        for q in range(count):
            here, total = around(start, q, i, weight)
            step = rhs[base + q, i] - here + total
            mine[0, q, i] = step
            lam[q, i] = here + step
        return carry

    lax.fori_loop(0, full, first, 0, unroll=full)
    for index, (keep, gain) in enumerate(weights()):
        source, target = mine.at[index % 2], mine.at[1 - index % 2]
        last = index == ITERS - 2

        def later(i, carry):
            weight = [coefs[k, i] for k in range(6)]
            for q in range(count):
                here, total = around(source, q, i, weight)
                if index > 0:
                    total = rest[q, i] - here + total
                step = keep * here + gain * total
                if not last:
                    rest[q, i] = total
                    target[q, i] = step
                lam[q, i] = lam[q, i] + step
            return carry

        lax.fori_loop(0, full, later, 0, unroll=full)


def load_start(warm, source, got, start):
    count, full = start.shape[:2]
    layers = full // 2
    for q in range(count):
        start[q, :layers] = warm[source + q].astype(jnp.float32)
        start[q, layers:] = got[q] if len(got.shape) == 4 else got[layers * q : layers * (q + 1)]


def split_time(weights, model, beside, time, opposite, parts):
    layers = model.shape[0]
    here, there = model[...], beside[...]
    time[...] = weights[0] * here + weights[1] * there
    parts[:layers] = weights[2] * here + weights[3] * there
    opposite[...] = weights[4] * here + weights[5] * there
    parts[layers:] = weights[6] * here + weights[7] * there


def join_time(time, opposite, near, times, joined):
    layers = time.shape[0]
    times[...] = time[...] + near[:layers]
    joined[...] = opposite[...] + near[layers:]


def solve_first(coefs, got, warm, rhs, own, sent, start, rest, lam, mine):
    count, layers = own.shape[:2]
    half = warm.shape[0] // 2
    load_start(warm, half * tile_of(lax.axis_index("space")), got, start)
    sweeps(coefs, rhs, 0, start, rest, lam, mine)
    for q in range(count):
        own[q] = lam[q, :layers]
        sent[layers * q : layers * (q + 1)] = lam[q, layers:]


def solve_second(coefs, got, warm, rhs, forward, own_first, sent_first, own, sent, start, rest, lam, mine):
    count, layers = own.shape[:2]
    tile = tile_of(lax.axis_index("space"))
    half = warm.shape[0] // 2
    early, source = half - count, half * tile
    load_start(warm, source + early, got, start)
    sweeps(coefs, rhs, early, start, rest, lam, mine)
    near = (layers - 1) * (1 - tile)
    far = (layers - 1) * tile
    total = None
    for q in range(half):
        slope = forward[source + q, near].astype(jnp.float32) - got[count * layers + q]
        if q < early:
            drop = own_first[q, near] - sent_first[layers * q + far]
        else:
            drop = lam[q - early, near] - lam[q - early, layers + far]
        total = slope * drop if total is None else total + slope * drop
    for q in range(count):
        own[q] = lam[q, :layers]
        sent[layers * q : layers * (q + 1)] = lam[q, layers:]
    sent[count * layers] = total


def data_sums(pairs, layers, along_x, along_y, along_z, mass):
    def add(ref, i, value, first):
        ref[i] = value if first else ref[i] + value

    for i in range(layers):
        totals = [None] * 4
        for forward, lam in pairs:
            here, other = forward(i), lam(i)
            terms = [None, face_prod(here, other, 0), face_prod(here, other, 1), here * other]
            if i + 1 < layers:
                terms[0] = (here - forward(i + 1)) * (other - lam(i + 1))
            totals = [t if a is None else (a if t is None else a + t) for a, t in zip(totals, terms)]
        if i + 1 < layers:
            along_x[i] = along_x[i] + totals[0]
        along_y[i] = along_y[i] + totals[1]
        along_z[i] = along_z[i] + totals[2]
        mass[i] = mass[i] + totals[3]


def gather_terms(forward, own_first, own_second, sums, adjoint, rounded, sem):
    early, layers = own_first.shape[:2]
    half = rounded.shape[0]
    mine = half * tile_of(lax.axis_index("space"))
    rounded[:early] = own_first[...].astype(jnp.bfloat16)
    rounded[early:] = own_second[...].astype(jnp.bfloat16)
    copy = pltpu.make_async_copy(rounded, adjoint.at[pl.ds(mine, half)], sem)
    copy.start()
    sums[...] = jnp.zeros(sums.shape, jnp.float32)
    pairs = []
    for q in range(half):
        own, at = (own_first, q) if q < early else (own_second, q - early)
        pairs.append((
            lambda i, q=q: forward[mine + q, i].astype(jnp.float32),
            lambda i, own=own, at=at: own[at, i],
        ))
    data_sums(pairs, layers, sums.at[0], sums.at[1], sums.at[2], sums.at[3])
    copy.wait()


def finish(sums, back_first, back, sent, forward, model, other, times, far, kept, adjoint, gradient, rounded, result, sems):
    tile = tile_of(lax.axis_index("space"))
    half = rounded.shape[0]
    shape = model.shape[1:]
    layers = model.shape[0]
    early = back_first.shape[0] // layers
    count = half - early
    theirs = half * (1 - tile)
    rows = [(back_first, q) for q in range(early)] + [(back, q) for q in range(count)]
    for q, (source, at) in enumerate(rows):
        rounded[q] = source[layers * at : layers * (at + 1)].astype(jnp.bfloat16)
    copies = [pltpu.make_async_copy(rounded, adjoint.at[pl.ds(theirs, half)], sems.at[layers])]
    copies[0].start()
    pairs = []
    for q, (source, at) in enumerate(rows):
        pairs.append((
            lambda i, q=q: forward[theirs + q, i].astype(jnp.float32),
            lambda i, source=source, at=at: source[layers * at + i],
        ))
    in_y, in_z = inner(shape, 0), inner(shape, 1)
    low = jnp.where(tile == 0, 0.0, 1.0)
    high = 1.0 - low
    cross = back[count * layers] + sent[count * layers]
    bridge = other[(layers - 1) * tile]
    products, falls = [low * cross], [low * (bridge - model[0])]
    for i in range(layers):
        if i + 1 < layers:
            total = sums[0, i]
            for f, l in pairs:
                total = total + (f(i) - f(i + 1)) * (l(i) - l(i + 1))
            products.append(total)
            falls.append(model[i] - model[i + 1])
        else:
            products.append(high * cross)
            falls.append(high * (model[i] - bridge))
    for i in range(layers):
        total_y, total_z, mass = sums[1, i], sums[2, i], sums[3, i]
        for f, l in pairs:
            here, there = f(i), l(i)
            total_y = total_y + face_prod(here, there, 0)
            total_z = total_z + face_prod(here, there, 1)
            mass = mass + here * there
        total_y = jnp.where(in_y, total_y, 0.0)
        total_z = jnp.where(in_z, total_z, 0.0)
        terms = products[i] + products[i + 1]
        terms = terms + (total_y + before(total_y, 0)) + (total_z + before(total_z, 1))
        value = model[i]
        fall_y = jnp.where(in_y, value - after(value, 0), 0.0)
        fall_z = jnp.where(in_z, value - after(value, 1), 0.0)
        space = falls[i + 1] - falls[i] + (fall_y - before(fall_y, 0)) + (fall_z - before(fall_z, 1))
        result[i] = space + (times[i] + far[i]) - jnp.exp(value) * (0.5 * terms + GROUND * mass)
        copies.append(pltpu.make_async_copy(result.at[i], gradient.at[i], sems.at[i]))
        copies[-1].start()
    for copy in copies:
        copy.wait()


V, S, H = pltpu.VMEM, pltpu.SMEM, pltpu.HBM


def call(kernel, operands, spaces, out_shapes, out_spaces=None, scratch=(), aliases=None, micros=1, room=16):
    several = len(out_shapes) > 1
    specs = [pl.BlockSpec(memory_space=m) for m in spaces]
    out_specs = [pl.BlockSpec(memory_space=m) for m in out_spaces or [V] * len(out_shapes)]
    return pl.pallas_call(
        kernel,
        out_shape=out_shapes if several else out_shapes[0],
        in_specs=specs,
        out_specs=out_specs if several else out_specs[0],
        scratch_shapes=list(scratch),
        input_output_aliases=aliases or {},
        compiler_params=pltpu.CompilerParams(vmem_limit_bytes=room * 2**20),
        cost_estimate=pl.CostEstimate(
            flops=micros * 10**9, bytes_accessed=micros * 3 * 10**6, transcendentals=0
        ),
    )(*operands)


def f32(*shape):
    return jax.ShapeDtypeStruct(shape, jnp.float32)


def bf16(*shape):
    return jax.ShapeDtypeStruct(shape, jnp.bfloat16)


def paired(model, forward, warm_start, residual_data, electrodes, survey_order):
    sources, layers, ny, nz = forward.shape
    half = sources // 2
    late = (half + 3) // 4
    early = half - late
    full = 2 * layers
    devices = lax.axis_size("space")
    pairs = []
    for p in range(1, devices, 2):
        pairs += [(p, (p + 1) % devices), ((p + 1) % devices, p)]

    def swap(x, mask=None):
        links = pairs if mask is None else [(p, p ^ mask) for p in range(devices)]
        return lax.ppermute(x, "space", links)

    dma = pltpu.SemaphoreType.DMA
    slab = (layers, ny, nz)
    other = swap(model)
    first = call(pack, (warm_start,), (V,), [f32(early, *slab)])
    got_first = swap(first)
    beside = swap(other, 1)
    coefs = call(
        prepare,
        (model, other),
        (V, V),
        [f32(7, full, ny, nz)],
        scratch=[V((full, ny, nz), jnp.float32)],
    )
    rhs, weights_time = call(
        inject,
        (survey_order, residual_data, electrodes.reshape(1, -1), coefs),
        (S, V, V, V),
        [f32(half, full, ny, nz), f32(8)],
        [V, S],
    )

    def fields(count):
        field = V((count, full, ny, nz), jnp.float32)
        return [field, field, field, V((2, count, full, ny, nz), jnp.float32)]

    time, opposite, parts = call(
        split_time,
        (weights_time, model, beside),
        (S, V, V),
        [f32(*slab), f32(*slab), f32(2 * layers, ny, nz)],
    )
    near = swap(parts, 4)
    second = call(
        pack_second, (warm_start, forward, parts), (V, V, V), [f32(late * layers + half, ny, nz)]
    )
    got_second = swap(second)
    own_first, sent_first = call(
        solve_first,
        (coefs, got_first, warm_start, rhs),
        (V, V, V, V),
        [f32(early, *slab), f32(early * layers, ny, nz)],
        scratch=fields(early),
        micros=3,
    )
    back_first = swap(sent_first)
    times, joined = call(join_time, (time, opposite, near), (V, V, V), [f32(*slab), f32(*slab)], micros=1)
    far = swap(joined, 8)
    own_second, sent_second = call(
        solve_second,
        (coefs, got_second, warm_start, rhs, forward, own_first, sent_first),
        (V, V, V, V, V, V, V),
        [f32(late, *slab), f32(late * layers + 1, ny, nz)],
        scratch=fields(late),
        micros=3,
    )
    back_second = swap(sent_second)
    sums, kept = call(
        gather_terms,
        (forward, own_first, own_second),
        (V, V, V),
        [f32(4, *slab), bf16(*forward.shape)],
        [V, H],
        scratch=[V((half, *slab), jnp.bfloat16), dma],
        micros=3,
    )
    adjoint, gradient = call(
        finish,
        (sums, back_first, back_second, sent_second, forward, model, other, times, far, kept),
        (V, V, V, V, V, V, V, V, V, H),
        [bf16(*forward.shape), f32(*slab)],
        [H, H],
        scratch=[V((half, *slab), jnp.bfloat16), V(slab, jnp.float32), dma((layers + 1,))],
        aliases={9: 0},
        micros=1,
    )
    return adjoint, gradient


def solution(mesh):
    body = paired if mesh.shape["space"] == 2 * SURVEYS else layered
    in_specs = (
        P(("groups", "space"), None, None),
        P(None, ("groups", "space"), None, None),
        P(None, ("groups", "space"), None, None),
        P("groups", None, None),
        P("groups"),
        P("groups"),
    )
    out_specs = (P(None, ("groups", "space"), None, None), P(("groups", "space"), None, None))
    return jax.shard_map(body, mesh=mesh, in_specs=in_specs, out_specs=out_specs, check_vma=False)
```

```python
import jax
import jax.numpy as jnp
from jax import lax
from jax.experimental import pallas as pl
from jax.experimental.pallas import tpu as pltpu
from jax.sharding import PartitionSpec as P

SURVEYS = 8
ITERS = 4


GROUND = 0.5
CENTER = 1.0
HALF_WIDTH = 0.99


def padded(shard, sides, width):
    for axis, dim in sides:
        devices, length = (lax.axis_size(axis), shard.shape[dim])
        up = [(i, (i + 1) % devices) for i in range(devices)]
        down = [(j, i) for i, j in up]
        last = lax.slice_in_dim(shard, length - width, length, axis=dim)
        leading = lax.slice_in_dim(shard, 0, width, axis=dim)
        before = lax.ppermute(last, axis, up)
        after = lax.ppermute(leading, axis, down)
        shard = jnp.concatenate([before, shard, after], axis=dim)
    return shard


def swapped(value, axis, bit):
    mask = 2**bit
    pairs = [(source, source ^ mask) for source in range(lax.axis_size(axis))]
    return lax.ppermute(value, axis, pairs)


def face_diff(field, axis):
    count = field.shape[axis]
    return lax.slice_in_dim(field, 0, count - 1, axis=axis) - lax.slice_in_dim(
        field, 1, count, axis=axis
    )


def edge_zeros(field, axis):
    shape = list(field.shape)
    shape[axis] = 1
    return jnp.zeros(shape, jnp.float32)


def pad_diff(faces, axis):
    zeros = edge_zeros(faces, axis)
    return jnp.concatenate([faces, zeros], axis=axis) - jnp.concatenate([zeros, faces], axis=axis)


def pad_sum(faces, axis):
    zeros = edge_zeros(faces, axis)
    return jnp.concatenate([faces, zeros], axis=axis) + jnp.concatenate([zeros, faces], axis=axis)


def extend(field):
    return padded(field, (("space", 1),), 1)


def layered(model, forward, warm_start, residual_data, electrodes, survey_order):
    sources, layers, rows_y, rows_z = forward.shape
    position = lax.axis_index("space")
    devices = lax.axis_size("space")
    tiles = devices // SURVEYS
    half_tiles = tiles // 2
    shifted = position + half_tiles
    tile = shifted % tiles
    survey = shifted // tiles % SURVEYS
    block = position // tiles
    rotation = jnp.where(position % tiles >= half_tiles, 1, 0).astype(jnp.int32)
    valid = jnp.ones((layers + 1,), jnp.float32)
    valid = valid.at[0].set(jnp.where(tile == 0, 0.0, 1.0))
    valid = valid.at[layers].set(jnp.where(tile == tiles - 1, 0.0, 1.0))
    valid_faces = valid[:, None, None]
    model_pad = padded(model, (("space", 0),), 1)
    sigma_pad = jnp.exp(model_pad)
    sigma = sigma_pad[1:-1]
    conduct_x = 0.5 * (sigma_pad[:-1] + sigma_pad[1:]) * valid_faces
    conduct_y = 0.5 * (sigma[:, :-1] + sigma[:, 1:])
    conduct_z = 0.5 * (sigma[:, :, :-1] + sigma[:, :, 1:])
    diagonal = (
        conduct_x[1:]
        + conduct_x[:-1]
        + pad_sum(conduct_y, 1)
        + pad_sum(conduct_z, 2)
        + GROUND * sigma
    )
    inverse_diag = (1.0 / diagonal)[None]

    def operate(field_pad):
        field = field_pad[:, 1:-1]
        flux_x = conduct_x[None] * (field_pad[:, :-1] - field_pad[:, 1:])
        total = flux_x[:, 1:] - flux_x[:, :-1]
        total = total + pad_diff(conduct_y[None] * face_diff(field, 2), 2)
        total = total + pad_diff(conduct_z[None] * face_diff(field, 3), 3)
        return total + GROUND * sigma[None] * field

    cells = layers * rows_y * rows_z
    residual = lax.dynamic_index_in_dim(residual_data, survey, 0, keepdims=False)
    local_index = electrodes - tile * cells
    inside = (local_index >= 0) & (local_index < cells)
    target = jnp.where(inside, local_index, 0)
    amount = jnp.where(inside[None, :], residual, 0.0)
    rhs = jnp.zeros((sources, cells), jnp.float32).at[:, target].add(amount)
    rhs = rhs.reshape(sources, layers, rows_y, rows_z)
    iterate = warm_start.astype(jnp.float32)
    remain = rhs - operate(extend(iterate))
    direction = remain * inverse_diag / CENTER
    weight_now = HALF_WIDTH / CENTER
    for sweep_index in range(ITERS):
        iterate = iterate + direction
        if sweep_index + 1 < ITERS:
            remain = remain - operate(extend(direction))
            weight_new = 1.0 / (2.0 * CENTER / HALF_WIDTH - weight_now)
            direction = weight_new * weight_now * direction + 2.0 * weight_new / HALF_WIDTH * (
                remain * inverse_diag
            )
            weight_now = weight_new
    both = padded(
        jnp.concatenate([forward.astype(jnp.float32), iterate], axis=0), (("space", 1),), 1
    )
    forward_pad = both[:sources]
    adjoint_pad = both[sources:]
    potential = forward_pad[:, 1:-1]
    product_x = (
        jnp.sum(
            (forward_pad[:, :-1] - forward_pad[:, 1:]) * (adjoint_pad[:, :-1] - adjoint_pad[:, 1:]),
            axis=0,
        )
        * valid_faces
    )
    terms = product_x[1:] + product_x[:-1]
    terms = terms + pad_sum(jnp.sum(face_diff(potential, 2) * face_diff(iterate, 2), axis=0), 1)
    terms = terms + pad_sum(jnp.sum(face_diff(potential, 3) * face_diff(iterate, 3), axis=0), 2)
    data_term = -sigma * (0.5 * terms + GROUND * jnp.sum(potential * iterate, axis=0))
    model_x = (model_pad[:-1] - model_pad[1:]) * valid_faces
    space_term = (
        model_x[1:]
        - model_x[:-1]
        + pad_diff(face_diff(model, 1), 1)
        + pad_diff(face_diff(model, 2), 2)
    )
    base_bit = tiles.bit_length() - 1
    collected = model
    for level in range(SURVEYS.bit_length() - 1):
        partner = swapped(collected, "space", base_bit + level)
        upper = block >> level & 1 == 1
        lower_half = jnp.where(upper, partner, collected)
        upper_half = jnp.where(upper, collected, partner)
        collected = jnp.concatenate([lower_half, upper_half], axis=0)
    all_blocks = collected.reshape(SURVEYS, layers, rows_y, rows_z)
    ranks = jnp.arange(SURVEYS, dtype=jnp.int32)
    placed = (survey_order[:, None] == ranks[None, :]).astype(jnp.float32)
    apart = jnp.abs(ranks[:, None] - ranks[None, :])
    degree = jnp.where((ranks == 0) | (ranks == SURVEYS - 1), 1.0, 2.0)
    path = jnp.where(apart == 0, degree[:, None], 0.0) - jnp.where(apart == 1, 1.0, 0.0)
    coupling = jnp.dot(
        placed.T,
        jnp.dot(path, placed, precision=lax.Precision.HIGHEST),
        precision=lax.Precision.HIGHEST,
    )
    row_weights = lax.dynamic_index_in_dim(coupling, survey, 0, keepdims=False)
    block_survey = (ranks + rotation) % SURVEYS
    picker = (block_survey[:, None] == ranks[None, :]).astype(jnp.float32)
    block_weights = jnp.dot(picker, row_weights, precision=lax.Precision.HIGHEST)
    time_term = jnp.sum(block_weights[:, None, None, None] * all_blocks, axis=0)
    return (iterate.astype(jnp.bfloat16), data_term + space_term + time_term)


def weights():
    now = HALF_WIDTH / CENTER
    steps = []
    for _ in range(ITERS - 1):
        new = 1.0 / (2.0 * CENTER / HALF_WIDTH - now)
        steps.append((new * now, 2.0 * new / HALF_WIDTH))
        now = new
    return steps


def after(x, axis):
    return pltpu.roll(x, x.shape[axis] - 1, axis)


def before(x, axis):
    return pltpu.roll(x, 1, axis)


def inner(shape, axis):
    return lax.broadcasted_iota(jnp.int32, shape, axis) < shape[axis] - 1


def face_prod(field, other, axis):
    return (field - after(field, axis)) * (other - after(other, axis))


def tile_of(position):
    return (position + 1) & 1


def survey_of(position):
    return ((position + 1) >> 1) & (SURVEYS - 1)


def pack(warm, first):
    tile = tile_of(lax.axis_index("space"))
    half = warm.shape[0] // 2
    for q in range(first.shape[0]):
        first[q] = warm[half * (1 - tile) + q].astype(jnp.float32)


def pack_second(warm, forward, parts, second):
    tile = tile_of(lax.axis_index("space"))
    half, layers = warm.shape[0] // 2, warm.shape[1]
    count = (second.shape[0] - half) // layers
    theirs = half * (1 - tile)
    face = (layers - 1) * (1 - tile)
    for q in range(count):
        source = theirs + half - count + q
        second[layers * q : layers * (q + 1)] = warm[source].astype(jnp.float32)
    for q in range(half):
        second[count * layers + q] = forward[theirs + q, face].astype(jnp.float32)


def inject(order, residual, electrodes, coefs, out, weights):
    position = lax.axis_index("space")
    tile = tile_of(position)
    surveys = order.shape[0]
    ranks = []
    for place in [position, position ^ 1] + [position ^ (4 * k) for k in range(4)]:
        found = 0
        for i in range(surveys):
            found = found + jnp.where(order[i] == survey_of(place), i, 0)
        ranks.append(found)
    for k in range(4):
        a = ranks[2 + k]
        ends = jnp.where(a == 0, 1, 0) + jnp.where(a == surveys - 1, 1, 0)
        for m in range(2):
            b = ranks[m]
            value = jnp.where(a == b, 2 - ends, jnp.where(jnp.abs(a - b) == 1, -1, 0))
            weights[2 * k + m] = value.astype(jnp.float32)
    sources, _, rows_y, rows_z = out.shape
    half = residual.shape[1] // 2
    cells = out.shape[1] * rows_y * rows_z
    where_cell = lax.rem(electrodes[...] + tile * (cells // 2), cells)
    row = where_cell // rows_z
    lane = lax.rem(where_cell, rows_z)
    count = row.shape[1]
    rows = cells // rows_z
    at_row = lax.broadcasted_iota(jnp.int32, (rows, count), 0) == row
    at_row = jnp.where(at_row, 1.0, 0.0).astype(jnp.bfloat16)
    at_lane = lax.broadcasted_iota(jnp.int32, (rows_z, count), 0) == lane
    mine = residual[survey_of(position)]
    mine = jnp.where(tile == 0, mine[:half], mine[half:])
    total = None
    for _ in range(3):
        part = mine.astype(jnp.bfloat16).astype(jnp.float32)
        mine = mine - part
        right = jnp.concatenate(
            [jnp.where(at_lane, part[q : q + 1], 0.0) for q in range(sources)], axis=0
        ).astype(jnp.bfloat16)
        term = lax.dot_general(
            at_row, right, (((1,), (1,)), ((), ())), preferred_element_type=jnp.float32
        )
        total = term if total is None else total + term
    for q in range(sources):
        out[q] = coefs[6] * total[:, q * rows_z : (q + 1) * rows_z].reshape(out.shape[1:])


def prepare(model, other, coefs, sigma):
    tile = tile_of(lax.axis_index("space"))
    layers = model.shape[0]
    full = 2 * layers
    shape = model.shape[1:]
    for i in range(layers):
        sigma[i] = jnp.exp(model[i])
        sigma[layers + i] = jnp.exp(other[i])
    in_y, in_z = inner(shape, 0), inner(shape, 1)
    middle = jnp.where(tile == 0, 1.0, 0.0)
    for i in range(full):
        mine = sigma[i]
        up = 0.5 * (mine + sigma[(i + 1) % full])
        down = 0.5 * (mine + sigma[(i - 1) % full])
        if i == layers - 1:
            up = up * middle
        if i == full - 1:
            up = up * (1.0 - middle)
        if i == layers:
            down = down * middle
        if i == 0:
            down = down * (1.0 - middle)
        right_y = jnp.where(in_y, 0.5 * (mine + after(mine, 0)), 0.0)
        right_z = jnp.where(in_z, 0.5 * (mine + after(mine, 1)), 0.0)
        left_y = before(right_y, 0)
        left_z = before(right_z, 1)
        scale = 1.0 / (up + down + right_y + left_y + right_z + left_z + GROUND * mine)
        for k, face in enumerate((up, down, right_y, left_y, right_z, left_z)):
            coefs[k, i] = face * scale
        coefs[6, i] = scale


def sweeps(coefs, rhs, base, start, rest, lam, mine):
    count, full = start.shape[:2]

    def around(field, q, i, weight):
        here = field[q, i]
        total = weight[0] * field[q, (i + 1) % full] + weight[1] * field[q, (i + full - 1) % full]
        total = total + (weight[2] * after(here, 0) + weight[3] * before(here, 0))
        total = total + (weight[4] * after(here, 1) + weight[5] * before(here, 1))
        return here, total

    def first(i, carry):
        weight = [coefs[k, i] for k in range(6)]
        for q in range(count):
            here, total = around(start, q, i, weight)
            step = rhs[base + q, i] - here + total
            mine[0, q, i] = step
            lam[q, i] = here + step
        return carry

    lax.fori_loop(0, full, first, 0, unroll=full)
    for index, (keep, gain) in enumerate(weights()):
        source, target = mine.at[index % 2], mine.at[1 - index % 2]
        last = index == ITERS - 2

        def later(i, carry):
            weight = [coefs[k, i] for k in range(6)]
            for q in range(count):
                here, total = around(source, q, i, weight)
                if index > 0:
                    total = rest[q, i] - here + total
                step = keep * here + gain * total
                if not last:
                    rest[q, i] = total
                    target[q, i] = step
                lam[q, i] = lam[q, i] + step
            return carry

        lax.fori_loop(0, full, later, 0, unroll=full)


def load_start(warm, source, got, start):
    count, full = start.shape[:2]
    layers = full // 2
    for q in range(count):
        start[q, :layers] = warm[source + q].astype(jnp.float32)
        start[q, layers:] = got[q] if len(got.shape) == 4 else got[layers * q : layers * (q + 1)]


def split_time(weights, model, beside, time, opposite, parts):
    layers = model.shape[0]
    here, there = model[...], beside[...]
    time[...] = weights[0] * here + weights[1] * there
    parts[:layers] = weights[2] * here + weights[3] * there
    opposite[...] = weights[4] * here + weights[5] * there
    parts[layers:] = weights[6] * here + weights[7] * there


def join_time(time, opposite, near, times, joined):
    layers = time.shape[0]
    times[...] = time[...] + near[:layers]
    joined[...] = opposite[...] + near[layers:]


def solve_first(coefs, got, warm, rhs, own, sent, start, rest, lam, mine):
    count, layers = own.shape[:2]
    half = warm.shape[0] // 2
    load_start(warm, half * tile_of(lax.axis_index("space")), got, start)
    sweeps(coefs, rhs, 0, start, rest, lam, mine)
    for q in range(count):
        own[q] = lam[q, :layers]
        sent[layers * q : layers * (q + 1)] = lam[q, layers:]


def solve_second(coefs, got, warm, rhs, forward, own_first, sent_first, own, sent, start, rest, lam, mine):
    count, layers = own.shape[:2]
    tile = tile_of(lax.axis_index("space"))
    half = warm.shape[0] // 2
    early, source = half - count, half * tile
    load_start(warm, source + early, got, start)
    sweeps(coefs, rhs, early, start, rest, lam, mine)
    near = (layers - 1) * (1 - tile)
    far = (layers - 1) * tile
    total = None
    for q in range(half):
        slope = forward[source + q, near].astype(jnp.float32) - got[count * layers + q]
        if q < early:
            drop = own_first[q, near] - sent_first[layers * q + far]
        else:
            drop = lam[q - early, near] - lam[q - early, layers + far]
        total = slope * drop if total is None else total + slope * drop
    for q in range(count):
        own[q] = lam[q, :layers]
        sent[layers * q : layers * (q + 1)] = lam[q, layers:]
    sent[count * layers] = total


def data_sums(pairs, layers, along_x, along_y, along_z, mass):
    def add(ref, i, value, first):
        ref[i] = value if first else ref[i] + value

    for i in range(layers):
        totals = [None] * 4
        for forward, lam in pairs:
            here, other = forward(i), lam(i)
            terms = [None, face_prod(here, other, 0), face_prod(here, other, 1), here * other]
            if i + 1 < layers:
                terms[0] = (here - forward(i + 1)) * (other - lam(i + 1))
            totals = [t if a is None else (a if t is None else a + t) for a, t in zip(totals, terms)]
        if i + 1 < layers:
            along_x[i] = along_x[i] + totals[0]
        along_y[i] = along_y[i] + totals[1]
        along_z[i] = along_z[i] + totals[2]
        mass[i] = mass[i] + totals[3]


def gather_terms(forward, own_first, own_second, sums, adjoint, rounded, sem):
    early, layers = own_first.shape[:2]
    half = rounded.shape[0]
    mine = half * tile_of(lax.axis_index("space"))
    rounded[:early] = own_first[...].astype(jnp.bfloat16)
    rounded[early:] = own_second[...].astype(jnp.bfloat16)
    copy = pltpu.make_async_copy(rounded, adjoint.at[pl.ds(mine, half)], sem)
    copy.start()
    sums[...] = jnp.zeros(sums.shape, jnp.float32)
    pairs = []
    for q in range(half):
        own, at = (own_first, q) if q < early else (own_second, q - early)
        pairs.append((
            lambda i, q=q: forward[mine + q, i].astype(jnp.float32),
            lambda i, own=own, at=at: own[at, i],
        ))
    data_sums(pairs, layers, sums.at[0], sums.at[1], sums.at[2], sums.at[3])
    copy.wait()


def gather_back(sums, back, forward, kept, added, adjoint, rounded, sem):
    early, layers = rounded.shape[:2]
    theirs = forward.shape[0] // 2 * (1 - tile_of(lax.axis_index("space")))
    for q in range(early):
        rounded[q] = back[layers * q : layers * (q + 1)].astype(jnp.bfloat16)
    copy = pltpu.make_async_copy(rounded, adjoint.at[pl.ds(theirs, early)], sem)
    copy.start()
    added[...] = sums[...]
    pairs = []
    for q in range(early):
        pairs.append((
            lambda i, q=q: forward[theirs + q, i].astype(jnp.float32),
            lambda i, q=q: back[layers * q + i],
        ))
    data_sums(pairs, layers, added.at[0], added.at[1], added.at[2], added.at[3])
    copy.wait()


def finish(sums, back, sent, forward, model, other, times, far, kept, adjoint, gradient, rounded, result, sems):
    tile = tile_of(lax.axis_index("space"))
    shape = model.shape[1:]
    count, layers = rounded.shape[:2]
    half = forward.shape[0] // 2
    theirs = half * (1 - tile) + half - count
    for q in range(count):
        rounded[q] = back[layers * q : layers * (q + 1)].astype(jnp.bfloat16)
    copies = [pltpu.make_async_copy(rounded, adjoint.at[pl.ds(theirs, count)], sems.at[layers])]
    copies[0].start()
    pairs = []
    for q in range(count):
        pairs.append((
            lambda i, q=q: forward[theirs + q, i].astype(jnp.float32),
            lambda i, q=q: back[layers * q + i],
        ))
    in_y, in_z = inner(shape, 0), inner(shape, 1)
    low = jnp.where(tile == 0, 0.0, 1.0)
    high = 1.0 - low
    cross = back[count * layers] + sent[count * layers]
    bridge = other[(layers - 1) * tile]
    products, falls = [low * cross], [low * (bridge - model[0])]
    for i in range(layers):
        if i + 1 < layers:
            total = sums[0, i]
            for f, l in pairs:
                total = total + (f(i) - f(i + 1)) * (l(i) - l(i + 1))
            products.append(total)
            falls.append(model[i] - model[i + 1])
        else:
            products.append(high * cross)
            falls.append(high * (model[i] - bridge))
    for i in range(layers):
        total_y, total_z, mass = sums[1, i], sums[2, i], sums[3, i]
        for f, l in pairs:
            here, there = f(i), l(i)
            total_y = total_y + face_prod(here, there, 0)
            total_z = total_z + face_prod(here, there, 1)
            mass = mass + here * there
        total_y = jnp.where(in_y, total_y, 0.0)
        total_z = jnp.where(in_z, total_z, 0.0)
        terms = products[i] + products[i + 1]
        terms = terms + (total_y + before(total_y, 0)) + (total_z + before(total_z, 1))
        value = model[i]
        fall_y = jnp.where(in_y, value - after(value, 0), 0.0)
        fall_z = jnp.where(in_z, value - after(value, 1), 0.0)
        space = falls[i + 1] - falls[i] + (fall_y - before(fall_y, 0)) + (fall_z - before(fall_z, 1))
        result[i] = space + (times[i] + far[i]) - jnp.exp(value) * (0.5 * terms + GROUND * mass)
        copies.append(pltpu.make_async_copy(result.at[i], gradient.at[i], sems.at[i]))
        copies[-1].start()
    for copy in copies:
        copy.wait()


V, S, H = pltpu.VMEM, pltpu.SMEM, pltpu.HBM


def call(kernel, operands, spaces, out_shapes, out_spaces=None, scratch=(), aliases=None, micros=1, room=16):
    several = len(out_shapes) > 1
    specs = [pl.BlockSpec(memory_space=m) for m in spaces]
    out_specs = [pl.BlockSpec(memory_space=m) for m in out_spaces or [V] * len(out_shapes)]
    return pl.pallas_call(
        kernel,
        out_shape=out_shapes if several else out_shapes[0],
        in_specs=specs,
        out_specs=out_specs if several else out_specs[0],
        scratch_shapes=list(scratch),
        input_output_aliases=aliases or {},
        compiler_params=pltpu.CompilerParams(vmem_limit_bytes=room * 2**20),
        cost_estimate=pl.CostEstimate(
            flops=micros * 10**9, bytes_accessed=micros * 3 * 10**6, transcendentals=0
        ),
    )(*operands)


def f32(*shape):
    return jax.ShapeDtypeStruct(shape, jnp.float32)


def bf16(*shape):
    return jax.ShapeDtypeStruct(shape, jnp.bfloat16)


def paired(model, forward, warm_start, residual_data, electrodes, survey_order):
    sources, layers, ny, nz = forward.shape
    half = sources // 2
    late = (half + 3) // 4
    early = half - late
    full = 2 * layers
    devices = lax.axis_size("space")
    pairs = []
    for p in range(1, devices, 2):
        pairs += [(p, (p + 1) % devices), ((p + 1) % devices, p)]

    def swap(x, mask=None):
        links = pairs if mask is None else [(p, p ^ mask) for p in range(devices)]
        return lax.ppermute(x, "space", links)

    dma = pltpu.SemaphoreType.DMA
    slab = (layers, ny, nz)
    other = swap(model)
    first = call(pack, (warm_start,), (V,), [f32(early, *slab)])
    got_first = swap(first)
    beside = swap(other, 1)
    coefs = call(
        prepare,
        (model, other),
        (V, V),
        [f32(7, full, ny, nz)],
        scratch=[V((full, ny, nz), jnp.float32)],
    )
    rhs, weights_time = call(
        inject,
        (survey_order, residual_data, electrodes.reshape(1, -1), coefs),
        (S, V, V, V),
        [f32(half, full, ny, nz), f32(8)],
        [V, S],
    )

    def fields(count):
        field = V((count, full, ny, nz), jnp.float32)
        return [field, field, field, V((2, count, full, ny, nz), jnp.float32)]

    time, opposite, parts = call(
        split_time,
        (weights_time, model, beside),
        (S, V, V),
        [f32(*slab), f32(*slab), f32(2 * layers, ny, nz)],
    )
    near = swap(parts, 4)
    second = call(
        pack_second, (warm_start, forward, parts), (V, V, V), [f32(late * layers + half, ny, nz)]
    )
    got_second = swap(second)
    own_first, sent_first = call(
        solve_first,
        (coefs, got_first, warm_start, rhs),
        (V, V, V, V),
        [f32(early, *slab), f32(early * layers, ny, nz)],
        scratch=fields(early),
        micros=3,
    )
    back_first = swap(sent_first)
    times, joined = call(join_time, (time, opposite, near), (V, V, V), [f32(*slab), f32(*slab)], micros=1)
    far = swap(joined, 8)
    own_second, sent_second = call(
        solve_second,
        (coefs, got_second, warm_start, rhs, forward, own_first, sent_first),
        (V, V, V, V, V, V, V),
        [f32(late, *slab), f32(late * layers + 1, ny, nz)],
        scratch=fields(late),
        micros=3,
    )
    back_second = swap(sent_second)
    sums, kept = call(
        gather_terms,
        (forward, own_first, own_second),
        (V, V, V),
        [f32(4, *slab), bf16(*forward.shape)],
        [V, H],
        scratch=[V((half, *slab), jnp.bfloat16), dma],
        micros=3,
    )
    added, joint = call(
        gather_back,
        (sums, back_first, forward, kept),
        (V, V, V, H),
        [f32(4, *slab), bf16(*forward.shape)],
        [V, H],
        scratch=[V((early, *slab), jnp.bfloat16), dma],
        aliases={3: 1},
        micros=1,
    )
    adjoint, gradient = call(
        finish,
        (added, back_second, sent_second, forward, model, other, times, far, joint),
        (V, V, V, V, V, V, V, V, H),
        [bf16(*forward.shape), f32(*slab)],
        [H, H],
        scratch=[V((late, *slab), jnp.bfloat16), V(slab, jnp.float32), dma((layers + 1,))],
        aliases={8: 0},
    )
    return adjoint, gradient


def solution(mesh):
    body = paired if mesh.shape["space"] == 2 * SURVEYS else layered
    in_specs = (
        P(("groups", "space"), None, None),
        P(None, ("groups", "space"), None, None),
        P(None, ("groups", "space"), None, None),
        P("groups", None, None),
        P("groups"),
        P("groups"),
    )
    out_specs = (P(None, ("groups", "space"), None, None), P(("groups", "space"), None, None))
    return jax.shard_map(body, mesh=mesh, in_specs=in_specs, out_specs=out_specs, check_vma=False)
```

```python
import jax
import jax.numpy as jnp
from jax import lax
from jax.experimental import pallas as pl
from jax.experimental.pallas import tpu as pltpu
from jax.sharding import PartitionSpec as P

SURVEYS = 8
ITERS = 4


GROUND = 0.5
CENTER = 1.0
HALF_WIDTH = 0.99


def padded(shard, sides, width):
    for axis, dim in sides:
        devices, length = (lax.axis_size(axis), shard.shape[dim])
        up = [(i, (i + 1) % devices) for i in range(devices)]
        down = [(j, i) for i, j in up]
        last = lax.slice_in_dim(shard, length - width, length, axis=dim)
        leading = lax.slice_in_dim(shard, 0, width, axis=dim)
        before = lax.ppermute(last, axis, up)
        after = lax.ppermute(leading, axis, down)
        shard = jnp.concatenate([before, shard, after], axis=dim)
    return shard


def swapped(value, axis, bit):
    mask = 2**bit
    pairs = [(source, source ^ mask) for source in range(lax.axis_size(axis))]
    return lax.ppermute(value, axis, pairs)


def face_diff(field, axis):
    count = field.shape[axis]
    return lax.slice_in_dim(field, 0, count - 1, axis=axis) - lax.slice_in_dim(
        field, 1, count, axis=axis
    )


def edge_zeros(field, axis):
    shape = list(field.shape)
    shape[axis] = 1
    return jnp.zeros(shape, jnp.float32)


def pad_diff(faces, axis):
    zeros = edge_zeros(faces, axis)
    return jnp.concatenate([faces, zeros], axis=axis) - jnp.concatenate([zeros, faces], axis=axis)


def pad_sum(faces, axis):
    zeros = edge_zeros(faces, axis)
    return jnp.concatenate([faces, zeros], axis=axis) + jnp.concatenate([zeros, faces], axis=axis)


def extend(field):
    return padded(field, (("space", 1),), 1)


def layered(model, forward, warm_start, residual_data, electrodes, survey_order):
    sources, layers, rows_y, rows_z = forward.shape
    position = lax.axis_index("space")
    devices = lax.axis_size("space")
    tiles = devices // SURVEYS
    half_tiles = tiles // 2
    shifted = position + half_tiles
    tile = shifted % tiles
    survey = shifted // tiles % SURVEYS
    block = position // tiles
    rotation = jnp.where(position % tiles >= half_tiles, 1, 0).astype(jnp.int32)
    valid = jnp.ones((layers + 1,), jnp.float32)
    valid = valid.at[0].set(jnp.where(tile == 0, 0.0, 1.0))
    valid = valid.at[layers].set(jnp.where(tile == tiles - 1, 0.0, 1.0))
    valid_faces = valid[:, None, None]
    model_pad = padded(model, (("space", 0),), 1)
    sigma_pad = jnp.exp(model_pad)
    sigma = sigma_pad[1:-1]
    conduct_x = 0.5 * (sigma_pad[:-1] + sigma_pad[1:]) * valid_faces
    conduct_y = 0.5 * (sigma[:, :-1] + sigma[:, 1:])
    conduct_z = 0.5 * (sigma[:, :, :-1] + sigma[:, :, 1:])
    diagonal = (
        conduct_x[1:]
        + conduct_x[:-1]
        + pad_sum(conduct_y, 1)
        + pad_sum(conduct_z, 2)
        + GROUND * sigma
    )
    inverse_diag = (1.0 / diagonal)[None]

    def operate(field_pad):
        field = field_pad[:, 1:-1]
        flux_x = conduct_x[None] * (field_pad[:, :-1] - field_pad[:, 1:])
        total = flux_x[:, 1:] - flux_x[:, :-1]
        total = total + pad_diff(conduct_y[None] * face_diff(field, 2), 2)
        total = total + pad_diff(conduct_z[None] * face_diff(field, 3), 3)
        return total + GROUND * sigma[None] * field

    cells = layers * rows_y * rows_z
    residual = lax.dynamic_index_in_dim(residual_data, survey, 0, keepdims=False)
    local_index = electrodes - tile * cells
    inside = (local_index >= 0) & (local_index < cells)
    target = jnp.where(inside, local_index, 0)
    amount = jnp.where(inside[None, :], residual, 0.0)
    rhs = jnp.zeros((sources, cells), jnp.float32).at[:, target].add(amount)
    rhs = rhs.reshape(sources, layers, rows_y, rows_z)
    iterate = warm_start.astype(jnp.float32)
    remain = rhs - operate(extend(iterate))
    direction = remain * inverse_diag / CENTER
    weight_now = HALF_WIDTH / CENTER
    for sweep_index in range(ITERS):
        iterate = iterate + direction
        if sweep_index + 1 < ITERS:
            remain = remain - operate(extend(direction))
            weight_new = 1.0 / (2.0 * CENTER / HALF_WIDTH - weight_now)
            direction = weight_new * weight_now * direction + 2.0 * weight_new / HALF_WIDTH * (
                remain * inverse_diag
            )
            weight_now = weight_new
    both = padded(
        jnp.concatenate([forward.astype(jnp.float32), iterate], axis=0), (("space", 1),), 1
    )
    forward_pad = both[:sources]
    adjoint_pad = both[sources:]
    potential = forward_pad[:, 1:-1]
    product_x = (
        jnp.sum(
            (forward_pad[:, :-1] - forward_pad[:, 1:]) * (adjoint_pad[:, :-1] - adjoint_pad[:, 1:]),
            axis=0,
        )
        * valid_faces
    )
    terms = product_x[1:] + product_x[:-1]
    terms = terms + pad_sum(jnp.sum(face_diff(potential, 2) * face_diff(iterate, 2), axis=0), 1)
    terms = terms + pad_sum(jnp.sum(face_diff(potential, 3) * face_diff(iterate, 3), axis=0), 2)
    data_term = -sigma * (0.5 * terms + GROUND * jnp.sum(potential * iterate, axis=0))
    model_x = (model_pad[:-1] - model_pad[1:]) * valid_faces
    space_term = (
        model_x[1:]
        - model_x[:-1]
        + pad_diff(face_diff(model, 1), 1)
        + pad_diff(face_diff(model, 2), 2)
    )
    base_bit = tiles.bit_length() - 1
    collected = model
    for level in range(SURVEYS.bit_length() - 1):
        partner = swapped(collected, "space", base_bit + level)
        upper = block >> level & 1 == 1
        lower_half = jnp.where(upper, partner, collected)
        upper_half = jnp.where(upper, collected, partner)
        collected = jnp.concatenate([lower_half, upper_half], axis=0)
    all_blocks = collected.reshape(SURVEYS, layers, rows_y, rows_z)
    ranks = jnp.arange(SURVEYS, dtype=jnp.int32)
    placed = (survey_order[:, None] == ranks[None, :]).astype(jnp.float32)
    apart = jnp.abs(ranks[:, None] - ranks[None, :])
    degree = jnp.where((ranks == 0) | (ranks == SURVEYS - 1), 1.0, 2.0)
    path = jnp.where(apart == 0, degree[:, None], 0.0) - jnp.where(apart == 1, 1.0, 0.0)
    coupling = jnp.dot(
        placed.T,
        jnp.dot(path, placed, precision=lax.Precision.HIGHEST),
        precision=lax.Precision.HIGHEST,
    )
    row_weights = lax.dynamic_index_in_dim(coupling, survey, 0, keepdims=False)
    block_survey = (ranks + rotation) % SURVEYS
    picker = (block_survey[:, None] == ranks[None, :]).astype(jnp.float32)
    block_weights = jnp.dot(picker, row_weights, precision=lax.Precision.HIGHEST)
    time_term = jnp.sum(block_weights[:, None, None, None] * all_blocks, axis=0)
    return (iterate.astype(jnp.bfloat16), data_term + space_term + time_term)


def weights():
    now = HALF_WIDTH / CENTER
    steps = []
    for _ in range(ITERS - 1):
        new = 1.0 / (2.0 * CENTER / HALF_WIDTH - now)
        steps.append((new * now, 2.0 * new / HALF_WIDTH))
        now = new
    return steps


def after(x, axis):
    return pltpu.roll(x, x.shape[axis] - 1, axis)


def before(x, axis):
    return pltpu.roll(x, 1, axis)


def inner(shape, axis):
    return lax.broadcasted_iota(jnp.int32, shape, axis) < shape[axis] - 1


def face_prod(field, other, axis):
    return (field - after(field, axis)) * (other - after(other, axis))


def tile_of(position):
    return (position + 1) & 1


def survey_of(position):
    return ((position + 1) >> 1) & (SURVEYS - 1)


def pack(warm, first):
    tile = tile_of(lax.axis_index("space"))
    half = warm.shape[0] // 2
    for q in range(first.shape[0]):
        first[q] = warm[half * (1 - tile) + q].astype(jnp.float32)


def pack_second(warm, forward, parts, second):
    tile = tile_of(lax.axis_index("space"))
    half, layers = warm.shape[0] // 2, warm.shape[1]
    count = (second.shape[0] - half) // layers
    theirs = half * (1 - tile)
    face = (layers - 1) * (1 - tile)
    for q in range(count):
        source = theirs + half - count + q
        second[layers * q : layers * (q + 1)] = warm[source].astype(jnp.float32)
    for q in range(half):
        second[count * layers + q] = forward[theirs + q, face].astype(jnp.float32)


def inject(order, residual, electrodes, coefs, out, weights):
    position = lax.axis_index("space")
    tile = tile_of(position)
    surveys = order.shape[0]
    ranks = []
    for place in [position, position ^ 1] + [position ^ (4 * k) for k in range(4)]:
        found = 0
        for i in range(surveys):
            found = found + jnp.where(order[i] == survey_of(place), i, 0)
        ranks.append(found)
    for k in range(4):
        a = ranks[2 + k]
        ends = jnp.where(a == 0, 1, 0) + jnp.where(a == surveys - 1, 1, 0)
        for m in range(2):
            b = ranks[m]
            value = jnp.where(a == b, 2 - ends, jnp.where(jnp.abs(a - b) == 1, -1, 0))
            weights[2 * k + m] = value.astype(jnp.float32)
    sources, _, rows_y, rows_z = out.shape
    half = residual.shape[1] // 2
    cells = out.shape[1] * rows_y * rows_z
    where_cell = lax.rem(electrodes[...] + tile * (cells // 2), cells)
    row = where_cell // rows_z
    lane = lax.rem(where_cell, rows_z)
    count = row.shape[1]
    rows = cells // rows_z
    at_row = lax.broadcasted_iota(jnp.int32, (rows, count), 0) == row
    at_row = jnp.where(at_row, 1.0, 0.0).astype(jnp.bfloat16)
    at_lane = lax.broadcasted_iota(jnp.int32, (rows_z, count), 0) == lane
    mine = residual[survey_of(position)]
    mine = jnp.where(tile == 0, mine[:half], mine[half:])
    total = None
    for _ in range(3):
        part = mine.astype(jnp.bfloat16).astype(jnp.float32)
        mine = mine - part
        right = jnp.concatenate(
            [jnp.where(at_lane, part[q : q + 1], 0.0) for q in range(sources)], axis=0
        ).astype(jnp.bfloat16)
        term = lax.dot_general(
            at_row, right, (((1,), (1,)), ((), ())), preferred_element_type=jnp.float32
        )
        total = term if total is None else total + term
    for q in range(sources):
        out[q] = coefs[6] * total[:, q * rows_z : (q + 1) * rows_z].reshape(out.shape[1:])


def prepare(model, other, coefs, sigma):
    tile = tile_of(lax.axis_index("space"))
    layers = model.shape[0]
    full = 2 * layers
    shape = model.shape[1:]
    for i in range(layers):
        sigma[i] = jnp.exp(model[i])
        sigma[layers + i] = jnp.exp(other[i])
    in_y, in_z = inner(shape, 0), inner(shape, 1)
    middle = jnp.where(tile == 0, 1.0, 0.0)
    for i in range(full):
        mine = sigma[i]
        up = 0.5 * (mine + sigma[(i + 1) % full])
        down = 0.5 * (mine + sigma[(i - 1) % full])
        if i == layers - 1:
            up = up * middle
        if i == full - 1:
            up = up * (1.0 - middle)
        if i == layers:
            down = down * middle
        if i == 0:
            down = down * (1.0 - middle)
        right_y = jnp.where(in_y, 0.5 * (mine + after(mine, 0)), 0.0)
        right_z = jnp.where(in_z, 0.5 * (mine + after(mine, 1)), 0.0)
        left_y = before(right_y, 0)
        left_z = before(right_z, 1)
        scale = 1.0 / (up + down + right_y + left_y + right_z + left_z + GROUND * mine)
        for k, face in enumerate((up, down, right_y, left_y, right_z, left_z)):
            coefs[k, i] = face * scale
        coefs[6, i] = scale


def sweeps(coefs, rhs, base, start, rest, lam, mine):
    count, full = start.shape[:2]

    def around(field, q, i, weight):
        here = field[q, i]
        total = weight[0] * field[q, (i + 1) % full] + weight[1] * field[q, (i + full - 1) % full]
        total = total + (weight[2] * after(here, 0) + weight[3] * before(here, 0))
        total = total + (weight[4] * after(here, 1) + weight[5] * before(here, 1))
        return here, total

    def first(i, carry):
        weight = [coefs[k, i] for k in range(6)]
        for q in range(count):
            here, total = around(start, q, i, weight)
            step = rhs[base + q, i] - here + total
            mine[0, q, i] = step
            lam[q, i] = here + step
        return carry

    lax.fori_loop(0, full, first, 0, unroll=full)
    for index, (keep, gain) in enumerate(weights()):
        source, target = mine.at[index % 2], mine.at[1 - index % 2]
        last = index == ITERS - 2

        def later(i, carry):
            weight = [coefs[k, i] for k in range(6)]
            for q in range(count):
                here, total = around(source, q, i, weight)
                if index > 0:
                    total = rest[q, i] - here + total
                step = keep * here + gain * total
                if not last:
                    rest[q, i] = total
                    target[q, i] = step
                lam[q, i] = lam[q, i] + step
            return carry

        lax.fori_loop(0, full, later, 0, unroll=full)


def load_start(warm, source, got, start):
    count, full = start.shape[:2]
    layers = full // 2
    for q in range(count):
        start[q, :layers] = warm[source + q].astype(jnp.float32)
        start[q, layers:] = got[q] if len(got.shape) == 4 else got[layers * q : layers * (q + 1)]


def split_time(weights, model, beside, time, opposite, parts):
    layers = model.shape[0]
    here, there = model[...], beside[...]
    time[...] = weights[0] * here + weights[1] * there
    parts[:layers] = weights[2] * here + weights[3] * there
    opposite[...] = weights[4] * here + weights[5] * there
    parts[layers:] = weights[6] * here + weights[7] * there


def join_time(time, opposite, near, times, joined):
    layers = time.shape[0]
    times[...] = time[...] + near[:layers]
    joined[...] = opposite[...] + near[layers:]


def solve_first(coefs, got, warm, rhs, own, sent, start, rest, lam, mine):
    count, layers = own.shape[:2]
    half = warm.shape[0] // 2
    load_start(warm, half * tile_of(lax.axis_index("space")), got, start)
    sweeps(coefs, rhs, 0, start, rest, lam, mine)
    for q in range(count):
        own[q] = lam[q, :layers]
        sent[layers * q : layers * (q + 1)] = lam[q, layers:]


def solve_second(coefs, got, warm, rhs, forward, own_first, sent_first, own, sent, start, rest, lam, mine):
    count, layers = own.shape[:2]
    tile = tile_of(lax.axis_index("space"))
    half = warm.shape[0] // 2
    early, source = half - count, half * tile
    load_start(warm, source + early, got, start)
    sweeps(coefs, rhs, early, start, rest, lam, mine)
    near = (layers - 1) * (1 - tile)
    far = (layers - 1) * tile
    total = None
    for q in range(half):
        slope = forward[source + q, near].astype(jnp.float32) - got[count * layers + q]
        if q < early:
            drop = own_first[q, near] - sent_first[layers * q + far]
        else:
            drop = lam[q - early, near] - lam[q - early, layers + far]
        total = slope * drop if total is None else total + slope * drop
    for q in range(count):
        own[q] = lam[q, :layers]
        sent[layers * q : layers * (q + 1)] = lam[q, layers:]
    sent[count * layers] = total


def data_sums(pairs, layers, along_x, along_y, along_z, mass):
    def add(ref, i, value, first):
        ref[i] = value if first else ref[i] + value

    for i in range(layers):
        totals = [None] * 4
        for forward, lam in pairs:
            here, other = forward(i), lam(i)
            terms = [None, face_prod(here, other, 0), face_prod(here, other, 1), here * other]
            if i + 1 < layers:
                terms[0] = (here - forward(i + 1)) * (other - lam(i + 1))
            totals = [t if a is None else (a if t is None else a + t) for a, t in zip(totals, terms)]
        if i + 1 < layers:
            along_x[i] = along_x[i] + totals[0]
        along_y[i] = along_y[i] + totals[1]
        along_z[i] = along_z[i] + totals[2]
        mass[i] = mass[i] + totals[3]


def gather_terms(forward, own_first, own_second, sums, adjoint, rounded, sem):
    early, layers = own_first.shape[:2]
    half = rounded.shape[0]
    mine = half * tile_of(lax.axis_index("space"))
    rounded[:early] = own_first[...].astype(jnp.bfloat16)
    rounded[early:] = own_second[...].astype(jnp.bfloat16)
    copy = pltpu.make_async_copy(rounded, adjoint.at[pl.ds(mine, half)], sem)
    copy.start()
    sums[...] = jnp.zeros(sums.shape, jnp.float32)
    pairs = []
    for q in range(half):
        own, at = (own_first, q) if q < early else (own_second, q - early)
        pairs.append((
            lambda i, q=q: forward[mine + q, i].astype(jnp.float32),
            lambda i, own=own, at=at: own[at, i],
        ))
    data_sums(pairs, layers, sums.at[0], sums.at[1], sums.at[2], sums.at[3])
    copy.wait()


def spread(along_x, along_y, along_z, first, last, shape):
    in_y, in_z = inner(shape, 0), inner(shape, 1)
    products = [first] + along_x + [last]
    terms = []
    for i in range(len(along_y)):
        total_y = jnp.where(in_y, along_y[i], 0.0)
        total_z = jnp.where(in_z, along_z[i], 0.0)
        sides = [p for p in products[i : i + 2] if p is not None]
        total = (total_y + before(total_y, 0)) + (total_z + before(total_z, 1))
        for side in sides:
            total = total + side
        terms.append(total)
    return terms


def gather_back(sums, back, forward, model, other, times, kept, base, sigma, adjoint, added, rounded, sem):
    early, layers = rounded.shape[:2]
    tile = tile_of(lax.axis_index("space"))
    theirs = forward.shape[0] // 2 * (1 - tile)
    shape = model.shape[1:]
    for q in range(early):
        rounded[q] = back[layers * q : layers * (q + 1)].astype(jnp.bfloat16)
    copy = pltpu.make_async_copy(rounded, adjoint.at[pl.ds(theirs, early)], sem)
    copy.start()
    added[...] = sums[...]
    pairs = []
    for q in range(early):
        pairs.append((
            lambda i, q=q: forward[theirs + q, i].astype(jnp.float32),
            lambda i, q=q: back[layers * q + i],
        ))
    data_sums(pairs, layers, added.at[0], added.at[1], added.at[2], added.at[3])
    along = [[added[k, i] for i in range(layers)] for k in range(4)]
    terms = spread(along[0][:-1], along[1], along[2], None, None, shape)
    in_y, in_z = inner(shape, 0), inner(shape, 1)
    low = jnp.where(tile == 0, 0.0, 1.0)
    bridge = other[(layers - 1) * tile]
    falls = [low * (bridge - model[0])]
    falls += [model[i] - model[i + 1] for i in range(layers - 1)]
    falls += [(1.0 - low) * (model[layers - 1] - bridge)]
    for i in range(layers):
        value = model[i]
        sigma[i] = jnp.exp(value)
        fall_y = jnp.where(in_y, value - after(value, 0), 0.0)
        fall_z = jnp.where(in_z, value - after(value, 1), 0.0)
        space = falls[i + 1] - falls[i] + (fall_y - before(fall_y, 0)) + (fall_z - before(fall_z, 1))
        base[i] = space + times[i] - sigma[i] * (0.5 * terms[i] + GROUND * along[3][i])
    copy.wait()


def finish(base, sigma, back, sent, forward, far, kept, adjoint, gradient, rounded, result, sems):
    tile = tile_of(lax.axis_index("space"))
    count, layers = rounded.shape[:2]
    half = forward.shape[0] // 2
    theirs = half * (1 - tile) + half - count
    for q in range(count):
        rounded[q] = back[layers * q : layers * (q + 1)].astype(jnp.bfloat16)
    copies = [pltpu.make_async_copy(rounded, adjoint.at[pl.ds(theirs, count)], sems.at[layers])]
    copies[0].start()
    along = [[None] * layers for _ in range(4)]
    for q in range(count):
        here = [forward[theirs + q, i].astype(jnp.float32) for i in range(layers)]
        there = [back[layers * q + i] for i in range(layers)]
        for i in range(layers):
            values = [None, face_prod(here[i], there[i], 0), face_prod(here[i], there[i], 1), here[i] * there[i]]
            if i + 1 < layers:
                values[0] = (here[i] - here[i + 1]) * (there[i] - there[i + 1])
            for k, value in enumerate(values):
                if value is not None:
                    along[k][i] = value if along[k][i] is None else along[k][i] + value
    cross = back[count * layers] + sent[count * layers]
    low = jnp.where(tile == 0, 0.0, 1.0)
    terms = spread(along[0][:-1], along[1], along[2], low * cross, (1.0 - low) * cross, cross.shape)
    for i in range(layers):
        change = sigma[i] * (0.5 * terms[i] + GROUND * along[3][i])
        result[i] = (base[i] + far[i]) - change
        copies.append(pltpu.make_async_copy(result.at[i], gradient.at[i], sems.at[i]))
        copies[-1].start()
    for copy in copies:
        copy.wait()


V, S, H = pltpu.VMEM, pltpu.SMEM, pltpu.HBM


def call(kernel, operands, spaces, out_shapes, out_spaces=None, scratch=(), aliases=None, micros=1, room=16):
    several = len(out_shapes) > 1
    specs = [pl.BlockSpec(memory_space=m) for m in spaces]
    out_specs = [pl.BlockSpec(memory_space=m) for m in out_spaces or [V] * len(out_shapes)]
    return pl.pallas_call(
        kernel,
        out_shape=out_shapes if several else out_shapes[0],
        in_specs=specs,
        out_specs=out_specs if several else out_specs[0],
        scratch_shapes=list(scratch),
        input_output_aliases=aliases or {},
        compiler_params=pltpu.CompilerParams(vmem_limit_bytes=room * 2**20),
        cost_estimate=pl.CostEstimate(
            flops=micros * 10**9, bytes_accessed=micros * 3 * 10**6, transcendentals=0
        ),
    )(*operands)


def f32(*shape):
    return jax.ShapeDtypeStruct(shape, jnp.float32)


def bf16(*shape):
    return jax.ShapeDtypeStruct(shape, jnp.bfloat16)


def paired(model, forward, warm_start, residual_data, electrodes, survey_order):
    sources, layers, ny, nz = forward.shape
    half = sources // 2
    late = (half + 3) // 4
    early = half - late
    full = 2 * layers
    devices = lax.axis_size("space")
    pairs = []
    for p in range(1, devices, 2):
        pairs += [(p, (p + 1) % devices), ((p + 1) % devices, p)]

    def swap(x, mask=None):
        links = pairs if mask is None else [(p, p ^ mask) for p in range(devices)]
        return lax.ppermute(x, "space", links)

    dma = pltpu.SemaphoreType.DMA
    slab = (layers, ny, nz)
    other = swap(model)
    first = call(pack, (warm_start,), (V,), [f32(early, *slab)])
    got_first = swap(first)
    beside = swap(other, 1)
    coefs = call(
        prepare,
        (model, other),
        (V, V),
        [f32(7, full, ny, nz)],
        scratch=[V((full, ny, nz), jnp.float32)],
    )
    rhs, weights_time = call(
        inject,
        (survey_order, residual_data, electrodes.reshape(1, -1), coefs),
        (S, V, V, V),
        [f32(half, full, ny, nz), f32(8)],
        [V, S],
    )

    def fields(count):
        field = V((count, full, ny, nz), jnp.float32)
        return [field, field, field, V((2, count, full, ny, nz), jnp.float32)]

    time, opposite, parts = call(
        split_time,
        (weights_time, model, beside),
        (S, V, V),
        [f32(*slab), f32(*slab), f32(2 * layers, ny, nz)],
    )
    near = swap(parts, 4)
    second = call(
        pack_second, (warm_start, forward, parts), (V, V, V), [f32(late * layers + half, ny, nz)]
    )
    got_second = swap(second)
    own_first, sent_first = call(
        solve_first,
        (coefs, got_first, warm_start, rhs),
        (V, V, V, V),
        [f32(early, *slab), f32(early * layers, ny, nz)],
        scratch=fields(early),
        micros=3,
    )
    back_first = swap(sent_first)
    times, joined = call(join_time, (time, opposite, near), (V, V, V), [f32(*slab), f32(*slab)], micros=1)
    far = swap(joined, 8)
    own_second, sent_second = call(
        solve_second,
        (coefs, got_second, warm_start, rhs, forward, own_first, sent_first),
        (V, V, V, V, V, V, V),
        [f32(late, *slab), f32(late * layers + 1, ny, nz)],
        scratch=fields(late),
        micros=3,
    )
    back_second = swap(sent_second)
    sums, kept = call(
        gather_terms,
        (forward, own_first, own_second),
        (V, V, V),
        [f32(4, *slab), bf16(*forward.shape)],
        [V, H],
        scratch=[V((half, *slab), jnp.bfloat16), dma],
        micros=3,
    )
    base, sigma, joint = call(
        gather_back,
        (sums, back_first, forward, model, other, times, kept),
        (V, V, V, V, V, V, H),
        [f32(*slab), f32(*slab), bf16(*forward.shape)],
        [V, V, H],
        scratch=[V((4, *slab), jnp.float32), V((early, *slab), jnp.bfloat16), dma],
        aliases={6: 2},
    )
    adjoint, gradient = call(
        finish,
        (base, sigma, back_second, sent_second, forward, far, joint),
        (V, V, V, V, V, V, H),
        [bf16(*forward.shape), f32(*slab)],
        [H, H],
        scratch=[V((late, *slab), jnp.bfloat16), V(slab, jnp.float32), dma((layers + 1,))],
        aliases={6: 0},
    )
    return adjoint, gradient


def solution(mesh):
    body = paired if mesh.shape["space"] == 2 * SURVEYS else layered
    in_specs = (
        P(("groups", "space"), None, None),
        P(None, ("groups", "space"), None, None),
        P(None, ("groups", "space"), None, None),
        P("groups", None, None),
        P("groups"),
        P("groups"),
    )
    out_specs = (P(None, ("groups", "space"), None, None), P(("groups", "space"), None, None))
    return jax.shard_map(body, mesh=mesh, in_specs=in_specs, out_specs=out_specs, check_vma=False)
```
